32 devices in a mesh: group: 2 (over y), sec: 16 (over z, x, core), op: 1.
Axes of the slice: x: 2, y: 2, z: 4, core: 2. Of those that a mesh axis runs over, the one named last changes fastest.
Arguments:
- psi: bfloat16 [32, 16, 256, 256], P(('group', 'sec')), parts along dimension 0, may hold values from -6 to 6
- left_env: bfloat16 [16, 16, 256, 256], P(('group', 'op'), 'sec'), parts along dimension 0, may hold values from -0.375 to 0.375
- right_env: bfloat16 [16, 16, 256, 256], P(('group', 'op'), 'sec'), parts along dimension 0, may hold values from -0.125 to 0.125
- source_map: int32 [16, 16], P(('group', 'op')), parts along dimension 0, may hold values from 0 to 15
Outputs:
- hpsi: bfloat16 [32, 16, 256, 256], P('group', 'sec', 'op'), parts along dimension 0
The draws below stay inside these ranges and needn't reach their ends.
There are 2 independent parts, one for each index of `group`. The reference program is written for one: setup_inputs(seed, part) draws one part's arguments, and reference() takes and returns one part's arrays. A program takes and returns all parts, laid end to end along the dimension named above; each array names one. Nothing has to cross between parts.
Inputs may be any that keep to these rules, and one draw needn't show every extreme that they name: source_map[k, q] is the right sector of psi that term k carries into output right sector q.
All inputs are finite; a program needn't handle non-finite values.
Results may differ from the reference program's by a relative error of at most 0.0049.
Values may be sent and summed in bfloat16 or wider, within the bound.
No kernel may reach another device: no remote copies, remote signals or barrier semaphores. Data moves between devices by JAX's collectives and lax.ppermute only.
A program may use at most 128 MiB of HBM per device.

```python
import jax
import jax.numpy as jnp
from jax import lax

B = 256
Q = 16
KTERMS = 8


def set_ends(array, own_key, low, largest):
    place = [jax.random.randint(jax.random.fold_in(own_key, axis), (), 0, length) for axis, length in enumerate(array.shape)]
    widest = array.shape.index(max(array.shape))
    neighbour = place[:widest] + [(place[widest] + 1) % array.shape[widest]] + place[widest + 1:]
    return array.at[tuple(place)].set(low).at[tuple(neighbour)].set(largest)


def shard_levels(stream_key, shape, split, low, top_value):
    loudness = 1.0
    for dim, blocks in split:
        draws = jax.random.uniform(jax.random.fold_in(jax.random.fold_in(stream_key, 6), dim), (blocks,), jnp.float32, low / len(split), top_value / len(split))
        loudness = loudness * jnp.repeat(jnp.exp(draws), shape[dim] // blocks).reshape((-1,) + (1,) * (len(shape) - 1 - dim))
    return loudness


def centred(own_key, extent, width, bound, shards=(), kind=jnp.bfloat16):
    entries = jax.random.normal(own_key, extent, jnp.float32) * width
    if len(shards) > 0:
        entries = shard_levels(own_key, extent, shards, -0.22, 0.18) * entries
    return jnp.clip(entries, min=-bound, max=bound).astype(kind)


def setup_inputs(seed: int = 0, part: int = 0) -> dict:
    key_of = jax.random.split(jax.random.key(seed), 5)
    part_keys = jax.random.split(jax.random.fold_in(key_of[4], part), 5)
    psi = centred(part_keys[0], (Q, Q, B, B), 1.0, 6.0, ((0, 16),))
    left_env = centred(part_keys[1], (KTERMS, Q, B, B), B ** -0.5, 0.375, ((1, 16),))
    right_env = centred(part_keys[2], (KTERMS, Q, B, B), (B * KTERMS) ** -0.5, 0.125, ((1, 16),))
    source_map = set_ends(jax.random.randint(part_keys[3], (KTERMS, Q), 0, Q), jax.random.fold_in(part_keys[3], 1), 0, Q - 1).astype(jnp.int32)
    return {"psi": psi, "left_env": left_env, "right_env": right_env, "source_map": source_map}


def reference(psi, left_env, right_env, source_map):
    def step(total, k):
        chosen = jnp.take(psi, source_map[k], axis=1).astype(jnp.float32)
        left = left_env[k].astype(jnp.float32)
        mid = jnp.einsum('aij,aqjm->aqim', left, chosen).astype(jnp.bfloat16)
        mid = lax.optimization_barrier(mid).astype(jnp.float32)
        right = right_env[k].astype(jnp.float32)
        return total + jnp.einsum('aqim,qnm->aqin', mid, right), None

    start = jnp.zeros((Q, Q, B, B), jnp.float32)
    total, unused = lax.scan(step, start, jnp.arange(KTERMS).astype(jnp.int32))
    return total.astype(jnp.bfloat16)
```

```python
import functools

import jax
import jax.numpy as jnp
from jax import lax
from jax.experimental import pallas as pl
from jax.experimental.pallas import tpu as pltpu
from jax.sharding import PartitionSpec as P

HBM = pl.BlockSpec(memory_space=pl.ANY)
SMEM = pl.BlockSpec(memory_space=pltpu.SMEM)
VMEM = pl.BlockSpec(memory_space=pltpu.VMEM)


def slot_kernel(count, choices, meta, source, *refs):
    lefts, psis = refs[:count], refs[count : 2 * count]
    rights = refs[2 * count : 2 * count + choices]
    out, left_buf, psi_buf, right_buf, left_sem, psi_sem, right_sem = refs[2 * count + choices :]
    terms = right_buf.shape[0]
    q = meta[0]

    def copies(k, i):
        return (
            pltpu.make_async_copy(lefts[i].at[k, 0], left_buf.at[i, k], left_sem.at[i, k]),
            pltpu.make_async_copy(psis[i].at[0, source[k, q]], psi_buf.at[i, k], psi_sem.at[i, k]),
        )

    def right_copy(k, choice):
        return pltpu.make_async_copy(rights[choice].at[k, 0], right_buf.at[k], right_sem.at[k])

    for k in range(terms):
        if choices == 1:
            right_copy(k, 0).start()
        else:
            for choice in range(choices):
                pl.when(meta[1] == choice)(lambda k=k, choice=choice: right_copy(k, choice).start())
        for copy in copies(k, 0):
            copy.start()
    for i in range(1, count):
        for k in range(terms):
            for copy in copies(k, i):
                copy.start()
    for i in range(count):
        total = None
        for k in range(terms):
            for copy in copies(k, i):
                copy.wait()
            if i == 0:
                right_copy(k, 0).wait()
            mid = jnp.dot(left_buf[i, k], psi_buf[i, k], preferred_element_type=jnp.float32).astype(jnp.bfloat16)
            term = lax.dot_general(mid, right_buf[k], (((1,), (1,)), ((), ())), preferred_element_type=jnp.float32)
            total = term if total is None else total + term
        out[i] = total.astype(out.dtype)


def slot(q, choice, source_map, lefts, psis, rights, dtype):
    terms, _, rows, columns = lefts[0].shape
    count = len(lefts)
    meta = jnp.stack([q, choice]).astype(jnp.int32)
    block = rows * columns
    return pl.pallas_call(
        functools.partial(slot_kernel, count, len(rights)),
        out_shape=jax.ShapeDtypeStruct((count, rows, columns), dtype),
        in_specs=[SMEM, SMEM] + [HBM] * (2 * count + len(rights)),
        out_specs=VMEM,
        scratch_shapes=[
            pltpu.VMEM((count, terms, rows, columns), jnp.bfloat16),
            pltpu.VMEM((count, terms, rows, columns), jnp.bfloat16),
            pltpu.VMEM((terms, rows, columns), jnp.bfloat16),
            pltpu.SemaphoreType.DMA((count, terms)),
            pltpu.SemaphoreType.DMA((count, terms)),
            pltpu.SemaphoreType.DMA((terms,)),
        ],
        compiler_params=pltpu.CompilerParams(vmem_limit_bytes=24 << 20),
        cost_estimate=pl.CostEstimate(
            flops=4 * count * terms * block * rows,
            bytes_accessed=2 * block * terms * (2 * count + 1) + 2 * block * count,
            transcendentals=0,
        ),
    )(meta, source_map, *lefts, *psis, *rights)


def place_kernel(width, meta, *refs):
    pieces, out, sem = refs[:-2], refs[-2], refs[-1]
    me = meta[0]

    def copy(j):
        return pltpu.make_async_copy(pieces[j // width].at[j % width], out.at[me ^ j], sem.at[j])

    for j in range(len(pieces) * width):
        copy(j).start()
    for j in range(len(pieces) * width):
        copy(j).wait()


def place(me, pieces):
    width, rows, columns = pieces[0].shape
    sectors = width * len(pieces)
    return pl.pallas_call(
        functools.partial(place_kernel, width),
        out_shape=jax.ShapeDtypeStruct((sectors, rows, columns), pieces[0].dtype),
        in_specs=[SMEM] + [HBM] * len(pieces),
        out_specs=HBM,
        scratch_shapes=[pltpu.SemaphoreType.DMA((sectors,))],
    )(me[None].astype(jnp.int32), *pieces)


def exchange(array, bits, members):
    return lax.ppermute(array, "sec", [(s, s ^ bits) for s in members])


def on_device(ops, psi, left_env, right_env, source_map):
    me = lax.axis_index("sec")
    row = me // 4
    outer = (row == 0) | (row == 3)
    dtype = jnp.bfloat16 if ops == 1 else jnp.float32
    every = range(16)
    inner_to_outer = range(4, 12)

    near = exchange(right_env, 4, every)
    middle = exchange(right_env, 12, inner_to_outer)
    far_in = exchange(near, 12, inner_to_outer)
    second = exchange(middle, 4, inner_to_outer)
    third = exchange(far_in, 4, inner_to_outer)

    left, sectors = [left_env], [psi]
    left.append(exchange(left_env, 1, every))
    sectors.append(exchange(psi, 1, every))
    left.append(exchange(left_env, 2, every))
    sectors.append(exchange(psi, 2, every))
    left.append(exchange(left[2], 1, every))
    sectors.append(exchange(sectors[2], 1, every))

    rights = ((right_env,), (near,), (second, far_in), (third, middle))
    choice = jnp.where(outer, 0, 1)
    pieces = []
    for step in range(4):
        for half in (slice(0, 2), slice(2, 4)):
            piece = slot(me ^ (4 * step), choice, source_map, left[half], sectors[half], rights[step], dtype)
            if step > 0:
                piece = exchange(piece, 4 * step, every)
            pieces.append(piece)
    out = place(me, pieces)[:, None]
    if ops > 1:
        out = lax.psum_scatter(out, "op", scatter_dimension=2, tiled=True).astype(jnp.bfloat16)
    return out


def solution(mesh):
    placed = (
        P(("group", "sec"), None, None, None),
        P(("group", "op"), "sec", None, None),
        P(("group", "op"), "sec", None, None),
        P(("group", "op"), None),
    )
    return jax.shard_map(
        functools.partial(on_device, mesh.shape["op"]),
        mesh=mesh,
        in_specs=placed,
        out_specs=P("group", "sec", "op", None),
        check_vma=False,
    )
```

```python
import functools

import jax
import jax.numpy as jnp
from jax import lax
from jax.experimental import pallas as pl
from jax.experimental.pallas import tpu as pltpu
from jax.sharding import PartitionSpec as P

HBM = pl.BlockSpec(memory_space=pl.ANY)
SMEM = pl.BlockSpec(memory_space=pltpu.SMEM)
VMEM = pl.BlockSpec(memory_space=pltpu.VMEM)


def slot_kernel(shape, meta, source, *refs):
    parts, choices = shape
    count = len(parts)
    lefts, refs = refs[:count], refs[count:]
    psis = []
    for number in parts:
        psis.append(refs[:number])
        refs = refs[number:]
    rights = refs[:choices]
    out, left_buf, psi_buf, right_buf, mid_buf, left_sem, psi_sem, right_sem = refs[choices:]
    terms, rows, columns = left_buf.shape[1:]
    q = meta[0]

    def left_copy(i, k):
        return pltpu.make_async_copy(lefts[i].at[k, 0], left_buf.at[i, k], left_sem.at[i, k])

    def psi_copy(i, k, part, place):
        return pltpu.make_async_copy(psis[i][part].at[0, place], psi_buf.at[i, k], psi_sem.at[i, k])

    def right_copy(k, choice):
        return pltpu.make_async_copy(
            rights[choice].at[k, 0], right_buf.at[:, pl.ds(k * columns, columns)], right_sem.at[k]
        )

    for k in range(terms):
        for i in range(count):
            left_copy(i, k).start()
            sector = source[k, q]
            if parts[i] == 1:
                psi_copy(i, k, 0, sector).start()
            else:
                held = psis[i][0].shape[1]
                for part in range(parts[i]):

                    @pl.when((sector >= part * held) & (sector < (part + 1) * held))
                    def _(i=i, k=k, part=part, place=sector - part * held):
                        psi_copy(i, k, part, place).start()

    for k in range(terms):
        if choices == 1:
            right_copy(k, 0).start()
        else:
            for choice in range(choices):

                @pl.when(meta[1] == choice)
                def _(k=k, choice=choice):
                    right_copy(k, choice).start()

    for k in range(terms):
        for i in range(count):
            left_copy(i, k).wait()
            psi_copy(i, k, 0, 0).wait()
            mid = jnp.dot(left_buf[i, k], psi_buf[i, k], preferred_element_type=jnp.float32)
            mid_buf[pl.ds(i * rows, rows), pl.ds(k * columns, columns)] = mid.astype(jnp.bfloat16)
    for k in range(terms):
        right_copy(k, 0).wait()
    total = lax.dot_general(
        mid_buf[...], right_buf[...], (((1,), (1,)), ((), ())), preferred_element_type=jnp.float32
    )
    out[...] = total.reshape(out.shape).astype(out.dtype)


def slot(q, choice, source_map, lefts, psis, rights, dtype):
    terms, _, rows, columns = lefts[0].shape
    count = len(lefts)
    parts = tuple(len(psi) for psi in psis)
    meta = jnp.stack([q, choice]).astype(jnp.int32)
    block = rows * columns
    return pl.pallas_call(
        functools.partial(slot_kernel, (parts, len(rights))),
        out_shape=jax.ShapeDtypeStruct((count, rows, columns), dtype),
        in_specs=[SMEM, SMEM] + [HBM] * (count + sum(parts) + len(rights)),
        out_specs=VMEM,
        scratch_shapes=[
            pltpu.VMEM((count, terms, rows, columns), jnp.bfloat16),
            pltpu.VMEM((count, terms, rows, columns), jnp.bfloat16),
            pltpu.VMEM((rows, terms * columns), jnp.bfloat16),
            pltpu.VMEM((count * rows, terms * columns), jnp.bfloat16),
            pltpu.SemaphoreType.DMA((count, terms)),
            pltpu.SemaphoreType.DMA((count, terms)),
            pltpu.SemaphoreType.DMA((terms,)),
        ],
        compiler_params=pltpu.CompilerParams(vmem_limit_bytes=24 << 20),
        cost_estimate=pl.CostEstimate(
            flops=4 * count * terms * block * rows,
            bytes_accessed=2 * block * terms * (2 * count + 1) + 2 * block * count,
            transcendentals=0,
        ),
    )(meta, source_map, *lefts, *[part for psi in psis for part in psi], *rights)


def place_kernel(width, meta, *refs):
    pieces, out, sem = refs[:-2], refs[-2], refs[-1]
    me = meta[0]

    def copy(j):
        return pltpu.make_async_copy(pieces[j // width].at[j % width], out.at[me ^ j], sem.at[j])

    for j in range(len(pieces) * width):
        copy(j).start()
    for j in range(len(pieces) * width):
        copy(j).wait()


def place(me, pieces):
    width, rows, columns = pieces[0].shape
    sectors = width * len(pieces)
    return pl.pallas_call(
        functools.partial(place_kernel, width),
        out_shape=jax.ShapeDtypeStruct((sectors, rows, columns), pieces[0].dtype),
        in_specs=[SMEM] + [HBM] * len(pieces),
        out_specs=VMEM,
        scratch_shapes=[pltpu.SemaphoreType.DMA((sectors,))],
        compiler_params=pltpu.CompilerParams(vmem_limit_bytes=16 << 20),
    )(me[None].astype(jnp.int32), *pieces)


def exchange(array, bits, members):
    return lax.ppermute(array, "sec", [(s, s ^ bits) for s in members])


def on_device(ops, psi, left_env, right_env, source_map):
    me = lax.axis_index("sec")
    row = me // 4
    choice = jnp.where((row == 0) | (row == 3), 0, 1)
    dtype = jnp.bfloat16 if ops == 1 else jnp.float32
    every = range(16)
    inner = range(4, 12)
    half = psi.shape[1] // 2
    low, high = psi[:, :half], psi[:, half:]

    def products(step, lefts, psis, rights):
        return slot(me ^ (4 * step), choice, source_map, lefts, psis, rights, dtype)

    near = exchange(right_env, 4, every)
    middle = exchange(right_env, 12, inner)
    x_left = exchange(left_env, 2, every)
    x_low = exchange(low, 2, every)
    core_left = exchange(left_env, 1, every)
    core_psi = exchange(psi, 1, every)
    own = ([left_env, core_left], [(psi,), (core_psi,)])

    near, middle, high_next = lax.optimization_barrier((near, middle, high))
    far_in = exchange(near, 12, inner)
    second = exchange(middle, 4, inner)
    x_high = exchange(high_next, 2, every)
    own_1 = products(1, *own, (near,))
    sent_1 = exchange(own_1, 4, every)

    second, far_in, x_left, x_low, own_1 = lax.optimization_barrier((second, far_in, x_left, x_low, own_1))
    third = exchange(far_in, 4, inner)
    across_left = exchange(x_left, 1, every)
    across_low = exchange(x_low, 1, every)
    own_2 = products(2, *own, (second, far_in))
    sent_2 = exchange(own_2, 8, every)

    third, x_high, own_2 = lax.optimization_barrier((third, x_high, own_2))
    across_high = exchange(x_high, 1, every)
    own_3 = products(3, *own, (third, middle))
    sent_3 = exchange(own_3, 12, every)
    other = ([x_left, across_left], [(x_low, x_high), (across_low, across_high)])
    other_1 = products(1, *other, (near,))
    other_sent_1 = exchange(other_1, 4, every)
    other_2 = products(2, *other, (second, far_in))
    other_sent_2 = exchange(other_2, 8, every)
    other_3 = products(3, *other, (third, middle))
    other_sent_3 = exchange(other_3, 12, every)
    own_0 = products(0, *own, (right_env,))
    other_0 = products(0, *other, (right_env,))

    pieces = [own_0, other_0, sent_1, other_sent_1, sent_2, other_sent_2, sent_3, other_sent_3]
    out = place(me, pieces)[:, None]
    if ops > 1:
        out = lax.psum_scatter(out, "op", scatter_dimension=2, tiled=True).astype(jnp.bfloat16)
    return out


def solution(mesh):
    placed = (
        P(("group", "sec"), None, None, None),
        P(("group", "op"), "sec", None, None),
        P(("group", "op"), "sec", None, None),
        P(("group", "op"), None),
    )
    return jax.shard_map(
        functools.partial(on_device, mesh.shape["op"]),
        mesh=mesh,
        in_specs=placed,
        out_specs=P("group", "sec", "op", None),
        check_vma=False,
    )
```

```python
import functools

import jax
import jax.numpy as jnp
from jax import lax
from jax.experimental import pallas as pl
from jax.experimental.pallas import tpu as pltpu
from jax.sharding import PartitionSpec as P

HBM = pl.BlockSpec(memory_space=pl.ANY)
SMEM = pl.BlockSpec(memory_space=pltpu.SMEM)
VMEM = pl.BlockSpec(memory_space=pltpu.VMEM)


def slot_kernel(shape, meta, source, *refs):
    parts, choices = shape
    count = len(parts)
    lefts, refs = refs[:count], refs[count:]
    psis = []
    for number in parts:
        psis.append(refs[:number])
        refs = refs[number:]
    rights = refs[:choices]
    out, right_buf, mid_buf = refs[choices:]
    terms, _, rows, columns = lefts[0].shape
    q = meta[0]

    def sector_block(held, sector):
        size = held[0].shape[1]
        block = held[0][0, sector % size]
        for part in range(1, len(held)):
            block = jnp.where(sector >= part * size, held[part][0, sector % size], block)
        return block

    for k in range(terms):
        span = pl.ds(k * columns, columns)
        right = rights[0][k, 0]
        for choice in range(1, choices):
            right = jnp.where(meta[1] >= choice, rights[choice][k, 0], right)
        right_buf[:, span] = right
        for i in range(count):
            mid = jnp.dot(lefts[i][k, 0], sector_block(psis[i], source[k, q]), preferred_element_type=jnp.float32)
            mid_buf[pl.ds(i * rows, rows), span] = mid.astype(jnp.bfloat16)
    total = lax.dot_general(
        mid_buf[...], right_buf[...], (((1,), (1,)), ((), ())), preferred_element_type=jnp.float32
    )
    out[...] = total.reshape(out.shape).astype(out.dtype)


def slot(q, choice, source_map, lefts, psis, rights, dtype):
    terms, _, rows, columns = lefts[0].shape
    count = len(lefts)
    parts = tuple(len(psi) for psi in psis)
    meta = jnp.stack([q, choice]).astype(jnp.int32)
    return pl.pallas_call(
        functools.partial(slot_kernel, (parts, len(rights))),
        out_shape=jax.ShapeDtypeStruct((count, rows, columns), dtype),
        in_specs=[SMEM, SMEM] + [VMEM] * (count + sum(parts) + len(rights)),
        out_specs=VMEM,
        scratch_shapes=[
            pltpu.VMEM((rows, terms * columns), jnp.bfloat16),
            pltpu.VMEM((count * rows, terms * columns), jnp.bfloat16),
        ],
        compiler_params=pltpu.CompilerParams(vmem_limit_bytes=24 << 20),
        cost_estimate=pl.CostEstimate(flops=1, bytes_accessed=1, transcendentals=0),
    )(meta, source_map, *lefts, *[part for psi in psis for part in psi], *rights)


def place_kernel(width, meta, *refs):
    pieces, out, sem = refs[:-2], refs[-2], refs[-1]
    me = meta[0]

    def copy(j):
        return pltpu.make_async_copy(pieces[j // width].at[j % width], out.at[me ^ j], sem.at[j])

    for j in range(len(pieces) * width):
        copy(j).start()
    for j in range(len(pieces) * width):
        copy(j).wait()


def place(me, pieces):
    width, rows, columns = pieces[0].shape
    sectors = width * len(pieces)
    return pl.pallas_call(
        functools.partial(place_kernel, width),
        out_shape=jax.ShapeDtypeStruct((sectors, rows, columns), pieces[0].dtype),
        in_specs=[SMEM] + [VMEM] * len(pieces),
        out_specs=HBM,
        scratch_shapes=[pltpu.SemaphoreType.DMA((sectors,))],
        compiler_params=pltpu.CompilerParams(vmem_limit_bytes=16 << 20),
    )(me[None].astype(jnp.int32), *pieces)


def exchange(array, bits, members):
    return lax.ppermute(array, "sec", [(s, s ^ bits) for s in members])


def on_device(ops, psi, left_env, right_env, source_map):
    me = lax.axis_index("sec")
    row = me // 4
    choice = jnp.where((row == 0) | (row == 3), 0, 1)
    dtype = jnp.bfloat16 if ops == 1 else jnp.float32
    every = range(16)
    inner = range(4, 12)

    def products(step, lefts, psis, rights):
        return slot(me ^ (4 * step), choice, source_map, lefts, [(psi,) for psi in psis], rights, dtype)

    near = exchange(right_env, 4, every)
    middle = exchange(right_env, 12, inner)
    x_psi = exchange(psi, 2, every)
    own = ([left_env, exchange(left_env, 1, every)], [psi, exchange(psi, 1, every)])

    near, middle = lax.optimization_barrier((near, middle))
    far_in = exchange(near, 12, inner)
    second = exchange(middle, 4, inner)
    own_1 = products(1, *own, (near,))
    own_0 = products(0, *own, (right_env,))

    second, far_in, x_psi, left_next, own_0, own_1 = lax.optimization_barrier(
        (second, far_in, x_psi, left_env, own_0, own_1)
    )
    sent_1 = exchange(own_1, 4, every)
    third = exchange(far_in, 4, inner)
    x_left = exchange(left_next, 2, every)
    across_psi = exchange(x_psi, 1, every)
    own_2 = products(2, *own, (second, far_in))
    sent_2 = exchange(own_2, 8, every)

    x_left, sent_1 = lax.optimization_barrier((x_left, sent_1))
    across_left = exchange(x_left, 1, every)
    other = ([x_left, across_left], [x_psi, across_psi])
    other_1 = products(1, *other, (near,))
    other_sent_1 = exchange(other_1, 4, every)
    other_2 = products(2, *other, (second, far_in))
    other_sent_2 = exchange(other_2, 8, every)

    third, sent_2 = lax.optimization_barrier((third, sent_2))
    own_3 = products(3, *own, (third, middle))
    sent_3 = exchange(own_3, 12, every)
    other_3 = products(3, *other, (third, middle))
    other_sent_3 = exchange(other_3, 12, every)
    other_0 = products(0, *other, (right_env,))

    pieces = [own_0, other_0, sent_1, other_sent_1, sent_2, other_sent_2, sent_3, other_sent_3]
    out = place(me, pieces)[:, None]
    if ops > 1:
        out = lax.psum_scatter(out, "op", scatter_dimension=2, tiled=True).astype(jnp.bfloat16)
    return out


def solution(mesh):
    placed = (
        P(("group", "sec"), None, None, None),
        P(("group", "op"), "sec", None, None),
        P(("group", "op"), "sec", None, None),
        P(("group", "op"), None),
    )
    return jax.shard_map(
        functools.partial(on_device, mesh.shape["op"]),
        mesh=mesh,
        in_specs=placed,
        out_specs=P("group", "sec", "op", None),
        check_vma=False,
    )
```

```python
import functools

import jax
import jax.numpy as jnp
from jax import lax
from jax.experimental import pallas as pl
from jax.experimental.pallas import tpu as pltpu
from jax.sharding import PartitionSpec as P

HBM = pl.BlockSpec(memory_space=pltpu.HBM)
SMEM = pl.BlockSpec(memory_space=pltpu.SMEM)
VMEM = pl.BlockSpec(memory_space=pltpu.VMEM)


def slot_kernel(count, choices, meta, source, *refs):
    parts = (len(refs) - choices - 8) // count - 1
    lefts, refs = refs[: parts * count], refs[parts * count :]
    psis, rights = refs[:count], refs[count : count + choices]
    out, left_buf, psi_buf, right_buf, mid_buf, left_sem, psi_sem, right_sem = refs[count + choices :]
    terms, rows, columns = left_buf.shape[1:]
    q = meta[0]

    def left_copy(i, k):
        part, place = divmod(k, terms // parts)
        return pltpu.make_async_copy(lefts[i * parts + part].at[place, 0], left_buf.at[i, k], left_sem.at[i, k])

    def psi_copy(i, k):
        return pltpu.make_async_copy(psis[i].at[0, source[k, q]], psi_buf.at[i, k], psi_sem.at[i, k])

    def right_copy(k, choice):
        return pltpu.make_async_copy(
            rights[choice].at[k, 0], right_buf.at[:, pl.ds(k * columns, columns)], right_sem.at[k]
        )

    for k in range(terms):
        for i in range(count):
            left_copy(i, k).start()
            psi_copy(i, k).start()
    for choice in range(choices):

        @pl.when(meta[1] == choice)
        def _(choice=choice):
            for k in range(terms):
                right_copy(k, choice).start()

    for k in range(terms):
        for i in range(count):
            left_copy(i, k).wait()
            psi_copy(i, k).wait()
            mid = jnp.dot(left_buf[i, k], psi_buf[i, k], preferred_element_type=jnp.float32)
            mid_buf[pl.ds(i * rows, rows), pl.ds(k * columns, columns)] = mid.astype(jnp.bfloat16)
    for k in range(terms):
        right_copy(k, 0).wait()
    total = lax.dot_general(
        mid_buf[...], right_buf[...], (((1,), (1,)), ((), ())), preferred_element_type=jnp.float32
    )
    out[...] = total.reshape(out.shape).astype(out.dtype)


def slot(q, choice, source_map, lefts, psis, rights, dtype, flops):
    terms, _, rows, columns = rights[0].shape
    count = len(psis)
    meta = jnp.stack([q, choice if len(rights) > 1 else 0 * q]).astype(jnp.int32)
    return pl.pallas_call(
        functools.partial(slot_kernel, count, len(rights)),
        out_shape=jax.ShapeDtypeStruct((count, rows, columns), dtype),
        in_specs=[SMEM, SMEM] + [HBM] * (len(lefts) + count + len(rights)),
        out_specs=VMEM,
        scratch_shapes=[
            pltpu.VMEM((count, terms, rows, columns), jnp.bfloat16),
            pltpu.VMEM((count, terms, rows, columns), jnp.bfloat16),
            pltpu.VMEM((rows, terms * columns), jnp.bfloat16),
            pltpu.VMEM((count * rows, terms * columns), jnp.bfloat16),
            pltpu.SemaphoreType.DMA((count, terms)),
            pltpu.SemaphoreType.DMA((count, terms)),
            pltpu.SemaphoreType.DMA((terms,)),
        ],
        compiler_params=pltpu.CompilerParams(vmem_limit_bytes=60 << 20),
        cost_estimate=pl.CostEstimate(flops=flops, bytes_accessed=1, transcendentals=0),
    )(meta, source_map, *lefts, *psis, *rights)


def place_kernel(width, meta, *refs):
    pieces, out, sem = refs[:-2], refs[-2], refs[-1]
    me = meta[0]

    def copy(j):
        return pltpu.make_async_copy(pieces[j // width].at[j % width], out.at[me ^ j], sem.at[j])

    for j in range(len(pieces) * width):
        copy(j).start()
    for j in range(len(pieces) * width):
        copy(j).wait()


def place(me, pieces):
    width, rows, columns = pieces[0].shape
    sectors = width * len(pieces)
    return pl.pallas_call(
        functools.partial(place_kernel, width),
        out_shape=jax.ShapeDtypeStruct((sectors, rows, columns), pieces[0].dtype),
        in_specs=[SMEM] + [VMEM] * len(pieces),
        out_specs=HBM,
        scratch_shapes=[pltpu.SemaphoreType.DMA((sectors,))],
        compiler_params=pltpu.CompilerParams(vmem_limit_bytes=16 << 20),
    )(me[None].astype(jnp.int32), *pieces)


def exchange(array, bits, members):
    return lax.ppermute(array, "sec", [(s, s ^ bits) for s in members])


def on_device(ops, psi, left_env, right_env, source_map):
    me = lax.axis_index("sec")
    row = me // 4
    choice = jnp.where((row == 0) | (row == 3), 0, 1)
    dtype = jnp.bfloat16 if ops == 1 else jnp.float32
    every = range(16)
    inner = range(4, 12)
    half = left_env.shape[0] // 2

    def products(step, lefts, psis, rights, flops=1):
        return slot(me ^ (4 * step), choice, source_map, lefts, psis, rights, dtype, flops)

    near = exchange(right_env, 4, every)
    middle = exchange(right_env, 12, inner)
    x_psi = exchange(psi, 2, every)
    own = ([left_env, exchange(left_env, 1, every)], [psi, exchange(psi, 1, every)])
    own_0 = products(0, *own, (right_env,))

    near, middle, own_0 = lax.optimization_barrier((near, middle, own_0))
    far_in = exchange(near, 12, inner)
    second = exchange(middle, 4, inner)
    own_1 = products(1, *own, (near,))
    sent_1 = exchange(own_1, 4, every)

    x_psi, low_next, sent_1 = lax.optimization_barrier((x_psi, left_env[:half], sent_1))
    x_low = exchange(low_next, 2, every)
    across_psi = exchange(x_psi, 1, every)

    second, far_in = lax.optimization_barrier((second, far_in))
    third = exchange(far_in, 4, inner)
    own_2 = products(2, *own, (second, far_in))
    sent_2 = exchange(own_2, 8, every)

    own_2, high_next = lax.optimization_barrier((own_2, left_env[half:]))
    x_high = exchange(high_next, 2, every)
    x_low, x_high, sent_2 = lax.optimization_barrier((x_low, x_high, sent_2))
    across_low = exchange(x_low, 1, every)
    across_high = exchange(x_high, 1, every)
    other = ([x_low, x_high, across_low, across_high], [x_psi, across_psi])
    other_2 = products(2, *other, (second, far_in))
    other_sent_2 = exchange(other_2, 8, every)
    other_1 = products(1, *other, (near,))
    other_sent_1 = exchange(other_1, 4, every)

    third, other_1, other_2 = lax.optimization_barrier((third, other_1, other_2))
    own_3 = products(3, *own, (third, middle))
    sent_3 = exchange(own_3, 12, every)
    other_3 = products(3, *other, (third, middle))
    other_sent_3 = exchange(other_3, 12, every)
    right_last, other_sent_1, other_sent_2 = lax.optimization_barrier((right_env, other_sent_1, other_sent_2))
    other_0 = products(0, *other, (right_last,), flops=10**10)

    pieces = [own_0, other_0, sent_1, other_sent_1, sent_2, other_sent_2, sent_3, other_sent_3]
    out = place(me, pieces)[:, None]
    if ops > 1:
        out = lax.psum_scatter(out, "op", scatter_dimension=2, tiled=True).astype(jnp.bfloat16)
    return out


def solution(mesh):
    placed = (
        P(("group", "sec"), None, None, None),
        P(("group", "op"), "sec", None, None),
        P(("group", "op"), "sec", None, None),
        P(("group", "op"), None),
    )
    return jax.shard_map(
        functools.partial(on_device, mesh.shape["op"]),
        mesh=mesh,
        in_specs=placed,
        out_specs=P("group", "sec", "op", None),
        check_vma=False,
    )
```

```python
import functools

import jax
import jax.numpy as jnp
from jax import lax
from jax.experimental import pallas as pl
from jax.experimental.pallas import tpu as pltpu
from jax.sharding import PartitionSpec as P

HBM = pl.BlockSpec(memory_space=pltpu.HBM)
SMEM = pl.BlockSpec(memory_space=pltpu.SMEM)
VMEM = pl.BlockSpec(memory_space=pltpu.VMEM)


def slot_kernel(step, count, choices, source, *refs):
    parts = (len(refs) - choices - 3) // count - 1
    lefts, refs = refs[: parts * count], refs[parts * count :]
    psis, rights = refs[:count], refs[count : count + choices]
    out, right_buf, mid_buf = refs[count + choices :]
    terms, _, rows, columns = rights[0].shape
    me = lax.axis_index("sec")
    row = me >> 2
    q = me ^ (4 * step)
    outer = (row == 0) | (row == 3)

    for k in range(terms):
        span = pl.ds(k * columns, columns)
        part, place = divmod(k, terms // parts)
        right = rights[0][k, 0]
        if choices > 1:
            right = jnp.where(outer, right, rights[1][k, 0])
        right_buf[:, span] = right
        for i in range(count):
            mid = jnp.dot(
                lefts[i * parts + part][place, 0], psis[i][0, source[k, q]], preferred_element_type=jnp.float32
            )
            mid_buf[pl.ds(i * rows, rows), span] = mid.astype(jnp.bfloat16)
    total = lax.dot_general(
        mid_buf[...], right_buf[...], (((1,), (1,)), ((), ())), preferred_element_type=jnp.float32
    )
    out[...] = total.reshape(out.shape).astype(out.dtype)


def slot(step, source_map, lefts, psis, rights, dtype, flops):
    terms, _, rows, columns = rights[0].shape
    count = len(psis)
    return pl.pallas_call(
        functools.partial(slot_kernel, step, count, len(rights)),
        out_shape=jax.ShapeDtypeStruct((count, rows, columns), dtype),
        in_specs=[SMEM] + [VMEM] * (len(lefts) + count + len(rights)),
        out_specs=VMEM,
        scratch_shapes=[
            pltpu.VMEM((rows, terms * columns), jnp.bfloat16),
            pltpu.VMEM((count * rows, terms * columns), jnp.bfloat16),
        ],
        compiler_params=pltpu.CompilerParams(vmem_limit_bytes=24 << 20),
        cost_estimate=pl.CostEstimate(flops=flops, bytes_accessed=1, transcendentals=0),
    )(source_map, *lefts, *psis, *rights)


def split_kernel(whole, low, high):
    half = low.shape[0]
    low[...] = whole[:half]
    high[...] = whole[half:]


def split(array):
    half = jax.ShapeDtypeStruct((array.shape[0] // 2,) + array.shape[1:], array.dtype)
    return pl.pallas_call(
        split_kernel,
        out_shape=(half, half),
        in_specs=[VMEM],
        out_specs=(VMEM, VMEM),
        compiler_params=pltpu.CompilerParams(vmem_limit_bytes=8 << 20),
        cost_estimate=pl.CostEstimate(flops=1, bytes_accessed=1, transcendentals=0),
    )(array)


def place_kernel(width, *refs):
    pieces, out, sem = refs[:-2], refs[-2], refs[-1]
    me = lax.axis_index("sec")

    def copy(j):
        return pltpu.make_async_copy(pieces[j // width].at[j % width], out.at[me ^ j], sem.at[j])

    for j in range(len(pieces) * width):
        copy(j).start()
    for j in range(len(pieces) * width):
        copy(j).wait()


def place(pieces):
    width, rows, columns = pieces[0].shape
    sectors = width * len(pieces)
    return pl.pallas_call(
        functools.partial(place_kernel, width),
        out_shape=jax.ShapeDtypeStruct((sectors, rows, columns), pieces[0].dtype),
        in_specs=[VMEM] * len(pieces),
        out_specs=HBM,
        scratch_shapes=[pltpu.SemaphoreType.DMA((sectors,))],
        compiler_params=pltpu.CompilerParams(vmem_limit_bytes=16 << 20),
    )(*pieces)


def exchange(array, bits, members):
    return lax.ppermute(array, "sec", [(s, s ^ bits) for s in members])


def on_device(ops, psi, left_env, right_env, source_map):
    dtype = jnp.bfloat16 if ops == 1 else jnp.float32
    every = range(16)
    inner = range(4, 12)
    low, high = split(left_env)

    def products(step, lefts, psis, rights, flops=1):
        return slot(step, source_map, lefts, psis, rights, dtype, flops)

    near = exchange(right_env, 4, every)
    middle = exchange(right_env, 12, inner)
    x_psi = exchange(psi, 2, every)
    own = ([left_env, exchange(left_env, 1, every)], [psi, exchange(psi, 1, every)])
    own_0 = products(0, *own, (right_env,))

    near, middle, own_0 = lax.optimization_barrier((near, middle, own_0))
    far_in = exchange(near, 12, inner)
    second = exchange(middle, 4, inner)
    own_1 = products(1, *own, (near,))
    sent_1 = exchange(own_1, 4, every)

    x_psi, low = lax.optimization_barrier((x_psi, low))
    x_low = exchange(low, 2, every)
    across_psi = exchange(x_psi, 1, every)

    second, far_in = lax.optimization_barrier((second, far_in))
    third = exchange(far_in, 4, inner)
    own_2 = products(2, *own, (second, far_in))
    sent_2 = exchange(own_2, 8, every)

    own_2, sent_1, high = lax.optimization_barrier((own_2, sent_1, high))
    x_high = exchange(high, 2, every)
    x_low, x_high, sent_2 = lax.optimization_barrier((x_low, x_high, sent_2))
    across_low = exchange(x_low, 1, every)
    across_high = exchange(x_high, 1, every)
    other = ([x_low, x_high, across_low, across_high], [x_psi, across_psi])
    other_2 = products(2, *other, (second, far_in))
    other_sent_2 = exchange(other_2, 8, every)
    other_1 = products(1, *other, (near,))
    other_sent_1 = exchange(other_1, 4, every)

    third, other_1, other_2 = lax.optimization_barrier((third, other_1, other_2))
    own_3 = products(3, *own, (third, middle))
    sent_3 = exchange(own_3, 12, every)
    other_3 = products(3, *other, (third, middle))
    other_sent_3 = exchange(other_3, 12, every)
    right_last, other_sent_1, other_sent_2 = lax.optimization_barrier((right_env, other_sent_1, other_sent_2))
    other_0 = products(0, *other, (right_last,), flops=10**10)

    pieces = [own_0, other_0, sent_1, other_sent_1, sent_2, other_sent_2, sent_3, other_sent_3]
    out = place(pieces)[:, None]
    if ops > 1:
        out = lax.psum_scatter(out, "op", scatter_dimension=2, tiled=True).astype(jnp.bfloat16)
    return out


def solution(mesh):
    placed = (
        P(("group", "sec"), None, None, None),
        P(("group", "op"), "sec", None, None),
        P(("group", "op"), "sec", None, None),
        P(("group", "op"), None),
    )
    return jax.shard_map(
        functools.partial(on_device, mesh.shape["op"]),
        mesh=mesh,
        in_specs=placed,
        out_specs=P("group", "sec", "op", None),
        check_vma=False,
    )
```

```python
import functools

import jax
import jax.numpy as jnp
from jax import lax
from jax.experimental import pallas as pl
from jax.experimental.pallas import tpu as pltpu
from jax.sharding import PartitionSpec as P

HBM = pl.BlockSpec(memory_space=pltpu.HBM)
SMEM = pl.BlockSpec(memory_space=pltpu.SMEM)
VMEM = pl.BlockSpec(memory_space=pltpu.VMEM)


def slot_kernel(step, parts, choices, source, *refs):
    count = len(parts)
    lefts, refs = refs[:count], refs[count:]
    psis = []
    for number in parts:
        psis.append(refs[:number])
        refs = refs[number:]
    rights = refs[:choices]
    out, right_buf, mid_buf = refs[choices:]
    terms, _, rows, columns = rights[0].shape
    me = lax.axis_index("sec")
    row = me >> 2
    q = me ^ (4 * step)
    outer = (row == 0) | (row == 3)

    def psi_block(held, sector):
        block, first = None, 0
        for part in held:
            size = part.shape[1]
            if block is None:
                block = part[0, jnp.minimum(sector, size - 1)]
            else:
                block = jnp.where(sector >= first, part[0, jnp.maximum(sector - first, 0)], block)
            first += size
        return block

    for k in range(terms):
        span = pl.ds(k * columns, columns)
        right = rights[0][k, 0]
        if choices > 1:
            right = jnp.where(outer, right, rights[1][k, 0])
        right_buf[:, span] = right
        for i in range(count):
            mid = jnp.dot(lefts[i][k, 0], psi_block(psis[i], source[k, q]), preferred_element_type=jnp.float32)
            mid_buf[pl.ds(i * rows, rows), span] = mid.astype(jnp.bfloat16)
    total = lax.dot_general(
        mid_buf[...], right_buf[...], (((1,), (1,)), ((), ())), preferred_element_type=jnp.float32
    )
    out[...] = total.reshape(out.shape).astype(out.dtype)


def slot(step, source_map, lefts, psis, rights, dtype, flops):
    terms, _, rows, columns = rights[0].shape
    count = len(psis)
    parts = tuple(len(psi) for psi in psis)
    return pl.pallas_call(
        functools.partial(slot_kernel, step, parts, len(rights)),
        out_shape=jax.ShapeDtypeStruct((count, rows, columns), dtype),
        in_specs=[SMEM] + [VMEM] * (count + sum(parts) + len(rights)),
        out_specs=VMEM,
        scratch_shapes=[
            pltpu.VMEM((rows, terms * columns), jnp.bfloat16),
            pltpu.VMEM((count * rows, terms * columns), jnp.bfloat16),
        ],
        compiler_params=pltpu.CompilerParams(vmem_limit_bytes=24 << 20),
        cost_estimate=pl.CostEstimate(flops=flops, bytes_accessed=1, transcendentals=0),
    )(source_map, *lefts, *[part for psi in psis for part in psi], *rights)


def split_kernel(whole, low, high):
    first = low.shape[1]
    low[...] = whole[:, :first]
    high[...] = whole[:, first:]


def split(array, first):
    sizes = (first, array.shape[1] - first)
    return pl.pallas_call(
        split_kernel,
        out_shape=tuple(
            jax.ShapeDtypeStruct((array.shape[0], size) + array.shape[2:], array.dtype) for size in sizes
        ),
        in_specs=[VMEM],
        out_specs=(VMEM, VMEM),
        compiler_params=pltpu.CompilerParams(vmem_limit_bytes=12 << 20),
        cost_estimate=pl.CostEstimate(flops=1, bytes_accessed=1, transcendentals=0),
    )(array)


def place_kernel(*refs):
    pieces, out, sem = refs[:-2], refs[-2], refs[-1]
    me = lax.axis_index("sec")
    blocks = [piece.at[i] for piece in pieces for i in range(piece.shape[0])]
    copies = [pltpu.make_async_copy(block, out.at[me ^ j], sem.at[j]) for j, block in enumerate(blocks)]
    for copy in copies:
        copy.start()
    for copy in copies:
        copy.wait()


def place(pieces):
    sectors = sum(piece.shape[0] for piece in pieces)
    return pl.pallas_call(
        place_kernel,
        out_shape=jax.ShapeDtypeStruct((sectors,) + pieces[0].shape[1:], pieces[0].dtype),
        in_specs=[VMEM] * len(pieces),
        out_specs=HBM,
        scratch_shapes=[pltpu.SemaphoreType.DMA((sectors,))],
        compiler_params=pltpu.CompilerParams(vmem_limit_bytes=16 << 20),
    )(*pieces)


def exchange(array, bits, members):
    return lax.ppermute(array, "sec", [(s, s ^ bits) for s in members])


def on_device(ops, psi, left_env, right_env, source_map):
    dtype = jnp.bfloat16 if ops == 1 else jnp.float32
    every = range(16)
    inner = range(4, 12)
    low, high = split(psi, 9 * psi.shape[1] // 16)

    def products(step, lefts, psis, rights, flops=1):
        return slot(step, source_map, lefts, psis, rights, dtype, flops)

    near = exchange(right_env, 4, every)
    middle = exchange(right_env, 12, inner)
    x_left = exchange(left_env, 2, every)
    own = ([left_env, exchange(left_env, 1, every)], [(psi,), (exchange(psi, 1, every),)])
    own_0 = products(0, *own, (right_env,))

    near, middle, x_left, own_0, low = lax.optimization_barrier((near, middle, x_left, own_0, low))
    far_in = exchange(near, 12, inner)
    second = exchange(middle, 4, inner)
    x_low = exchange(low, 2, every)
    across_left = exchange(x_left, 1, every)
    own_1 = products(1, *own, (near,))
    sent_1 = exchange(own_1, 4, every)

    third = exchange(far_in, 4, inner)
    sent_1, high = lax.optimization_barrier((sent_1, high))
    x_high = exchange(high, 2, every)
    across_low = exchange(x_low, 1, every)
    own_2 = products(2, *own, (second, far_in))
    sent_2 = exchange(own_2, 8, every)

    x_high, sent_2 = lax.optimization_barrier((x_high, sent_2))
    across_high = exchange(x_high, 1, every)
    other = ([x_left, across_left], [(x_low, x_high), (across_low, across_high)])
    other_2 = products(2, *other, (second, far_in))
    other_sent_2 = exchange(other_2, 8, every)
    other_1 = products(1, *other, (near,))
    other_sent_1 = exchange(other_1, 4, every)

    third, other_1, other_2 = lax.optimization_barrier((third, other_1, other_2))
    last_3 = products(3, own[0] + other[0], own[1] + other[1], (third, middle), flops=10**10)
    sent_3 = exchange(last_3, 12, every)
    right_last, other_sent_1, other_sent_2 = lax.optimization_barrier((right_env, other_sent_1, other_sent_2))
    other_0 = products(0, *other, (right_last,), flops=10**10)

    pieces = [own_0, other_0, sent_1, other_sent_1, sent_2, other_sent_2, sent_3]
    out = place(pieces)[:, None]
    if ops > 1:
        out = lax.psum_scatter(out, "op", scatter_dimension=2, tiled=True).astype(jnp.bfloat16)
    return out


def solution(mesh):
    placed = (
        P(("group", "sec"), None, None, None),
        P(("group", "op"), "sec", None, None),
        P(("group", "op"), "sec", None, None),
        P(("group", "op"), None),
    )
    return jax.shard_map(
        functools.partial(on_device, mesh.shape["op"]),
        mesh=mesh,
        in_specs=placed,
        out_specs=P("group", "sec", "op", None),
        check_vma=False,
    )
```

```python
import functools

import jax
import jax.numpy as jnp
from jax import lax
from jax.experimental import pallas as pl
from jax.experimental.pallas import tpu as pltpu
from jax.sharding import PartitionSpec as P

HBM = pl.BlockSpec(memory_space=pltpu.HBM)
SMEM = pl.BlockSpec(memory_space=pltpu.SMEM)
VMEM = pl.BlockSpec(memory_space=pltpu.VMEM)


def slot_kernel(step, parts, choices, source, *refs):
    count = len(parts)
    lefts, psis = [], []
    for number, _ in parts:
        lefts.append(refs[:number])
        refs = refs[number:]
    for _, number in parts:
        psis.append(refs[:number])
        refs = refs[number:]
    rights = refs[:choices]
    out, right_buf, mid_buf = refs[choices:]
    terms, _, rows, columns = rights[0].shape
    me = lax.axis_index("sec")
    row = me >> 2
    q = me ^ (4 * step)
    outer = (row == 0) | (row == 3)

    def psi_block(held, sector):
        if len(held) == 1:
            return held[0][0, sector]
        low, high = held
        size = low.shape[1]
        return jnp.where(
            sector < size, low[0, jnp.minimum(sector, size - 1)], high[0, jnp.maximum(sector - size, 0)]
        )

    for k in range(terms):
        span = pl.ds(k * columns, columns)
        right = rights[0][k, 0]
        if choices > 1:
            right = jnp.where(outer, right, rights[1][k, 0])
        right_buf[:, span] = right
        for i in range(count):
            part, place = divmod(k, terms // len(lefts[i]))
            mid = jnp.dot(lefts[i][part][place, 0], psi_block(psis[i], source[k, q]), preferred_element_type=jnp.float32)
            mid_buf[pl.ds(i * rows, rows), span] = mid.astype(jnp.bfloat16)
    total = lax.dot_general(
        mid_buf[...], right_buf[...], (((1,), (1,)), ((), ())), preferred_element_type=jnp.float32
    )
    out[...] = total.reshape(out.shape).astype(out.dtype)


def slot(step, source_map, lefts, psis, rights, dtype, flops):
    terms, _, rows, columns = rights[0].shape
    count = len(psis)
    parts = tuple((len(left), len(psi)) for left, psi in zip(lefts, psis))
    held = [part for left in lefts for part in left] + [part for psi in psis for part in psi] + list(rights)
    return pl.pallas_call(
        functools.partial(slot_kernel, step, parts, len(rights)),
        out_shape=jax.ShapeDtypeStruct((count, rows, columns), dtype),
        in_specs=[SMEM] + [VMEM] * len(held),
        out_specs=VMEM,
        scratch_shapes=[
            pltpu.VMEM((rows, terms * columns), jnp.bfloat16),
            pltpu.VMEM((count * rows, terms * columns), jnp.bfloat16),
        ],
        compiler_params=pltpu.CompilerParams(vmem_limit_bytes=24 << 20),
        cost_estimate=pl.CostEstimate(flops=flops, bytes_accessed=1, transcendentals=0),
    )(source_map, *held)


def split_kernel(axis, whole, low, high):
    half = low.shape[axis]
    before = (slice(None),) * axis
    low[...] = whole[(*before, slice(0, half))]
    high[...] = whole[(*before, slice(half, None))]


def split(array, axis):
    shape = list(array.shape)
    shape[axis] //= 2
    half = jax.ShapeDtypeStruct(tuple(shape), array.dtype)
    return pl.pallas_call(
        functools.partial(split_kernel, axis),
        out_shape=(half, half),
        in_specs=[VMEM],
        out_specs=(VMEM, VMEM),
        compiler_params=pltpu.CompilerParams(vmem_limit_bytes=12 << 20),
        cost_estimate=pl.CostEstimate(flops=1, bytes_accessed=1, transcendentals=0),
    )(array)


def place_kernel(*refs):
    pieces, out, sem = refs[:-2], refs[-2], refs[-1]
    me = lax.axis_index("sec")
    row = me >> 2
    outer = (row == 0) | (row == 3)

    def copies(pieces, first):
        blocks = [piece.at[i] for piece in pieces for i in range(piece.shape[0])]
        return [
            pltpu.make_async_copy(block, out.at[me ^ (j ^ 2)], sem.at[j]) for j, block in enumerate(blocks, first)
        ]

    last = out.shape[0] - pieces[-1].shape[0]
    shared = copies(pieces[:-2], 0)
    for copy in shared:
        copy.start()

    @pl.when(outer)
    def _():
        for copy in copies(pieces[-2:-1], last):
            copy.start()

    @pl.when(jnp.logical_not(outer))
    def _():
        for copy in copies(pieces[-1:], last):
            copy.start()

    for copy in shared + copies(pieces[-1:], last):
        copy.wait()


def place(pieces):
    sectors = sum(piece.shape[0] for piece in pieces[:-1])
    return pl.pallas_call(
        place_kernel,
        out_shape=jax.ShapeDtypeStruct((sectors,) + pieces[0].shape[1:], pieces[0].dtype),
        in_specs=[VMEM] * len(pieces),
        out_specs=HBM,
        scratch_shapes=[pltpu.SemaphoreType.DMA((sectors,))],
        compiler_params=pltpu.CompilerParams(vmem_limit_bytes=16 << 20),
    )(*pieces)


def exchange(array, bits, members):
    return lax.ppermute(array, "sec", [(s, s ^ bits) for s in members])


def on_device(ops, psi, left_env, right_env, source_map):
    dtype = jnp.bfloat16 if ops == 1 else jnp.float32
    every = range(16)
    inner = range(4, 12)
    outer = [s for s in every if s not in inner]

    def products(step, lefts, psis, rights, flops=1):
        return slot(step, source_map, lefts, psis, rights, dtype, flops)

    near = exchange(right_env, 4, every)
    middle = exchange(right_env, 12, inner)
    x_psi = exchange(psi, 2, every)
    own = ([(left_env,), (exchange(left_env, 1, every),)], [(psi,), (exchange(psi, 1, every),)])
    own_0 = products(0, *own, (right_env,))

    near, middle, own_0 = lax.optimization_barrier((near, middle, own_0))
    far_in = exchange(near, 12, inner)
    second = exchange(middle, 4, inner)
    own_1 = products(1, *own, (near,))
    sent_1 = exchange(own_1, 4, every)

    x_psi, left_next = lax.optimization_barrier((x_psi, left_env))
    x_left = exchange(left_next, 2, every)
    across_psi = [exchange(part, 1, every) for part in split(x_psi, 1)]

    second, far_in = lax.optimization_barrier((second, far_in))
    third = exchange(far_in, 4, inner)
    second, *across_psi = lax.optimization_barrier((second, *across_psi))
    own_2 = products(2, *own, (second, far_in))
    sent_2 = exchange(own_2, 8, every)
    own_middle = products(3, *own, (middle,))
    sent_middle = exchange(own_middle, 12, inner)

    x_left, sent_1, sent_2 = lax.optimization_barrier((x_left, sent_1, sent_2))
    across_left = [exchange(part, 1, every) for part in split(x_left, 0)]
    other = ([(x_left,), across_left], [(x_psi,), across_psi])
    other_2 = products(2, *other, (second, far_in))
    other_sent_2 = exchange(other_2, 8, every)
    near, sent_middle, other_2 = lax.optimization_barrier((near, sent_middle, other_2))
    other_1 = products(1, *other, (near,))
    other_sent_1 = exchange(other_1, 4, every)

    third, other_1, other_2 = lax.optimization_barrier((third, other_1, other_2))
    other_3 = products(3, *other, (third, middle), flops=10**10)
    other_sent_3 = exchange(other_3, 12, every)
    third, other_3 = lax.optimization_barrier((third, other_3))
    own_third = products(3, *own, (third,))
    sent_third = exchange(own_third, 12, outer)
    right_last, other_sent_1, other_sent_2 = lax.optimization_barrier((right_env, other_sent_1, other_sent_2))
    other_0 = products(0, *other, (right_last,), flops=10**10)

    pieces = [other_0, own_0, other_sent_1, sent_1, other_sent_2, sent_2, other_sent_3, sent_third, sent_middle]
    out = place(pieces)[:, None]
    if ops > 1:
        out = lax.psum_scatter(out, "op", scatter_dimension=2, tiled=True).astype(jnp.bfloat16)
    return out


def solution(mesh):
    placed = (
        P(("group", "sec"), None, None, None),
        P(("group", "op"), "sec", None, None),
        P(("group", "op"), "sec", None, None),
        P(("group", "op"), None),
    )
    return jax.shard_map(
        functools.partial(on_device, mesh.shape["op"]),
        mesh=mesh,
        in_specs=placed,
        out_specs=P("group", "sec", "op", None),
        check_vma=False,
    )
```

```python
import functools

import jax
import jax.numpy as jnp
from jax import lax
from jax.experimental import pallas as pl
from jax.experimental.pallas import tpu as pltpu
from jax.sharding import PartitionSpec as P

HBM = pl.BlockSpec(memory_space=pltpu.HBM)
SMEM = pl.BlockSpec(memory_space=pltpu.SMEM)
VMEM = pl.BlockSpec(memory_space=pltpu.VMEM)


def slot_kernel(step, parts, choices, source, *refs):
    count = len(parts)
    lefts, psis = [], []
    for number, _ in parts:
        lefts.append(refs[:number])
        refs = refs[number:]
    for _, number in parts:
        psis.append(refs[:number])
        refs = refs[number:]
    rights = refs[:choices]
    out, right_buf, mid_buf = refs[choices:]
    terms, _, rows, columns = rights[0].shape
    me = lax.axis_index("sec")
    row = me >> 2
    q = me ^ (4 * step)
    outer = (row == 0) | (row == 3)

    def psi_block(held, sector):
        if len(held) == 1:
            return held[0][0, sector]
        low, high = held
        size = low.shape[1]
        return jnp.where(
            sector < size, low[0, jnp.minimum(sector, size - 1)], high[0, jnp.maximum(sector - size, 0)]
        )

    for k in range(terms):
        span = pl.ds(k * columns, columns)
        right = rights[0][k, 0]
        if choices > 1:
            right = jnp.where(outer, right, rights[1][k, 0])
        right_buf[:, span] = right
        for i in range(count):
            part, place = divmod(k, terms // len(lefts[i]))
            mid = jnp.dot(lefts[i][part][place, 0], psi_block(psis[i], source[k, q]), preferred_element_type=jnp.float32)
            mid_buf[pl.ds(i * rows, rows), span] = mid.astype(jnp.bfloat16)
    total = lax.dot_general(
        mid_buf[...], right_buf[...], (((1,), (1,)), ((), ())), preferred_element_type=jnp.float32
    )
    out[...] = total.reshape(out.shape).astype(out.dtype)


def slot(step, source_map, lefts, psis, rights, dtype, flops):
    terms, _, rows, columns = rights[0].shape
    count = len(psis)
    parts = tuple((len(left), len(psi)) for left, psi in zip(lefts, psis))
    held = [part for left in lefts for part in left] + [part for psi in psis for part in psi] + list(rights)
    return pl.pallas_call(
        functools.partial(slot_kernel, step, parts, len(rights)),
        out_shape=jax.ShapeDtypeStruct((count, rows, columns), dtype),
        in_specs=[SMEM] + [VMEM] * len(held),
        out_specs=VMEM,
        scratch_shapes=[
            pltpu.VMEM((rows, terms * columns), jnp.bfloat16),
            pltpu.VMEM((count * rows, terms * columns), jnp.bfloat16),
        ],
        compiler_params=pltpu.CompilerParams(vmem_limit_bytes=24 << 20),
        cost_estimate=pl.CostEstimate(flops=flops, bytes_accessed=1, transcendentals=0),
    )(source_map, *held)


def split_kernel(whole, low, high):
    half = low.shape[0]
    low[...] = whole[:half]
    high[...] = whole[half:]


def split(array):
    half = jax.ShapeDtypeStruct((array.shape[0] // 2,) + array.shape[1:], array.dtype)
    return pl.pallas_call(
        split_kernel,
        out_shape=(half, half),
        in_specs=[VMEM],
        out_specs=(VMEM, VMEM),
        compiler_params=pltpu.CompilerParams(vmem_limit_bytes=8 << 20),
        cost_estimate=pl.CostEstimate(flops=1, bytes_accessed=1, transcendentals=0),
    )(array)


def place_kernel(*refs):
    pieces, out, sem = refs[:-2], refs[-2], refs[-1]
    me = lax.axis_index("sec")
    row = me >> 2
    outer = (row == 0) | (row == 3)

    def copies(pieces, first):
        blocks = [piece.at[i] for piece in pieces for i in range(piece.shape[0])]
        return [
            pltpu.make_async_copy(block, out.at[me ^ j], sem.at[j]) for j, block in enumerate(blocks, first)
        ]

    last = out.shape[0] - pieces[-1].shape[0]
    shared = copies(pieces[:-2], 0)
    for copy in shared:
        copy.start()

    @pl.when(outer)
    def _():
        for copy in copies(pieces[-2:-1], last):
            copy.start()

    @pl.when(jnp.logical_not(outer))
    def _():
        for copy in copies(pieces[-1:], last):
            copy.start()

    for copy in shared + copies(pieces[-1:], last):
        copy.wait()


def place(pieces):
    sectors = sum(piece.shape[0] for piece in pieces[:-1])
    return pl.pallas_call(
        place_kernel,
        out_shape=jax.ShapeDtypeStruct((sectors,) + pieces[0].shape[1:], pieces[0].dtype),
        in_specs=[VMEM] * len(pieces),
        out_specs=HBM,
        scratch_shapes=[pltpu.SemaphoreType.DMA((sectors,))],
        compiler_params=pltpu.CompilerParams(vmem_limit_bytes=16 << 20),
    )(*pieces)


def exchange(array, bits, members):
    return lax.ppermute(array, "sec", [(s, s ^ bits) for s in members])


def on_device(ops, psi, left_env, right_env, source_map):
    dtype = jnp.bfloat16 if ops == 1 else jnp.float32
    every = range(16)
    inner = range(4, 12)
    outer = [s for s in every if s not in inner]
    low, high = split(left_env)

    def products(step, lefts, psis, rights, flops=1):
        return slot(step, source_map, lefts, psis, rights, dtype, flops)

    near = exchange(right_env, 4, every)
    middle = exchange(right_env, 12, inner)
    x_psi = exchange(psi, 2, every)
    own = ([(left_env,), (exchange(left_env, 1, every),)], [(psi,), (exchange(psi, 1, every),)])
    own_0 = products(0, *own, (right_env,))

    near, middle, own_0 = lax.optimization_barrier((near, middle, own_0))
    far_in = exchange(near, 12, inner)
    second = exchange(middle, 4, inner)
    own_1 = products(1, *own, (near,))
    sent_1 = exchange(own_1, 4, every)

    x_psi, low = lax.optimization_barrier((x_psi, low))
    x_low = exchange(low, 2, every)
    across_psi = exchange(x_psi, 1, every)

    second, far_in = lax.optimization_barrier((second, far_in))
    third = exchange(far_in, 4, inner)
    own_2 = products(2, *own, (second, far_in))
    sent_2 = exchange(own_2, 8, every)

    own_2, sent_1, high = lax.optimization_barrier((own_2, sent_1, high))
    x_high = exchange(high, 2, every)
    x_low, x_high, sent_2 = lax.optimization_barrier((x_low, x_high, sent_2))
    across_low = exchange(x_low, 1, every)
    across_high = exchange(x_high, 1, every)
    other = ([(x_low, x_high), (across_low, across_high)], [(x_psi,), (across_psi,)])
    other_2 = products(2, *other, (second, far_in))
    other_sent_2 = exchange(other_2, 8, every)
    both = (own[0] + other[0], own[1] + other[1])
    last_middle = products(3, *both, (middle,))
    sent_middle = exchange(last_middle, 12, inner)
    near, other_2, last_middle = lax.optimization_barrier((near, other_2, last_middle))
    other_1 = products(1, *other, (near,))
    other_sent_1 = exchange(other_1, 4, every)

    third, other_1 = lax.optimization_barrier((third, other_1))
    last_third = products(3, *both, (third,))
    sent_third = exchange(last_third, 12, outer)
    right_last, other_sent_1, other_sent_2 = lax.optimization_barrier((right_env, other_sent_1, other_sent_2))
    other_0 = products(0, *other, (right_last,), flops=10**10)

    pieces = [own_0, other_0, sent_1, other_sent_1, sent_2, other_sent_2, sent_third, sent_middle]
    out = place(pieces)[:, None]
    if ops > 1:
        out = lax.psum_scatter(out, "op", scatter_dimension=2, tiled=True).astype(jnp.bfloat16)
    return out


def solution(mesh):
    placed = (
        P(("group", "sec"), None, None, None),
        P(("group", "op"), "sec", None, None),
        P(("group", "op"), "sec", None, None),
        P(("group", "op"), None),
    )
    return jax.shard_map(
        functools.partial(on_device, mesh.shape["op"]),
        mesh=mesh,
        in_specs=placed,
        out_specs=P("group", "sec", "op", None),
        check_vma=False,
    )
```

```python
import functools

import jax
import jax.numpy as jnp
from jax import lax
from jax.experimental import pallas as pl
from jax.experimental.pallas import tpu as pltpu
from jax.sharding import PartitionSpec as P

HBM = pl.BlockSpec(memory_space=pltpu.HBM)
SMEM = pl.BlockSpec(memory_space=pltpu.SMEM)
VMEM = pl.BlockSpec(memory_space=pltpu.VMEM)


def slot_kernel(step, parts, choices, source, *refs):
    count = len(parts)
    lefts, psis = [], []
    for number, _ in parts:
        lefts.append(refs[:number])
        refs = refs[number:]
    for _, number in parts:
        psis.append(refs[:number])
        refs = refs[number:]
    rights = refs[:choices]
    out, right_buf, mid_buf = refs[choices:]
    terms, _, rows, columns = rights[0].shape
    me = lax.axis_index("sec")
    row = me >> 2
    q = me ^ (4 * step)
    outer = (row == 0) | (row == 3)

    def psi_block(held, sector):
        if len(held) == 1:
            return held[0][0, sector]
        low, high = held
        size = low.shape[1]
        return jnp.where(
            sector < size, low[0, jnp.minimum(sector, size - 1)], high[0, jnp.maximum(sector - size, 0)]
        )

    for k in range(terms):
        span = pl.ds(k * columns, columns)
        right = rights[0][k, 0]
        if choices > 1:
            right = jnp.where(outer, right, rights[1][k, 0])
        right_buf[:, span] = right
        for i in range(count):
            part, place = divmod(k, terms // len(lefts[i]))
            mid = jnp.dot(lefts[i][part][place, 0], psi_block(psis[i], source[k, q]), preferred_element_type=jnp.float32)
            mid_buf[pl.ds(i * rows, rows), span] = mid.astype(jnp.bfloat16)
    total = lax.dot_general(
        mid_buf[...], right_buf[...], (((1,), (1,)), ((), ())), preferred_element_type=jnp.float32
    )
    out[...] = total.reshape(out.shape).astype(out.dtype)


def slot(step, source_map, lefts, psis, rights, dtype, flops):
    terms, _, rows, columns = rights[0].shape
    count = len(psis)
    parts = tuple((len(left), len(psi)) for left, psi in zip(lefts, psis))
    held = [part for left in lefts for part in left] + [part for psi in psis for part in psi] + list(rights)
    return pl.pallas_call(
        functools.partial(slot_kernel, step, parts, len(rights)),
        out_shape=jax.ShapeDtypeStruct((count, rows, columns), dtype),
        in_specs=[SMEM] + [VMEM] * len(held),
        out_specs=VMEM,
        scratch_shapes=[
            pltpu.VMEM((rows, terms * columns), jnp.bfloat16),
            pltpu.VMEM((count * rows, terms * columns), jnp.bfloat16),
        ],
        compiler_params=pltpu.CompilerParams(vmem_limit_bytes=24 << 20),
        cost_estimate=pl.CostEstimate(flops=flops, bytes_accessed=1, transcendentals=0),
    )(source_map, *held)


def split_kernel(whole, low, high):
    half = low.shape[0]
    low[...] = whole[:half]
    high[...] = whole[half:]


def split(array):
    half = jax.ShapeDtypeStruct((array.shape[0] // 2,) + array.shape[1:], array.dtype)
    return pl.pallas_call(
        split_kernel,
        out_shape=(half, half),
        in_specs=[VMEM],
        out_specs=(VMEM, VMEM),
        compiler_params=pltpu.CompilerParams(vmem_limit_bytes=8 << 20),
        cost_estimate=pl.CostEstimate(flops=1, bytes_accessed=1, transcendentals=0),
    )(array)


def place_kernel(*refs):
    pieces, out, sem = refs[:-2], refs[-2], refs[-1]
    me = lax.axis_index("sec")
    row = me >> 2
    outer = (row == 0) | (row == 3)

    def copies(pieces, first):
        blocks = [piece.at[i] for piece in pieces for i in range(piece.shape[0])]
        return [
            pltpu.make_async_copy(block, out.at[me ^ j], sem.at[j]) for j, block in enumerate(blocks, first)
        ]

    last = out.shape[0] - pieces[-1].shape[0]
    shared = copies(pieces[:-2], 0)
    for copy in shared:
        copy.start()

    @pl.when(outer)
    def _():
        for copy in copies(pieces[-2:-1], last):
            copy.start()

    @pl.when(jnp.logical_not(outer))
    def _():
        for copy in copies(pieces[-1:], last):
            copy.start()

    for copy in shared + copies(pieces[-1:], last):
        copy.wait()


def place(pieces):
    sectors = sum(piece.shape[0] for piece in pieces[:-1])
    return pl.pallas_call(
        place_kernel,
        out_shape=jax.ShapeDtypeStruct((sectors,) + pieces[0].shape[1:], pieces[0].dtype),
        in_specs=[VMEM] * len(pieces),
        out_specs=HBM,
        scratch_shapes=[pltpu.SemaphoreType.DMA((sectors,))],
        compiler_params=pltpu.CompilerParams(vmem_limit_bytes=16 << 20),
    )(*pieces)


def exchange(array, bits, members):
    return lax.ppermute(array, "sec", [(s, s ^ bits) for s in members])


def on_device(ops, psi, left_env, right_env, source_map):
    dtype = jnp.bfloat16 if ops == 1 else jnp.float32
    every = range(16)
    inner = range(4, 12)
    outer = [s for s in every if s not in inner]
    low, high = split(left_env)

    def products(step, lefts, psis, rights, flops=1):
        return slot(step, source_map, lefts, psis, rights, dtype, flops)

    near = exchange(right_env, 4, every)
    middle = exchange(right_env, 12, inner)
    x_psi = exchange(psi, 2, every)
    own = ([(left_env,), (exchange(left_env, 1, every),)], [(psi,), (exchange(psi, 1, every),)])
    own_0 = products(0, *own, (right_env,))

    near, middle, own_0 = lax.optimization_barrier((near, middle, own_0))
    far_in = exchange(near, 12, inner)
    second = exchange(middle, 4, inner)
    own_1 = products(1, *own, (near,))
    sent_1 = exchange(own_1, 4, every)

    x_psi, low = lax.optimization_barrier((x_psi, low))
    x_low = exchange(low, 2, every)
    across_psi = exchange(x_psi, 1, every)

    second, far_in = lax.optimization_barrier((second, far_in))
    third = exchange(far_in, 4, inner)
    own_2 = products(2, *own, (second, far_in))
    sent_2 = exchange(own_2, 8, every)

    own_2, sent_1, high = lax.optimization_barrier((own_2, sent_1, high))
    x_high = exchange(high, 2, every)
    x_low, x_high, sent_2 = lax.optimization_barrier((x_low, x_high, sent_2))
    across_low = exchange(x_low, 1, every)
    across_high = exchange(x_high, 1, every)
    other = ([(x_low, x_high), (across_low, across_high)], [(x_psi,), (across_psi,)])
    both = (own[0] + other[0], own[1] + other[1])
    other_2 = products(2, *other, (second, far_in))
    other_sent_2 = exchange(other_2, 8, every)
    last_middle = products(3, *both, (middle,))
    sent_middle = exchange(last_middle, 12, inner)
    other_1 = products(1, *other, (near,))
    other_sent_1 = exchange(other_1, 4, every)

    third, other_1, other_2, last_middle = lax.optimization_barrier((third, other_1, other_2, last_middle))
    last_third = products(3, *both, (third,))
    sent_third = exchange(last_third, 12, outer)
    right_last, other_sent_2, other_sent_1 = lax.optimization_barrier((right_env, other_sent_2, other_sent_1))
    other_0 = products(0, *other, (right_last,), flops=10**10)

    pieces = [own_0, other_0, sent_1, other_sent_1, sent_2, other_sent_2, sent_third, sent_middle]
    out = place(pieces)[:, None]
    if ops > 1:
        out = lax.psum_scatter(out, "op", scatter_dimension=2, tiled=True).astype(jnp.bfloat16)
    return out


def solution(mesh):
    placed = (
        P(("group", "sec"), None, None, None),
        P(("group", "op"), "sec", None, None),
        P(("group", "op"), "sec", None, None),
        P(("group", "op"), None),
    )
    return jax.shard_map(
        functools.partial(on_device, mesh.shape["op"]),
        mesh=mesh,
        in_specs=placed,
        out_specs=P("group", "sec", "op", None),
        check_vma=False,
    )
```

```python
import functools

import jax
import jax.numpy as jnp
from jax import lax
from jax.experimental import pallas as pl
from jax.experimental.pallas import tpu as pltpu
from jax.sharding import PartitionSpec as P

HBM = pl.BlockSpec(memory_space=pltpu.HBM)
SMEM = pl.BlockSpec(memory_space=pltpu.SMEM)
VMEM = pl.BlockSpec(memory_space=pltpu.VMEM)


def slot_kernel(step, parts, choices, source, *refs):
    count = len(parts)
    lefts, psis = [], []
    for number, _ in parts:
        lefts.append(refs[:number])
        refs = refs[number:]
    for _, number in parts:
        psis.append(refs[:number])
        refs = refs[number:]
    rights = refs[:choices]
    out, mid_buf, right_buf = refs[choices:]
    terms, _, rows, columns = rights[0].shape
    me = lax.axis_index("sec")
    row = me >> 2
    q = me ^ (4 * step)
    outer = (row == 0) | (row == 3)

    def psi_block(held, sector):
        if len(held) == 1:
            return held[0][0, sector]
        low, high = held
        size = low.shape[1]
        return jnp.where(
            sector < size, low[0, jnp.minimum(sector, size - 1)], high[0, jnp.maximum(sector - size, 0)]
        )

    def left_block(held, k):
        for part in held:
            if k < part.shape[0]:
                return part[k, 0]
            k -= part.shape[0]

    for k in range(terms):
        span = pl.ds(k * columns, columns)
        right = rights[0][k, 0]
        if choices > 1:
            right = jnp.where(outer, right, rights[1][k, 0])
        right_buf[:, span] = right
        for i in range(count):
            mid = jnp.dot(
                left_block(lefts[i], k), psi_block(psis[i], source[k, q]), preferred_element_type=jnp.float32
            )
            mid_buf[pl.ds(i * rows, rows), span] = mid.astype(jnp.bfloat16)
    second_product(mid_buf, right_buf, out)


def second_product(mid, right, out):
    total = lax.dot_general(mid[...], right[...], (((1,), (1,)), ((), ())), preferred_element_type=jnp.float32)
    out[...] = total.reshape(out.shape).astype(out.dtype)


def second_kernel(mid, right, out, right_buf):
    terms, _, _, columns = right.shape
    for k in range(terms):
        right_buf[:, pl.ds(k * columns, columns)] = right[k, 0]
    second_product(mid, right_buf, out)


def second(mid, right, dtype):
    terms, _, rows, columns = right.shape
    return pl.pallas_call(
        second_kernel,
        out_shape=jax.ShapeDtypeStruct((mid.shape[0] // rows, rows, columns), dtype),
        in_specs=[VMEM, VMEM],
        out_specs=VMEM,
        scratch_shapes=[pltpu.VMEM((rows, terms * columns), jnp.bfloat16)],
        compiler_params=pltpu.CompilerParams(vmem_limit_bytes=16 << 20),
        cost_estimate=pl.CostEstimate(flops=1, bytes_accessed=1, transcendentals=0),
    )(mid, right)


def slot(step, source_map, lefts, psis, rights, dtype, flops, keep_mid):
    terms, _, rows, columns = rights[0].shape
    count = len(psis)
    parts = tuple((len(left), len(psi)) for left, psi in zip(lefts, psis))
    held = [part for left in lefts for part in left] + [part for psi in psis for part in psi] + list(rights)
    out = jax.ShapeDtypeStruct((count, rows, columns), dtype)
    mid = jax.ShapeDtypeStruct((count * rows, terms * columns), jnp.bfloat16)
    scratch = [pltpu.VMEM((rows, terms * columns), jnp.bfloat16)]
    if not keep_mid:
        scratch = [pltpu.VMEM(mid.shape, mid.dtype)] + scratch
    return pl.pallas_call(
        functools.partial(slot_kernel, step, parts, len(rights)),
        out_shape=(out, mid) if keep_mid else out,
        in_specs=[SMEM] + [VMEM] * len(held),
        out_specs=(VMEM, VMEM) if keep_mid else VMEM,
        scratch_shapes=scratch,
        compiler_params=pltpu.CompilerParams(vmem_limit_bytes=24 << 20),
        cost_estimate=pl.CostEstimate(flops=flops, bytes_accessed=1, transcendentals=0),
    )(source_map, *held)


def split_kernel(whole, low, high):
    first = low.shape[0]
    low[...] = whole[:first]
    high[...] = whole[first:]


def split(array, first):
    sizes = (first, array.shape[0] - first)
    return pl.pallas_call(
        split_kernel,
        out_shape=tuple(jax.ShapeDtypeStruct((size,) + array.shape[1:], array.dtype) for size in sizes),
        in_specs=[VMEM],
        out_specs=(VMEM, VMEM),
        compiler_params=pltpu.CompilerParams(vmem_limit_bytes=8 << 20),
        cost_estimate=pl.CostEstimate(flops=1, bytes_accessed=1, transcendentals=0),
    )(array)


def place_kernel(first, choices, *refs):
    *pieces, out, sem = refs
    me = lax.axis_index("sec")
    row = me >> 2
    outer = (row == 0) | (row == 3)

    def copies(pieces):
        blocks = [piece.at[i] for piece in pieces for i in range(piece.shape[0])]
        return [
            pltpu.make_async_copy(block, out.at[me ^ j], sem.at[j - first]) for j, block in enumerate(blocks, first)
        ]

    if choices == 1:
        for copy in copies(pieces):
            copy.start()
    else:
        pieces = pieces[-2:]

        @pl.when(outer)
        def _():
            for copy in copies(pieces[:1]):
                copy.start()

        @pl.when(jnp.logical_not(outer))
        def _():
            for copy in copies(pieces[1:]):
                copy.start()

    for copy in copies(pieces[-1:] if choices == 2 else pieces):
        copy.wait()


def place(first, sectors, pieces, out=None):
    blocks = sum(piece.shape[0] for piece in pieces)
    held = [] if out is None else [out]
    return pl.pallas_call(
        functools.partial(place_kernel, first, 1 if out is None else 2),
        out_shape=jax.ShapeDtypeStruct((sectors,) + pieces[0].shape[1:], pieces[0].dtype),
        in_specs=[HBM] * len(held) + [VMEM] * len(pieces),
        out_specs=HBM,
        scratch_shapes=[pltpu.SemaphoreType.DMA((blocks,))],
        input_output_aliases={} if out is None else {0: 0},
        compiler_params=pltpu.CompilerParams(vmem_limit_bytes=16 << 20),
        cost_estimate=pl.CostEstimate(flops=1, bytes_accessed=1, transcendentals=0),
    )(*held, *pieces)


def exchange(array, bits, members):
    return lax.ppermute(array, "sec", [(s, s ^ bits) for s in members])


def on_device(ops, psi, left_env, right_env, source_map):
    dtype = jnp.bfloat16 if ops == 1 else jnp.float32
    every = range(16)
    inner = range(4, 12)
    outer = [s for s in every if s not in inner]
    low, high = split(left_env, 3 * left_env.shape[0] // 4)

    def products(step, lefts, psis, rights, flops=1, keep_mid=False):
        return slot(step, source_map, lefts, psis, rights, dtype, flops, keep_mid)

    near = exchange(right_env, 4, every)
    middle = exchange(right_env, 12, inner)
    x_psi = exchange(psi, 2, every)
    own = ([(left_env,), (exchange(left_env, 1, every),)], [(psi,), (exchange(psi, 1, every),)])
    own_0 = products(0, *own, (right_env,))

    near, middle, own_0 = lax.optimization_barrier((near, middle, own_0))
    far_in = exchange(near, 12, inner)
    far_out = exchange(middle, 4, inner)
    own_1 = products(1, *own, (near,))
    sent_1 = exchange(own_1, 4, every)

    x_psi, low = lax.optimization_barrier((x_psi, low))
    x_low = exchange(low, 2, every)
    across_psi = exchange(x_psi, 1, every)

    far_out, far_in = lax.optimization_barrier((far_out, far_in))
    third = exchange(far_in, 4, inner)
    own_2 = products(2, *own, (far_out, far_in))
    sent_2 = exchange(own_2, 8, every)

    own_2, sent_1, high = lax.optimization_barrier((own_2, sent_1, high))
    x_high = exchange(high, 2, every)
    x_low, x_high, sent_2 = lax.optimization_barrier((x_low, x_high, sent_2))
    across_low = exchange(x_low, 1, every)
    across_high = exchange(x_high, 1, every)
    other = ([(x_low, x_high), (across_low, across_high)], [(x_psi,), (across_psi,)])
    both = (own[0] + other[0], own[1] + other[1])
    other_2 = products(2, *other, (far_out, far_in))
    other_sent_2 = exchange(other_2, 8, every)
    last_middle, mid = products(3, *both, (middle,), keep_mid=True)
    sent_middle = exchange(last_middle, 12, inner)
    other_1 = products(1, *other, (near,))
    other_sent_1 = exchange(other_1, 4, every)

    third, other_1, other_2, last_middle = lax.optimization_barrier((third, other_1, other_2, last_middle))
    last_third = second(mid, third, dtype)
    sent_third = exchange(last_third, 12, outer)
    right_last, other_sent_2, other_sent_1 = lax.optimization_barrier((right_env, other_sent_2, other_sent_1))
    other_0 = products(0, *other, (right_last,), flops=10**10)

    out = place(0, 16, [own_0, other_0, sent_1, other_sent_1, sent_2, other_sent_2])
    out = place(12, 16, [sent_third, sent_middle], out)[:, None]
    if ops > 1:
        out = lax.psum_scatter(out, "op", scatter_dimension=2, tiled=True).astype(jnp.bfloat16)
    return out


def solution(mesh):
    placed = (
        P(("group", "sec"), None, None, None),
        P(("group", "op"), "sec", None, None),
        P(("group", "op"), "sec", None, None),
        P(("group", "op"), None),
    )
    return jax.shard_map(
        functools.partial(on_device, mesh.shape["op"]),
        mesh=mesh,
        in_specs=placed,
        out_specs=P("group", "sec", "op", None),
        check_vma=False,
    )
```

```python
import functools

import jax
import jax.numpy as jnp
from jax import lax
from jax.experimental import pallas as pl
from jax.experimental.pallas import tpu as pltpu
from jax.sharding import PartitionSpec as P

HBM = pl.BlockSpec(memory_space=pltpu.HBM)
SMEM = pl.BlockSpec(memory_space=pltpu.SMEM)
VMEM = pl.BlockSpec(memory_space=pltpu.VMEM)


def slot_kernel(step, parts, choices, source, *refs):
    count = len(parts)
    lefts, psis = [], []
    for number, _ in parts:
        lefts.append(refs[:number])
        refs = refs[number:]
    for _, number in parts:
        psis.append(refs[:number])
        refs = refs[number:]
    rights = refs[:choices]
    out, mid_buf, right_buf = refs[choices:]
    terms, _, rows, columns = rights[0].shape
    me = lax.axis_index("sec")
    row = me >> 2
    q = me ^ (4 * step)
    outer = (row == 0) | (row == 3)

    def psi_block(held, sector):
        if len(held) == 1:
            return held[0][0, sector]
        low, high = held
        size = low.shape[1]
        return jnp.where(
            sector < size, low[0, jnp.minimum(sector, size - 1)], high[0, jnp.maximum(sector - size, 0)]
        )

    def left_block(held, k):
        for part in held:
            if k < part.shape[0]:
                return part[k, 0]
            k -= part.shape[0]

    for k in range(terms):
        span = pl.ds(k * columns, columns)
        right = rights[0][k, 0]
        if choices > 1:
            right = jnp.where(outer, right, rights[1][k, 0])
        right_buf[:, span] = right
        for i in range(count):
            mid = jnp.dot(
                left_block(lefts[i], k), psi_block(psis[i], source[k, q]), preferred_element_type=jnp.float32
            )
            mid_buf[pl.ds(i * rows, rows), span] = mid.astype(jnp.bfloat16)
    second_product(mid_buf, right_buf, out)


def second_product(mid, right, out):
    total = lax.dot_general(mid[...], right[...], (((1,), (1,)), ((), ())), preferred_element_type=jnp.float32)
    out[...] = total.reshape(out.shape).astype(out.dtype)


def second_kernel(mid, right, out, right_buf):
    terms, _, _, columns = right.shape
    for k in range(terms):
        right_buf[:, pl.ds(k * columns, columns)] = right[k, 0]
    second_product(mid, right_buf, out)


def second(mid, right, dtype):
    terms, _, rows, columns = right.shape
    return pl.pallas_call(
        second_kernel,
        out_shape=jax.ShapeDtypeStruct((mid.shape[0] // rows, rows, columns), dtype),
        in_specs=[VMEM, VMEM],
        out_specs=VMEM,
        scratch_shapes=[pltpu.VMEM((rows, terms * columns), jnp.bfloat16)],
        compiler_params=pltpu.CompilerParams(vmem_limit_bytes=16 << 20),
        cost_estimate=pl.CostEstimate(flops=1, bytes_accessed=1, transcendentals=0),
    )(mid, right)


def slot(step, source_map, lefts, psis, rights, dtype, flops, keep_mid):
    terms, _, rows, columns = rights[0].shape
    count = len(psis)
    parts = tuple((len(left), len(psi)) for left, psi in zip(lefts, psis))
    held = [part for left in lefts for part in left] + [part for psi in psis for part in psi] + list(rights)
    out = jax.ShapeDtypeStruct((count, rows, columns), dtype)
    mid = jax.ShapeDtypeStruct((count * rows, terms * columns), jnp.bfloat16)
    scratch = [pltpu.VMEM((rows, terms * columns), jnp.bfloat16)]
    if not keep_mid:
        scratch = [pltpu.VMEM(mid.shape, mid.dtype)] + scratch
    return pl.pallas_call(
        functools.partial(slot_kernel, step, parts, len(rights)),
        out_shape=(out, mid) if keep_mid else out,
        in_specs=[SMEM] + [VMEM] * len(held),
        out_specs=(VMEM, VMEM) if keep_mid else VMEM,
        scratch_shapes=scratch,
        compiler_params=pltpu.CompilerParams(vmem_limit_bytes=24 << 20),
        cost_estimate=pl.CostEstimate(flops=flops, bytes_accessed=1, transcendentals=0),
    )(source_map, *held)


def split_kernel(whole, low, high):
    first = low.shape[0]
    low[...] = whole[:first]
    high[...] = whole[first:]


def split(array, first):
    sizes = (first, array.shape[0] - first)
    return pl.pallas_call(
        split_kernel,
        out_shape=tuple(jax.ShapeDtypeStruct((size,) + array.shape[1:], array.dtype) for size in sizes),
        in_specs=[VMEM],
        out_specs=(VMEM, VMEM),
        compiler_params=pltpu.CompilerParams(vmem_limit_bytes=8 << 20),
        cost_estimate=pl.CostEstimate(flops=1, bytes_accessed=1, transcendentals=0),
    )(array)


def place_kernel(first, choices, *refs):
    *pieces, out, sem = refs
    me = lax.axis_index("sec")
    row = me >> 2
    outer = (row == 0) | (row == 3)

    def copies(pieces):
        blocks = [piece.at[i] for piece in pieces for i in range(piece.shape[0])]
        return [
            pltpu.make_async_copy(block, out.at[me ^ j], sem.at[j - first]) for j, block in enumerate(blocks, first)
        ]

    if choices == 1:
        for copy in copies(pieces):
            copy.start()
    else:
        pieces = pieces[-2:]

        @pl.when(outer)
        def _():
            for copy in copies(pieces[:1]):
                copy.start()

        @pl.when(jnp.logical_not(outer))
        def _():
            for copy in copies(pieces[1:]):
                copy.start()

    for copy in copies(pieces[-1:] if choices == 2 else pieces):
        copy.wait()


def place(first, sectors, pieces, out=None):
    blocks = sum(piece.shape[0] for piece in pieces)
    held = [] if out is None else [out]
    return pl.pallas_call(
        functools.partial(place_kernel, first, 1 if out is None else 2),
        out_shape=jax.ShapeDtypeStruct((sectors,) + pieces[0].shape[1:], pieces[0].dtype),
        in_specs=[HBM] * len(held) + [VMEM] * len(pieces),
        out_specs=HBM,
        scratch_shapes=[pltpu.SemaphoreType.DMA((blocks,))],
        input_output_aliases={} if out is None else {0: 0},
        compiler_params=pltpu.CompilerParams(vmem_limit_bytes=16 << 20),
        cost_estimate=pl.CostEstimate(flops=1, bytes_accessed=1, transcendentals=0),
    )(*held, *pieces)


def exchange(array, bits, members):
    return lax.ppermute(array, "sec", [(s, s ^ bits) for s in members])


def on_device(ops, psi, left_env, right_env, source_map):
    dtype = jnp.bfloat16 if ops == 1 else jnp.float32
    every = range(16)
    inner = range(4, 12)
    outer = [s for s in every if s not in inner]
    low, high = split(left_env, 3 * left_env.shape[0] // 4)

    def products(step, lefts, psis, rights, flops=1, keep_mid=False):
        return slot(step, source_map, lefts, psis, rights, dtype, flops, keep_mid)

    near = exchange(right_env, 4, every)
    middle = exchange(right_env, 12, inner)
    x_psi = exchange(psi, 2, every)
    own = ([(left_env,), (exchange(left_env, 1, every),)], [(psi,), (exchange(psi, 1, every),)])
    own_0 = products(0, *own, (right_env,))

    middle, near, own_0 = lax.optimization_barrier((middle, near, own_0))
    far_in = exchange(near, 12, inner)
    far_out = exchange(middle, 4, inner)
    own_1 = products(1, *own, (near,))
    sent_1 = exchange(own_1, 4, every)

    x_psi, low = lax.optimization_barrier((x_psi, low))
    x_low = exchange(low, 2, every)
    across_psi = exchange(x_psi, 1, every)

    far_out, far_in = lax.optimization_barrier((far_out, far_in))
    third = exchange(far_in, 4, inner)
    own_2 = products(2, *own, (far_out, far_in))
    sent_2 = exchange(own_2, 8, every)

    own_2, sent_1, high = lax.optimization_barrier((own_2, sent_1, high))
    x_high = exchange(high, 2, every)
    x_low, x_high, sent_2 = lax.optimization_barrier((x_low, x_high, sent_2))
    across_low = exchange(x_low, 1, every)
    across_high = exchange(x_high, 1, every)
    other = ([(x_low, x_high), (across_low, across_high)], [(x_psi,), (across_psi,)])
    both = (own[0] + other[0], own[1] + other[1])
    other_2 = products(2, *other, (far_out, far_in))
    other_sent_2 = exchange(other_2, 8, every)
    last_middle, mid = products(3, *both, (middle,), keep_mid=True)
    sent_middle = exchange(last_middle, 12, inner)
    other_1 = products(1, *other, (near,))
    other_sent_1 = exchange(other_1, 4, every)

    third, other_1, other_2, last_middle = lax.optimization_barrier((third, other_1, other_2, last_middle))
    last_third = second(mid, third, dtype)
    sent_third = exchange(last_third, 12, outer)
    right_last, other_sent_2, other_sent_1 = lax.optimization_barrier((right_env, other_sent_2, other_sent_1))
    other_0 = products(0, *other, (right_last,), flops=10**10)

    out = place(0, 16, [own_0, other_0, sent_1, other_sent_1, sent_2, other_sent_2])
    out = place(12, 16, [sent_third, sent_middle], out)[:, None]
    if ops > 1:
        out = lax.psum_scatter(out, "op", scatter_dimension=2, tiled=True).astype(jnp.bfloat16)
    return out


def solution(mesh):
    placed = (
        P(("group", "sec"), None, None, None),
        P(("group", "op"), "sec", None, None),
        P(("group", "op"), "sec", None, None),
        P(("group", "op"), None),
    )
    return jax.shard_map(
        functools.partial(on_device, mesh.shape["op"]),
        mesh=mesh,
        in_specs=placed,
        out_specs=P("group", "sec", "op", None),
        check_vma=False,
    )
```

```python
import functools

import jax
import jax.numpy as jnp
from jax import lax
from jax.experimental import pallas as pl
from jax.experimental.pallas import tpu as pltpu
from jax.sharding import PartitionSpec as P

HBM = pl.BlockSpec(memory_space=pltpu.HBM)
SMEM = pl.BlockSpec(memory_space=pltpu.SMEM)
VMEM = pl.BlockSpec(memory_space=pltpu.VMEM)


def slot_kernel(step, parts, choices, source, *refs):
    count = len(parts)
    lefts, psis = [], []
    for number, _ in parts:
        lefts.append(refs[:number])
        refs = refs[number:]
    for _, number in parts:
        psis.append(refs[:number])
        refs = refs[number:]
    rights = refs[:choices]
    out, mid_buf, right_buf = refs[choices:]
    terms, _, rows, columns = rights[0].shape
    me = lax.axis_index("sec")
    row = me >> 2
    q = me ^ (4 * step)
    outer = (row == 0) | (row == 3)

    def psi_block(held, sector):
        if len(held) == 1:
            return held[0][0, sector]
        low, high = held
        size = low.shape[1]
        return jnp.where(
            sector < size, low[0, jnp.minimum(sector, size - 1)], high[0, jnp.maximum(sector - size, 0)]
        )

    def left_block(held, k):
        for part in held:
            if k < part.shape[0]:
                return part[k, 0]
            k -= part.shape[0]

    for k in range(terms):
        span = pl.ds(k * columns, columns)
        right = rights[0][k, 0]
        if choices > 1:
            right = jnp.where(outer, right, rights[1][k, 0])
        right_buf[:, span] = right
        for i in range(count):
            mid = jnp.dot(
                left_block(lefts[i], k), psi_block(psis[i], source[k, q]), preferred_element_type=jnp.float32
            )
            mid_buf[pl.ds(i * rows, rows), span] = mid.astype(jnp.bfloat16)
    second_product(mid_buf, right_buf, out)


def second_product(mid, right, out):
    total = lax.dot_general(mid[...], right[...], (((1,), (1,)), ((), ())), preferred_element_type=jnp.float32)
    out[...] = total.reshape(out.shape).astype(out.dtype)


def second_kernel(*refs):
    *mids, right, out, right_buf = refs
    terms, _, _, columns = right.shape
    for k in range(terms):
        right_buf[:, pl.ds(k * columns, columns)] = right[k, 0]
    size = out.shape[0] // len(mids)
    for i, mid in enumerate(mids):
        second_product(mid, right_buf, out.at[pl.ds(i * size, size)])


def second(mids, right, dtype, flops):
    terms, _, rows, columns = right.shape
    return pl.pallas_call(
        second_kernel,
        out_shape=jax.ShapeDtypeStruct((sum(mid.shape[0] for mid in mids) // rows, rows, columns), dtype),
        in_specs=[VMEM] * (len(mids) + 1),
        out_specs=VMEM,
        scratch_shapes=[pltpu.VMEM((rows, terms * columns), jnp.bfloat16)],
        compiler_params=pltpu.CompilerParams(vmem_limit_bytes=16 << 20),
        cost_estimate=pl.CostEstimate(flops=flops, bytes_accessed=1, transcendentals=0),
    )(*mids, right)


def slot(step, source_map, lefts, psis, rights, dtype, flops, keep_mid):
    terms, _, rows, columns = rights[0].shape
    count = len(psis)
    parts = tuple((len(left), len(psi)) for left, psi in zip(lefts, psis))
    held = [part for left in lefts for part in left] + [part for psi in psis for part in psi] + list(rights)
    out = jax.ShapeDtypeStruct((count, rows, columns), dtype)
    mid = jax.ShapeDtypeStruct((count * rows, terms * columns), jnp.bfloat16)
    scratch = [pltpu.VMEM((rows, terms * columns), jnp.bfloat16)]
    if not keep_mid:
        scratch = [pltpu.VMEM(mid.shape, mid.dtype)] + scratch
    return pl.pallas_call(
        functools.partial(slot_kernel, step, parts, len(rights)),
        out_shape=(out, mid) if keep_mid else out,
        in_specs=[SMEM] + [VMEM] * len(held),
        out_specs=(VMEM, VMEM) if keep_mid else VMEM,
        scratch_shapes=scratch,
        compiler_params=pltpu.CompilerParams(vmem_limit_bytes=24 << 20),
        cost_estimate=pl.CostEstimate(flops=flops, bytes_accessed=1, transcendentals=0),
    )(source_map, *held)


def split_kernel(axis, whole, low, high):
    first = low.shape[axis]
    before = (slice(None),) * axis
    low[...] = whole[(*before, slice(0, first))]
    high[...] = whole[(*before, slice(first, None))]


def split(array, axis, first):
    def part(size):
        shape = array.shape[:axis] + (size,) + array.shape[axis + 1 :]
        return jax.ShapeDtypeStruct(shape, array.dtype)

    return pl.pallas_call(
        functools.partial(split_kernel, axis),
        out_shape=(part(first), part(array.shape[axis] - first)),
        in_specs=[VMEM],
        out_specs=(VMEM, VMEM),
        compiler_params=pltpu.CompilerParams(vmem_limit_bytes=12 << 20),
        cost_estimate=pl.CostEstimate(flops=1, bytes_accessed=1, transcendentals=0),
    )(array)


def place_kernel(first, choices, *refs):
    *pieces, out, sem = refs
    me = lax.axis_index("sec")
    row = me >> 2
    outer = (row == 0) | (row == 3)

    def copies(pieces):
        blocks = [piece.at[i] for piece in pieces for i in range(piece.shape[0])]
        return [
            pltpu.make_async_copy(block, out.at[me ^ j], sem.at[j - first]) for j, block in enumerate(blocks, first)
        ]

    if choices == 1:
        for copy in copies(pieces):
            copy.start()
    else:
        pieces = pieces[1:]

        @pl.when(outer)
        def _():
            for copy in copies(pieces[:1]):
                copy.start()

        @pl.when(jnp.logical_not(outer))
        def _():
            for copy in copies(pieces[1:]):
                copy.start()

        pieces = pieces[:1]

    for copy in copies(pieces):
        copy.wait()


def place(first, sectors, pieces, out=None):
    blocks = sum(piece.shape[0] for piece in (pieces if out is None else pieces[:1]))
    held = [] if out is None else [out]
    return pl.pallas_call(
        functools.partial(place_kernel, first, 1 if out is None else 2),
        out_shape=jax.ShapeDtypeStruct((sectors,) + pieces[0].shape[1:], pieces[0].dtype),
        in_specs=[HBM] * len(held) + [VMEM] * len(pieces),
        out_specs=HBM,
        scratch_shapes=[pltpu.SemaphoreType.DMA((blocks,))],
        input_output_aliases={} if out is None else {0: 0},
        compiler_params=pltpu.CompilerParams(vmem_limit_bytes=16 << 20),
        cost_estimate=pl.CostEstimate(flops=1, bytes_accessed=1, transcendentals=0),
    )(*held, *pieces)


def exchange(array, bits, members):
    return lax.ppermute(array, "sec", [(s, s ^ bits) for s in members])


def on_device(ops, psi, left_env, right_env, source_map):
    dtype = jnp.bfloat16 if ops == 1 else jnp.float32
    every = range(16)
    inner = range(4, 12)
    outer = [s for s in every if s not in inner]
    low, high = split(left_env, 0, 5 * left_env.shape[0] // 8)

    def products(step, lefts, psis, rights, flops=1, keep_mid=False):
        return slot(step, source_map, lefts, psis, rights, dtype, flops, keep_mid)

    near = exchange(right_env, 4, every)
    middle = exchange(right_env, 12, inner)
    x_psi = exchange(psi, 2, every)
    own = ([(left_env,), (exchange(left_env, 1, every),)], [(psi,), (exchange(psi, 1, every),)])
    own_0 = products(0, *own, (right_env,))

    near, middle, own_0 = lax.optimization_barrier((near, middle, own_0))
    far_in = exchange(near, 12, inner)
    far_out = exchange(middle, 4, inner)

    x_psi, low = lax.optimization_barrier((x_psi, low))
    x_low = exchange(low, 2, every)
    across_psi = [exchange(part, 1, every) for part in split(x_psi, 1, 5 * x_psi.shape[1] // 8)]

    far_out, far_in = lax.optimization_barrier((far_out, far_in))
    third = exchange(far_in, 4, inner)
    own_middle, own_mid = products(3, *own, (middle,), keep_mid=True)
    sent_own_middle = exchange(own_middle, 12, inner)
    own_2 = products(2, *own, (far_out, far_in))
    sent_2 = exchange(own_2, 8, every)

    own_2, sent_own_middle, high = lax.optimization_barrier((own_2, sent_own_middle, high))
    x_high = exchange(high, 2, every)
    across_low = exchange(x_low, 1, every)
    x_high, sent_2 = lax.optimization_barrier((x_high, sent_2))
    across_high = exchange(x_high, 1, every)
    other = ([(x_low, x_high), (across_low, across_high)], [(x_psi,), across_psi])
    other_2 = products(2, *other, (far_out, far_in))
    other_sent_2 = exchange(other_2, 8, every)
    other_middle, other_mid = products(3, *other, (middle,), keep_mid=True)
    sent_other_middle = exchange(other_middle, 12, inner)
    both_1 = products(1, own[0] + other[0], own[1] + other[1], (near,))
    sent_1 = exchange(both_1, 4, every)

    third, both_1, other_2, other_middle = lax.optimization_barrier((third, both_1, other_2, other_middle))
    last_third = second((own_mid, other_mid), third, dtype, 10**10)
    sent_third = exchange(last_third, 12, outer)
    right_last, other_sent_2, sent_1 = lax.optimization_barrier((right_env, other_sent_2, sent_1))
    other_0 = products(0, *other, (right_last,), flops=10**10)

    out = place(0, 16, [own_0, other_0, sent_1, sent_2, other_sent_2])
    out = place(12, 16, [sent_third, sent_own_middle, sent_other_middle], out)[:, None]
    if ops > 1:
        out = lax.psum_scatter(out, "op", scatter_dimension=2, tiled=True).astype(jnp.bfloat16)
    return out


def solution(mesh):
    placed = (
        P(("group", "sec"), None, None, None),
        P(("group", "op"), "sec", None, None),
        P(("group", "op"), "sec", None, None),
        P(("group", "op"), None),
    )
    return jax.shard_map(
        functools.partial(on_device, mesh.shape["op"]),
        mesh=mesh,
        in_specs=placed,
        out_specs=P("group", "sec", "op", None),
        check_vma=False,
    )
```

```python
import functools

import jax
import jax.numpy as jnp
from jax import lax
from jax.experimental import pallas as pl
from jax.experimental.pallas import tpu as pltpu
from jax.sharding import PartitionSpec as P

HBM = pl.BlockSpec(memory_space=pltpu.HBM)
SMEM = pl.BlockSpec(memory_space=pltpu.SMEM)
VMEM = pl.BlockSpec(memory_space=pltpu.VMEM)


def slot_kernel(step, parts, choices, source, *refs):
    count = len(parts)
    lefts, psis = [], []
    for number, _ in parts:
        lefts.append(refs[:number])
        refs = refs[number:]
    for _, number in parts:
        psis.append(refs[:number])
        refs = refs[number:]
    rights = refs[:choices]
    out, mid_buf, right_buf = refs[choices:]
    terms, _, rows, columns = rights[0].shape
    me = lax.axis_index("sec")
    row = me >> 2
    q = me ^ (4 * step)
    outer = (row == 0) | (row == 3)

    def psi_block(held, sector):
        if len(held) == 1:
            return held[0][0, sector]
        low, high = held
        size = low.shape[1]
        return jnp.where(
            sector < size, low[0, jnp.minimum(sector, size - 1)], high[0, jnp.maximum(sector - size, 0)]
        )

    def left_block(held, k):
        for part in held:
            if k < part.shape[0]:
                return part[k, 0]
            k -= part.shape[0]

    for k in range(terms):
        span = pl.ds(k * columns, columns)
        right = rights[0][k, 0]
        if choices > 1:
            right = jnp.where(outer, right, rights[1][k, 0])
        right_buf[:, span] = right
        for i in range(count):
            mid = jnp.dot(
                left_block(lefts[i], k), psi_block(psis[i], source[k, q]), preferred_element_type=jnp.float32
            )
            mid_buf[pl.ds(i * rows, rows), span] = mid.astype(jnp.bfloat16)
    second_product(mid_buf, right_buf, out)


def second_product(mid, right, out):
    total = lax.dot_general(mid[...], right[...], (((1,), (1,)), ((), ())), preferred_element_type=jnp.float32)
    out[...] = total.reshape(out.shape).astype(out.dtype)


def second_kernel(*refs):
    *mids, right, out, right_buf = refs
    terms, _, _, columns = right.shape
    for k in range(terms):
        right_buf[:, pl.ds(k * columns, columns)] = right[k, 0]
    size = out.shape[0] // len(mids)
    for i, mid in enumerate(mids):
        second_product(mid, right_buf, out.at[pl.ds(i * size, size)])


def second(mids, right, dtype, flops):
    terms, _, rows, columns = right.shape
    return pl.pallas_call(
        second_kernel,
        out_shape=jax.ShapeDtypeStruct((sum(mid.shape[0] for mid in mids) // rows, rows, columns), dtype),
        in_specs=[VMEM] * (len(mids) + 1),
        out_specs=VMEM,
        scratch_shapes=[pltpu.VMEM((rows, terms * columns), jnp.bfloat16)],
        compiler_params=pltpu.CompilerParams(vmem_limit_bytes=16 << 20),
        cost_estimate=pl.CostEstimate(flops=flops, bytes_accessed=1, transcendentals=0),
    )(*mids, right)


def slot(step, source_map, lefts, psis, rights, dtype, flops, keep_mid):
    terms, _, rows, columns = rights[0].shape
    count = len(psis)
    parts = tuple((len(left), len(psi)) for left, psi in zip(lefts, psis))
    held = [part for left in lefts for part in left] + [part for psi in psis for part in psi] + list(rights)
    out = jax.ShapeDtypeStruct((count, rows, columns), dtype)
    mid = jax.ShapeDtypeStruct((count * rows, terms * columns), jnp.bfloat16)
    scratch = [pltpu.VMEM((rows, terms * columns), jnp.bfloat16)]
    if not keep_mid:
        scratch = [pltpu.VMEM(mid.shape, mid.dtype)] + scratch
    return pl.pallas_call(
        functools.partial(slot_kernel, step, parts, len(rights)),
        out_shape=(out, mid) if keep_mid else out,
        in_specs=[SMEM] + [VMEM] * len(held),
        out_specs=(VMEM, VMEM) if keep_mid else VMEM,
        scratch_shapes=scratch,
        compiler_params=pltpu.CompilerParams(vmem_limit_bytes=24 << 20),
        cost_estimate=pl.CostEstimate(flops=flops, bytes_accessed=1, transcendentals=0),
    )(source_map, *held)


def split_kernel(axis, whole, low, high):
    first = low.shape[axis]
    before = (slice(None),) * axis
    low[...] = whole[(*before, slice(0, first))]
    high[...] = whole[(*before, slice(first, None))]


def split(array, axis, first):
    def part(size):
        shape = array.shape[:axis] + (size,) + array.shape[axis + 1 :]
        return jax.ShapeDtypeStruct(shape, array.dtype)

    return pl.pallas_call(
        functools.partial(split_kernel, axis),
        out_shape=(part(first), part(array.shape[axis] - first)),
        in_specs=[VMEM],
        out_specs=(VMEM, VMEM),
        compiler_params=pltpu.CompilerParams(vmem_limit_bytes=12 << 20),
        cost_estimate=pl.CostEstimate(flops=1, bytes_accessed=1, transcendentals=0),
    )(array)


def place_kernel(starts, chosen, *refs):
    *pieces, out, sem = refs
    pieces = pieces[-len(starts) :]
    me = lax.axis_index("sec")
    row = me >> 2
    outer = (row == 0) | (row == 3)

    def copies(chosen_pieces):
        return [
            pltpu.make_async_copy(piece.at[i], out.at[me ^ (start + i)], sem.at[start + i])
            for start, piece in chosen_pieces
            for i in range(piece.shape[0])
        ]

    held = list(zip(starts, pieces))
    if chosen:

        @pl.when(outer)
        def _():
            for copy in copies(held[:1]):
                copy.start()

        @pl.when(jnp.logical_not(outer))
        def _():
            for copy in copies(held[1:]):
                copy.start()

        held = held[:1]
    else:
        for copy in copies(held):
            copy.start()
    for copy in copies(held):
        copy.wait()


def place(sectors, held, out=None, flops=1):
    starts, pieces = zip(*held)
    before = [] if out is None else [out]
    return pl.pallas_call(
        functools.partial(place_kernel, starts, out is not None),
        out_shape=jax.ShapeDtypeStruct((sectors,) + pieces[0].shape[1:], pieces[0].dtype),
        in_specs=[HBM] * len(before) + [VMEM] * len(pieces),
        out_specs=HBM,
        scratch_shapes=[pltpu.SemaphoreType.DMA((sectors,))],
        input_output_aliases={} if out is None else {0: 0},
        compiler_params=pltpu.CompilerParams(vmem_limit_bytes=16 << 20),
        cost_estimate=pl.CostEstimate(flops=flops, bytes_accessed=1, transcendentals=0),
    )(*before, *pieces)


def exchange(array, bits, members):
    return lax.ppermute(array, "sec", [(s, s ^ bits) for s in members])


def on_device(ops, psi, left_env, right_env, source_map):
    dtype = jnp.bfloat16 if ops == 1 else jnp.float32
    every = range(16)
    inner = range(4, 12)
    outer = [s for s in every if s not in inner]

    def products(step, lefts, psis, rights, flops=1, keep_mid=False):
        return slot(step, source_map, lefts, psis, rights, dtype, flops, keep_mid)

    near = exchange(right_env, 4, every)
    middle = exchange(right_env, 12, inner)
    x_psi = exchange(psi, 2, every)
    own = ([(left_env,), (exchange(left_env, 1, every),)], [(psi,), (exchange(psi, 1, every),)])
    own_0 = products(0, *own, (right_env,))

    near, middle, own_0 = lax.optimization_barrier((near, middle, own_0))
    far_in = exchange(near, 12, inner)
    far_out = exchange(middle, 4, inner)

    x_psi, left_next = lax.optimization_barrier((x_psi, left_env))
    x_left = exchange(left_next, 2, every)
    across_psi = [exchange(part, 1, every) for part in split(x_psi, 1, 6 * x_psi.shape[1] // 8)]
    own_1 = products(1, *own, (near,))
    sent_1 = exchange(own_1, 4, every)

    far_out, far_in = lax.optimization_barrier((far_out, far_in))
    third = exchange(far_in, 4, inner)
    far_out, sent_1 = lax.optimization_barrier((far_out, sent_1))
    own_2 = products(2, *own, (far_out, far_in))
    sent_2 = exchange(own_2, 8, every)
    own_middle, own_mid = products(3, *own, (middle,), keep_mid=True)
    sent_own_middle = exchange(own_middle, 12, inner)

    x_left, sent_2, sent_own_middle = lax.optimization_barrier((x_left, sent_2, sent_own_middle))
    across_left = [exchange(part, 1, every) for part in split(x_left, 0, 5 * x_left.shape[0] // 8)]
    other = ([(x_left,), across_left], [(x_psi,), across_psi])
    other_2 = products(2, *other, (far_out, far_in))
    other_sent_2 = exchange(other_2, 8, every)
    other_middle, other_mid = products(3, *other, (middle,), keep_mid=True)
    sent_other_middle = exchange(other_middle, 12, inner)
    other_1 = products(1, *other, (near,))
    other_sent_1 = exchange(other_1, 4, every)

    third, other_1, other_middle, other_2 = lax.optimization_barrier((third, other_1, other_middle, other_2))
    last_third = second((own_mid, other_mid), third, dtype, 10**10)
    sent_third = exchange(last_third, 12, outer)
    right_last, last_third = lax.optimization_barrier((right_env, last_third))
    other_0 = products(0, *other, (right_last,))

    other_sent_2, other_sent_1 = lax.optimization_barrier((other_sent_2, other_sent_1))
    held = [(0, own_0), (2, other_0), (8, sent_2), (10, other_sent_2), (4, sent_1), (6, other_sent_1)]
    out = place(16, held, flops=10**10)
    out = place(16, [(12, sent_third), (12, sent_own_middle), (14, sent_other_middle)], out)[:, None]
    if ops > 1:
        out = lax.psum_scatter(out, "op", scatter_dimension=2, tiled=True).astype(jnp.bfloat16)
    return out


def solution(mesh):
    placed = (
        P(("group", "sec"), None, None, None),
        P(("group", "op"), "sec", None, None),
        P(("group", "op"), "sec", None, None),
        P(("group", "op"), None),
    )
    return jax.shard_map(
        functools.partial(on_device, mesh.shape["op"]),
        mesh=mesh,
        in_specs=placed,
        out_specs=P("group", "sec", "op", None),
        check_vma=False,
    )
```

```python
import functools

import jax
import jax.numpy as jnp
from jax import lax
from jax.experimental import pallas as pl
from jax.experimental.pallas import tpu as pltpu
from jax.sharding import PartitionSpec as P

HBM = pl.BlockSpec(memory_space=pltpu.HBM)
SMEM = pl.BlockSpec(memory_space=pltpu.SMEM)
VMEM = pl.BlockSpec(memory_space=pltpu.VMEM)


def slot_kernel(step, parts, choices, source, *refs):
    count = len(parts)
    lefts, psis = [], []
    for number, _ in parts:
        lefts.append(refs[:number])
        refs = refs[number:]
    for _, number in parts:
        psis.append(refs[:number])
        refs = refs[number:]
    rights = refs[:choices]
    out, mid_buf, right_buf = refs[choices:]
    terms, _, rows, columns = rights[0].shape
    me = lax.axis_index("sec")
    row = me >> 2
    q = me ^ (4 * step)
    outer = (row == 0) | (row == 3)

    def psi_block(held, sector):
        if len(held) == 1:
            return held[0][0, sector]
        low, high = held
        size = low.shape[1]
        return jnp.where(
            sector < size, low[0, jnp.minimum(sector, size - 1)], high[0, jnp.maximum(sector - size, 0)]
        )

    def left_block(held, k):
        for part in held:
            if k < part.shape[0]:
                return part[k, 0]
            k -= part.shape[0]

    for k in range(terms):
        span = pl.ds(k * columns, columns)
        right = rights[0][k, 0]
        if choices > 1:
            right = jnp.where(outer, right, rights[1][k, 0])
        right_buf[:, span] = right
        for i in range(count):
            mid = jnp.dot(
                left_block(lefts[i], k), psi_block(psis[i], source[k, q]), preferred_element_type=jnp.float32
            )
            mid_buf[pl.ds(i * rows, rows), span] = mid.astype(jnp.bfloat16)
    second_product(mid_buf, right_buf, out)


def second_product(mid, right, out):
    total = lax.dot_general(mid[...], right[...], (((1,), (1,)), ((), ())), preferred_element_type=jnp.float32)
    out[...] = total.reshape(out.shape).astype(out.dtype)


def second_kernel(*refs):
    *mids, right, out, right_buf = refs
    terms, _, _, columns = right.shape
    for k in range(terms):
        right_buf[:, pl.ds(k * columns, columns)] = right[k, 0]
    size = out.shape[0] // len(mids)
    for i, mid in enumerate(mids):
        second_product(mid, right_buf, out.at[pl.ds(i * size, size)])


def second(mids, right, dtype, flops):
    terms, _, rows, columns = right.shape
    return pl.pallas_call(
        second_kernel,
        out_shape=jax.ShapeDtypeStruct((sum(mid.shape[0] for mid in mids) // rows, rows, columns), dtype),
        in_specs=[VMEM] * (len(mids) + 1),
        out_specs=VMEM,
        scratch_shapes=[pltpu.VMEM((rows, terms * columns), jnp.bfloat16)],
        compiler_params=pltpu.CompilerParams(vmem_limit_bytes=16 << 20),
        cost_estimate=pl.CostEstimate(flops=flops, bytes_accessed=1, transcendentals=0),
    )(*mids, right)


def slot(step, source_map, lefts, psis, rights, dtype, flops, keep_mid):
    terms, _, rows, columns = rights[0].shape
    count = len(psis)
    parts = tuple((len(left), len(psi)) for left, psi in zip(lefts, psis))
    held = [part for left in lefts for part in left] + [part for psi in psis for part in psi] + list(rights)
    out = jax.ShapeDtypeStruct((count, rows, columns), dtype)
    mid = jax.ShapeDtypeStruct((count * rows, terms * columns), jnp.bfloat16)
    scratch = [pltpu.VMEM((rows, terms * columns), jnp.bfloat16)]
    if not keep_mid:
        scratch = [pltpu.VMEM(mid.shape, mid.dtype)] + scratch
    return pl.pallas_call(
        functools.partial(slot_kernel, step, parts, len(rights)),
        out_shape=(out, mid) if keep_mid else out,
        in_specs=[SMEM] + [VMEM] * len(held),
        out_specs=(VMEM, VMEM) if keep_mid else VMEM,
        scratch_shapes=scratch,
        compiler_params=pltpu.CompilerParams(vmem_limit_bytes=24 << 20),
        cost_estimate=pl.CostEstimate(flops=flops, bytes_accessed=1, transcendentals=0),
    )(source_map, *held)


def split_kernel(axis, whole, low, high):
    first = low.shape[axis]
    before = (slice(None),) * axis
    low[...] = whole[(*before, slice(0, first))]
    high[...] = whole[(*before, slice(first, None))]


def split(array, axis, first):
    def part(size):
        shape = array.shape[:axis] + (size,) + array.shape[axis + 1 :]
        return jax.ShapeDtypeStruct(shape, array.dtype)

    return pl.pallas_call(
        functools.partial(split_kernel, axis),
        out_shape=(part(first), part(array.shape[axis] - first)),
        in_specs=[VMEM],
        out_specs=(VMEM, VMEM),
        compiler_params=pltpu.CompilerParams(vmem_limit_bytes=12 << 20),
        cost_estimate=pl.CostEstimate(flops=1, bytes_accessed=1, transcendentals=0),
    )(array)


def place_kernel(starts, chosen, *refs):
    *pieces, out, sem = refs
    pieces = pieces[-len(starts) :]
    me = lax.axis_index("sec")
    row = me >> 2
    outer = (row == 0) | (row == 3)

    def copies(chosen_pieces):
        return [
            pltpu.make_async_copy(piece.at[i], out.at[me ^ (start + i)], sem.at[start + i])
            for start, piece in chosen_pieces
            for i in range(piece.shape[0])
        ]

    held = list(zip(starts, pieces))
    if chosen:

        @pl.when(outer)
        def _():
            for copy in copies(held[:1]):
                copy.start()

        @pl.when(jnp.logical_not(outer))
        def _():
            for copy in copies(held[1:]):
                copy.start()

        held = held[:1]
    else:
        for copy in copies(held):
            copy.start()
    for copy in copies(held):
        copy.wait()


def place(sectors, held, out=None, flops=1):
    starts, pieces = zip(*held)
    before = [] if out is None else [out]
    return pl.pallas_call(
        functools.partial(place_kernel, starts, out is not None),
        out_shape=jax.ShapeDtypeStruct((sectors,) + pieces[0].shape[1:], pieces[0].dtype),
        in_specs=[HBM] * len(before) + [VMEM] * len(pieces),
        out_specs=HBM,
        scratch_shapes=[pltpu.SemaphoreType.DMA((sectors,))],
        input_output_aliases={} if out is None else {0: 0},
        compiler_params=pltpu.CompilerParams(vmem_limit_bytes=16 << 20),
        cost_estimate=pl.CostEstimate(flops=flops, bytes_accessed=1, transcendentals=0),
    )(*before, *pieces)


def exchange(array, bits, members):
    return lax.ppermute(array, "sec", [(s, s ^ bits) for s in members])


def on_device(ops, psi, left_env, right_env, source_map):
    dtype = jnp.bfloat16 if ops == 1 else jnp.float32
    every = range(16)
    inner = range(4, 12)
    outer = [s for s in every if s not in inner]

    def products(step, lefts, psis, rights, flops=1, keep_mid=False):
        return slot(step, source_map, lefts, psis, rights, dtype, flops, keep_mid)

    near = exchange(right_env, 4, every)
    middle = exchange(right_env, 12, inner)
    x_psi = exchange(psi, 2, every)
    own = ([(left_env,), (exchange(left_env, 1, every),)], [(psi,), (exchange(psi, 1, every),)])
    own_0 = products(0, *own, (right_env,))

    near, middle, own_0 = lax.optimization_barrier((near, middle, own_0))
    far_in = exchange(near, 12, inner)
    far_out = exchange(middle, 4, inner)

    x_psi, left_next = lax.optimization_barrier((x_psi, left_env))
    x_left = exchange(left_next, 2, every)
    across_psi = [exchange(part, 1, every) for part in split(x_psi, 1, 6 * x_psi.shape[1] // 8)]
    own_1 = products(1, *own, (near,))
    sent_1 = exchange(own_1, 4, every)

    far_out, far_in = lax.optimization_barrier((far_out, far_in))
    third = exchange(far_in, 4, inner)
    own_2 = products(2, *own, (far_out, far_in))
    own_2, sent_1 = lax.optimization_barrier((own_2, sent_1))
    sent_2 = exchange(own_2, 8, every)

    x_left, sent_2 = lax.optimization_barrier((x_left, sent_2))
    own_middle, own_mid = products(3, *own, (middle,), keep_mid=True)
    sent_own_middle = exchange(own_middle, 12, inner)
    across_left = [exchange(part, 1, every) for part in split(x_left, 0, 5 * x_left.shape[0] // 8)]
    other = ([(x_left,), across_left], [(x_psi,), across_psi])
    other_2 = products(2, *other, (far_out, far_in))
    other_sent_2 = exchange(other_2, 8, every)
    other_middle, other_mid = products(3, *other, (middle,), keep_mid=True)
    sent_other_middle = exchange(other_middle, 12, inner)
    other_1 = products(1, *other, (near,))
    other_sent_1 = exchange(other_1, 4, every)

    third, other_2, other_middle, other_1, sent_own_middle = lax.optimization_barrier((third, other_2, other_middle, other_1, sent_own_middle))
    last_third = second((own_mid, other_mid), third, dtype, 10**10)
    sent_third = exchange(last_third, 12, outer)
    right_last, last_third = lax.optimization_barrier((right_env, last_third))
    other_0 = products(0, *other, (right_last,))

    held = [(0, own_0), (2, other_0), (8, sent_2), (10, other_sent_2), (4, sent_1), (6, other_sent_1)]
    out = place(16, held, flops=10**10)
    out = place(16, [(12, sent_third), (12, sent_own_middle), (14, sent_other_middle)], out)[:, None]
    if ops > 1:
        out = lax.psum_scatter(out, "op", scatter_dimension=2, tiled=True).astype(jnp.bfloat16)
    return out


def solution(mesh):
    placed = (
        P(("group", "sec"), None, None, None),
        P(("group", "op"), "sec", None, None),
        P(("group", "op"), "sec", None, None),
        P(("group", "op"), None),
    )
    return jax.shard_map(
        functools.partial(on_device, mesh.shape["op"]),
        mesh=mesh,
        in_specs=placed,
        out_specs=P("group", "sec", "op", None),
        check_vma=False,
    )
```

```python
import functools

import jax
import jax.numpy as jnp
from jax import lax
from jax.experimental import pallas as pl
from jax.experimental.pallas import tpu as pltpu
from jax.sharding import PartitionSpec as P

HBM = pl.BlockSpec(memory_space=pltpu.HBM)
SMEM = pl.BlockSpec(memory_space=pltpu.SMEM)
VMEM = pl.BlockSpec(memory_space=pltpu.VMEM)


def slot_kernel(step, parts, choices, source, *refs):
    count = len(parts)
    lefts, psis = [], []
    for number, _ in parts:
        lefts.append(refs[:number])
        refs = refs[number:]
    for _, number in parts:
        psis.append(refs[:number])
        refs = refs[number:]
    rights = refs[:choices]
    out, mid_buf, right_buf = refs[choices:]
    terms, _, rows, columns = rights[0].shape
    me = lax.axis_index("sec")
    row = me >> 2
    q = me ^ (4 * step)
    outer = (row == 0) | (row == 3)

    def psi_block(held, sector):
        if len(held) == 1:
            return held[0][0, sector]
        low, high = held
        size = low.shape[1]
        return jnp.where(
            sector < size, low[0, jnp.minimum(sector, size - 1)], high[0, jnp.maximum(sector - size, 0)]
        )

    def left_block(held, k):
        for part in held:
            if k < part.shape[0]:
                return part[k, 0]
            k -= part.shape[0]

    for k in range(terms):
        span = pl.ds(k * columns, columns)
        right = rights[0][k, 0]
        if choices > 1:
            right = jnp.where(outer, right, rights[1][k, 0])
        right_buf[:, span] = right
        for i in range(count):
            mid = jnp.dot(
                left_block(lefts[i], k), psi_block(psis[i], source[k, q]), preferred_element_type=jnp.float32
            )
            mid_buf[pl.ds(i * rows, rows), span] = mid.astype(jnp.bfloat16)
    second_product(mid_buf, right_buf, out)


def second_product(mid, right, out):
    total = lax.dot_general(mid[...], right[...], (((1,), (1,)), ((), ())), preferred_element_type=jnp.float32)
    out[...] = total.reshape(out.shape).astype(out.dtype)


def second_kernel(*refs):
    *mids, right, out, right_buf = refs
    terms, _, _, columns = right.shape
    for k in range(terms):
        right_buf[:, pl.ds(k * columns, columns)] = right[k, 0]
    size = out.shape[0] // len(mids)
    for i, mid in enumerate(mids):
        second_product(mid, right_buf, out.at[pl.ds(i * size, size)])


def second(mids, right, dtype, flops):
    terms, _, rows, columns = right.shape
    return pl.pallas_call(
        second_kernel,
        out_shape=jax.ShapeDtypeStruct((sum(mid.shape[0] for mid in mids) // rows, rows, columns), dtype),
        in_specs=[VMEM] * (len(mids) + 1),
        out_specs=VMEM,
        scratch_shapes=[pltpu.VMEM((rows, terms * columns), jnp.bfloat16)],
        compiler_params=pltpu.CompilerParams(vmem_limit_bytes=16 << 20),
        cost_estimate=pl.CostEstimate(flops=flops, bytes_accessed=1, transcendentals=0),
    )(*mids, right)


def slot(step, source_map, lefts, psis, rights, dtype, flops, keep_mid):
    terms, _, rows, columns = rights[0].shape
    count = len(psis)
    parts = tuple((len(left), len(psi)) for left, psi in zip(lefts, psis))
    held = [part for left in lefts for part in left] + [part for psi in psis for part in psi] + list(rights)
    out = jax.ShapeDtypeStruct((count, rows, columns), dtype)
    mid = jax.ShapeDtypeStruct((count * rows, terms * columns), jnp.bfloat16)
    scratch = [pltpu.VMEM((rows, terms * columns), jnp.bfloat16)]
    if not keep_mid:
        scratch = [pltpu.VMEM(mid.shape, mid.dtype)] + scratch
    return pl.pallas_call(
        functools.partial(slot_kernel, step, parts, len(rights)),
        out_shape=(out, mid) if keep_mid else out,
        in_specs=[SMEM] + [VMEM] * len(held),
        out_specs=(VMEM, VMEM) if keep_mid else VMEM,
        scratch_shapes=scratch,
        compiler_params=pltpu.CompilerParams(vmem_limit_bytes=24 << 20),
        cost_estimate=pl.CostEstimate(flops=flops, bytes_accessed=1, transcendentals=0),
    )(source_map, *held)


def split_kernel(axis, whole, low, high):
    first = low.shape[axis]
    before = (slice(None),) * axis
    low[...] = whole[(*before, slice(0, first))]
    high[...] = whole[(*before, slice(first, None))]


def split(array, axis, first):
    def part(size):
        shape = array.shape[:axis] + (size,) + array.shape[axis + 1 :]
        return jax.ShapeDtypeStruct(shape, array.dtype)

    return pl.pallas_call(
        functools.partial(split_kernel, axis),
        out_shape=(part(first), part(array.shape[axis] - first)),
        in_specs=[VMEM],
        out_specs=(VMEM, VMEM),
        compiler_params=pltpu.CompilerParams(vmem_limit_bytes=12 << 20),
        cost_estimate=pl.CostEstimate(flops=1, bytes_accessed=1, transcendentals=0),
    )(array)


def place_kernel(starts, chosen, *refs):
    *pieces, out, sem = refs
    pieces = pieces[-len(starts) :]
    me = lax.axis_index("sec")
    row = me >> 2
    outer = (row == 0) | (row == 3)

    def copies(chosen_pieces):
        return [
            pltpu.make_async_copy(piece.at[i], out.at[me ^ (start + i)], sem.at[start + i])
            for start, piece in chosen_pieces
            for i in range(piece.shape[0])
        ]

    held = list(zip(starts, pieces))
    if chosen:

        @pl.when(outer)
        def _():
            for copy in copies(held[:1]):
                copy.start()

        @pl.when(jnp.logical_not(outer))
        def _():
            for copy in copies(held[1:]):
                copy.start()

        held = held[:1]
    else:
        for copy in copies(held):
            copy.start()
    for copy in copies(held):
        copy.wait()


def place(sectors, held, out=None, flops=1):
    starts, pieces = zip(*held)
    before = [] if out is None else [out]
    return pl.pallas_call(
        functools.partial(place_kernel, starts, out is not None),
        out_shape=jax.ShapeDtypeStruct((sectors,) + pieces[0].shape[1:], pieces[0].dtype),
        in_specs=[HBM] * len(before) + [VMEM] * len(pieces),
        out_specs=HBM,
        scratch_shapes=[pltpu.SemaphoreType.DMA((sectors,))],
        input_output_aliases={} if out is None else {0: 0},
        compiler_params=pltpu.CompilerParams(vmem_limit_bytes=16 << 20),
        cost_estimate=pl.CostEstimate(flops=flops, bytes_accessed=1, transcendentals=0),
    )(*before, *pieces)


def exchange(array, bits, members):
    return lax.ppermute(array, "sec", [(s, s ^ bits) for s in members])


def on_device(ops, psi, left_env, right_env, source_map):
    dtype = jnp.bfloat16 if ops == 1 else jnp.float32
    every = range(16)
    inner = range(4, 12)
    outer = [s for s in every if s not in inner]

    def products(step, lefts, psis, rights, flops=1, keep_mid=False):
        return slot(step, source_map, lefts, psis, rights, dtype, flops, keep_mid)

    near = exchange(right_env, 4, every)
    middle = exchange(right_env, 12, inner)
    x_psi = exchange(psi, 2, every)
    own = ([(left_env,), (exchange(left_env, 1, every),)], [(psi,), (exchange(psi, 1, every),)])
    own_0 = products(0, *own, (right_env,))

    near, middle, own_0 = lax.optimization_barrier((near, middle, own_0))
    far_in = exchange(near, 12, inner)
    far_out = exchange(middle, 4, inner)

    x_psi, left_next = lax.optimization_barrier((x_psi, left_env))
    x_left = exchange(left_next, 2, every)
    across_psi = [exchange(part, 1, every) for part in split(x_psi, 1, 9 * x_psi.shape[1] // 16)]
    own_middle, own_mid = products(3, *own, (middle,), keep_mid=True)
    sent_own_middle = exchange(own_middle, 12, inner)
    own_1 = products(1, *own, (near,))
    sent_1 = exchange(own_1, 4, every)

    far_out, far_in = lax.optimization_barrier((far_out, far_in))
    third = exchange(far_in, 4, inner)
    own_2 = products(2, *own, (far_out, far_in))
    own_2, sent_1, sent_own_middle = lax.optimization_barrier((own_2, sent_1, sent_own_middle))
    sent_2 = exchange(own_2, 8, every)

    x_left, sent_2 = lax.optimization_barrier((x_left, sent_2))
    across_left = [exchange(part, 1, every) for part in split(x_left, 0, 5 * x_left.shape[0] // 8)]
    other = ([(x_left,), across_left], [(x_psi,), across_psi])
    other_2 = products(2, *other, (far_out, far_in))
    other_sent_2 = exchange(other_2, 8, every)
    other_middle, other_mid = products(3, *other, (middle,), keep_mid=True)
    sent_other_middle = exchange(other_middle, 12, inner)
    other_1 = products(1, *other, (near,))
    other_sent_1 = exchange(other_1, 4, every)

    third, other_1, other_2, other_middle = lax.optimization_barrier((third, other_1, other_2, other_middle))
    last_third = second((own_mid, other_mid), third, dtype, 10**10)
    sent_third = exchange(last_third, 12, outer)
    right_last, last_third = lax.optimization_barrier((right_env, last_third))
    other_0 = products(0, *other, (right_last,))

    held = [(0, own_0), (2, other_0), (8, sent_2), (10, other_sent_2), (4, sent_1), (6, other_sent_1)]
    out = place(16, held, flops=10**10)
    out = place(16, [(12, sent_third), (12, sent_own_middle), (14, sent_other_middle)], out)[:, None]
    if ops > 1:
        out = lax.psum_scatter(out, "op", scatter_dimension=2, tiled=True).astype(jnp.bfloat16)
    return out


def solution(mesh):
    placed = (
        P(("group", "sec"), None, None, None),
        P(("group", "op"), "sec", None, None),
        P(("group", "op"), "sec", None, None),
        P(("group", "op"), None),
    )
    return jax.shard_map(
        functools.partial(on_device, mesh.shape["op"]),
        mesh=mesh,
        in_specs=placed,
        out_specs=P("group", "sec", "op", None),
        check_vma=False,
    )
```

```python
import functools

import jax
import jax.numpy as jnp
from jax import lax
from jax.experimental import pallas as pl
from jax.experimental.pallas import tpu as pltpu
from jax.sharding import PartitionSpec as P

HBM = pl.BlockSpec(memory_space=pltpu.HBM)
SMEM = pl.BlockSpec(memory_space=pltpu.SMEM)
VMEM = pl.BlockSpec(memory_space=pltpu.VMEM)


def slot_kernel(step, parts, choices, source, *refs):
    count = len(parts)
    lefts, psis = [], []
    for number, _ in parts:
        lefts.append(refs[:number])
        refs = refs[number:]
    for _, number in parts:
        psis.append(refs[:number])
        refs = refs[number:]
    rights = refs[:choices]
    out, mid_buf, right_buf = refs[choices:]
    terms, _, rows, columns = rights[0].shape
    me = lax.axis_index("sec")
    row = me >> 2
    q = me ^ (4 * step)
    outer = (row == 0) | (row == 3)

    def psi_block(held, sector):
        if len(held) == 1:
            return held[0][0, sector]
        low, high = held
        size = low.shape[1]
        return jnp.where(
            sector < size, low[0, jnp.minimum(sector, size - 1)], high[0, jnp.maximum(sector - size, 0)]
        )

    def left_block(held, k):
        for part in held:
            if k < part.shape[0]:
                return part[k, 0]
            k -= part.shape[0]

    for k in range(terms):
        span = pl.ds(k * columns, columns)
        right = rights[0][k, 0]
        if choices > 1:
            right = jnp.where(outer, right, rights[1][k, 0])
        right_buf[:, span] = right
        for i in range(count):
            mid = jnp.dot(
                left_block(lefts[i], k), psi_block(psis[i], source[k, q]), preferred_element_type=jnp.float32
            )
            mid_buf[pl.ds(i * rows, rows), span] = mid.astype(jnp.bfloat16)
    second_product(mid_buf, right_buf, out)


def second_product(mid, right, out):
    total = lax.dot_general(mid[...], right[...], (((1,), (1,)), ((), ())), preferred_element_type=jnp.float32)
    out[...] = total.reshape(out.shape).astype(out.dtype)


def second_kernel(*refs):
    *mids, right, out, right_buf = refs
    terms, _, _, columns = right.shape
    for k in range(terms):
        right_buf[:, pl.ds(k * columns, columns)] = right[k, 0]
    size = out.shape[0] // len(mids)
    for i, mid in enumerate(mids):
        second_product(mid, right_buf, out.at[pl.ds(i * size, size)])


def second(mids, right, dtype, flops):
    terms, _, rows, columns = right.shape
    return pl.pallas_call(
        second_kernel,
        out_shape=jax.ShapeDtypeStruct((sum(mid.shape[0] for mid in mids) // rows, rows, columns), dtype),
        in_specs=[VMEM] * (len(mids) + 1),
        out_specs=VMEM,
        scratch_shapes=[pltpu.VMEM((rows, terms * columns), jnp.bfloat16)],
        compiler_params=pltpu.CompilerParams(vmem_limit_bytes=16 << 20),
        cost_estimate=pl.CostEstimate(flops=flops, bytes_accessed=1, transcendentals=0),
    )(*mids, right)


def slot(step, source_map, lefts, psis, rights, dtype, flops, keep_mid):
    terms, _, rows, columns = rights[0].shape
    count = len(psis)
    parts = tuple((len(left), len(psi)) for left, psi in zip(lefts, psis))
    held = [part for left in lefts for part in left] + [part for psi in psis for part in psi] + list(rights)
    out = jax.ShapeDtypeStruct((count, rows, columns), dtype)
    mid = jax.ShapeDtypeStruct((count * rows, terms * columns), jnp.bfloat16)
    scratch = [pltpu.VMEM((rows, terms * columns), jnp.bfloat16)]
    if not keep_mid:
        scratch = [pltpu.VMEM(mid.shape, mid.dtype)] + scratch
    return pl.pallas_call(
        functools.partial(slot_kernel, step, parts, len(rights)),
        out_shape=(out, mid) if keep_mid else out,
        in_specs=[SMEM] + [VMEM] * len(held),
        out_specs=(VMEM, VMEM) if keep_mid else VMEM,
        scratch_shapes=scratch,
        compiler_params=pltpu.CompilerParams(vmem_limit_bytes=24 << 20),
        cost_estimate=pl.CostEstimate(flops=flops, bytes_accessed=1, transcendentals=0),
    )(source_map, *held)


def split_kernel(axis, whole, low, high):
    first = low.shape[axis]
    before = (slice(None),) * axis
    low[...] = whole[(*before, slice(0, first))]
    high[...] = whole[(*before, slice(first, None))]


def split(array, axis, first):
    def part(size):
        shape = array.shape[:axis] + (size,) + array.shape[axis + 1 :]
        return jax.ShapeDtypeStruct(shape, array.dtype)

    return pl.pallas_call(
        functools.partial(split_kernel, axis),
        out_shape=(part(first), part(array.shape[axis] - first)),
        in_specs=[VMEM],
        out_specs=(VMEM, VMEM),
        compiler_params=pltpu.CompilerParams(vmem_limit_bytes=12 << 20),
        cost_estimate=pl.CostEstimate(flops=1, bytes_accessed=1, transcendentals=0),
    )(array)


def place_kernel(starts, chosen, *refs):
    *pieces, out, sem = refs
    pieces = pieces[-len(starts) :]
    me = lax.axis_index("sec")
    row = me >> 2
    outer = (row == 0) | (row == 3)

    def copies(chosen_pieces):
        return [
            pltpu.make_async_copy(piece.at[i], out.at[me ^ (start + i)], sem.at[start + i])
            for start, piece in chosen_pieces
            for i in range(piece.shape[0])
        ]

    held = list(zip(starts, pieces))
    if chosen:

        @pl.when(outer)
        def _():
            for copy in copies(held[:1]):
                copy.start()

        @pl.when(jnp.logical_not(outer))
        def _():
            for copy in copies(held[1:]):
                copy.start()

        held = held[:1]
    else:
        for copy in copies(held):
            copy.start()
    for copy in copies(held):
        copy.wait()


def place(sectors, held, out=None, flops=1):
    starts, pieces = zip(*held)
    before = [] if out is None else [out]
    return pl.pallas_call(
        functools.partial(place_kernel, starts, out is not None),
        out_shape=jax.ShapeDtypeStruct((sectors,) + pieces[0].shape[1:], pieces[0].dtype),
        in_specs=[HBM] * len(before) + [VMEM] * len(pieces),
        out_specs=HBM,
        scratch_shapes=[pltpu.SemaphoreType.DMA((sectors,))],
        input_output_aliases={} if out is None else {0: 0},
        compiler_params=pltpu.CompilerParams(vmem_limit_bytes=16 << 20),
        cost_estimate=pl.CostEstimate(flops=flops, bytes_accessed=1, transcendentals=0),
    )(*before, *pieces)


def exchange(array, bits, members):
    return lax.ppermute(array, "sec", [(s, s ^ bits) for s in members])


def on_device(ops, psi, left_env, right_env, source_map):
    dtype = jnp.bfloat16 if ops == 1 else jnp.float32
    every = range(16)
    inner = range(4, 12)
    outer = [s for s in every if s not in inner]

    def products(step, lefts, psis, rights, flops=1, keep_mid=False):
        return slot(step, source_map, lefts, psis, rights, dtype, flops, keep_mid)

    near = exchange(right_env, 4, every)
    middle = exchange(right_env, 12, inner)
    x_psi = exchange(psi, 2, every)
    own = ([(left_env,), (exchange(left_env, 1, every),)], [(psi,), (exchange(psi, 1, every),)])
    own_0 = products(0, *own, (right_env,))

    near, middle, own_0 = lax.optimization_barrier((near, middle, own_0))
    far_in = exchange(near, 12, inner)
    far_out = exchange(middle, 4, inner)

    own_middle, own_mid = products(3, *own, (middle,), keep_mid=True)
    own_1 = products(1, *own, (near,))
    x_psi, left_next, own_1, own_middle = lax.optimization_barrier((x_psi, left_env, own_1, own_middle))
    x_left = exchange(left_next, 2, every)
    across_psi = [exchange(part, 1, every) for part in split(x_psi, 1, 9 * x_psi.shape[1] // 16)]
    sent_1 = exchange(own_1, 4, every)
    sent_own_middle = exchange(own_middle, 12, inner)

    far_out, far_in = lax.optimization_barrier((far_out, far_in))
    third = exchange(far_in, 4, inner)
    own_2 = products(2, *own, (far_out, far_in))
    own_2, sent_1, sent_own_middle = lax.optimization_barrier((own_2, sent_1, sent_own_middle))
    sent_2 = exchange(own_2, 8, every)

    x_left, sent_2 = lax.optimization_barrier((x_left, sent_2))
    across_left = [exchange(part, 1, every) for part in split(x_left, 0, 5 * x_left.shape[0] // 8)]
    other = ([(x_left,), across_left], [(x_psi,), across_psi])
    other_2 = products(2, *other, (far_out, far_in))
    other_sent_2 = exchange(other_2, 8, every)
    other_middle, other_mid = products(3, *other, (middle,), keep_mid=True)
    sent_other_middle = exchange(other_middle, 12, inner)
    other_1 = products(1, *other, (near,))
    other_sent_1 = exchange(other_1, 4, every)

    third, other_1, other_2, other_middle = lax.optimization_barrier((third, other_1, other_2, other_middle))
    last_third = second((own_mid, other_mid), third, dtype, 10**10)
    sent_third = exchange(last_third, 12, outer)
    right_last, last_third = lax.optimization_barrier((right_env, last_third))
    other_0 = products(0, *other, (right_last,))

    held = [(0, own_0), (2, other_0), (8, sent_2), (10, other_sent_2), (4, sent_1), (6, other_sent_1)]
    out = place(16, held, flops=10**10)
    out = place(16, [(12, sent_third), (12, sent_own_middle), (14, sent_other_middle)], out)[:, None]
    if ops > 1:
        out = lax.psum_scatter(out, "op", scatter_dimension=2, tiled=True).astype(jnp.bfloat16)
    return out


def solution(mesh):
    placed = (
        P(("group", "sec"), None, None, None),
        P(("group", "op"), "sec", None, None),
        P(("group", "op"), "sec", None, None),
        P(("group", "op"), None),
    )
    return jax.shard_map(
        functools.partial(on_device, mesh.shape["op"]),
        mesh=mesh,
        in_specs=placed,
        out_specs=P("group", "sec", "op", None),
        check_vma=False,
    )
```

```python
import functools

import jax
import jax.numpy as jnp
from jax import lax
from jax.experimental import pallas as pl
from jax.experimental.pallas import tpu as pltpu
from jax.sharding import PartitionSpec as P

HBM = pl.BlockSpec(memory_space=pltpu.HBM)
SMEM = pl.BlockSpec(memory_space=pltpu.SMEM)
VMEM = pl.BlockSpec(memory_space=pltpu.VMEM)


def slot_kernel(step, parts, choices, source, *refs):
    count = len(parts)
    lefts, psis = [], []
    for number, _ in parts:
        lefts.append(refs[:number])
        refs = refs[number:]
    for _, number in parts:
        psis.append(refs[:number])
        refs = refs[number:]
    rights = refs[:choices]
    out, mid_buf, right_buf = refs[choices:]
    terms, _, rows, columns = rights[0].shape
    me = lax.axis_index("sec")
    row = me >> 2
    q = me ^ (4 * step)
    outer = (row == 0) | (row == 3)

    def psi_block(held, sector):
        if len(held) == 1:
            return held[0][0, sector]
        low, high = held
        size = low.shape[1]
        return jnp.where(
            sector < size, low[0, jnp.minimum(sector, size - 1)], high[0, jnp.maximum(sector - size, 0)]
        )

    def left_block(held, k):
        for part in held:
            if k < part.shape[0]:
                return part[k, 0]
            k -= part.shape[0]

    for k in range(terms):
        span = pl.ds(k * columns, columns)
        right = rights[0][k, 0]
        if choices > 1:
            right = jnp.where(outer, right, rights[1][k, 0])
        right_buf[:, span] = right
        for i in range(count):
            mid = jnp.dot(
                left_block(lefts[i], k), psi_block(psis[i], source[k, q]), preferred_element_type=jnp.float32
            )
            mid_buf[pl.ds(i * rows, rows), span] = mid.astype(jnp.bfloat16)
    second_product(mid_buf, right_buf, out)


def second_product(mid, right, out):
    total = lax.dot_general(mid[...], right[...], (((1,), (1,)), ((), ())), preferred_element_type=jnp.float32)
    out[...] = total.reshape(out.shape).astype(out.dtype)


def second_kernel(*refs):
    *mids, right, out, right_buf = refs
    terms, _, _, columns = right.shape
    for k in range(terms):
        right_buf[:, pl.ds(k * columns, columns)] = right[k, 0]
    size = out.shape[0] // len(mids)
    for i, mid in enumerate(mids):
        second_product(mid, right_buf, out.at[pl.ds(i * size, size)])


def second(mids, right, dtype, flops):
    terms, _, rows, columns = right.shape
    return pl.pallas_call(
        second_kernel,
        out_shape=jax.ShapeDtypeStruct((sum(mid.shape[0] for mid in mids) // rows, rows, columns), dtype),
        in_specs=[VMEM] * (len(mids) + 1),
        out_specs=VMEM,
        scratch_shapes=[pltpu.VMEM((rows, terms * columns), jnp.bfloat16)],
        compiler_params=pltpu.CompilerParams(vmem_limit_bytes=16 << 20),
        cost_estimate=pl.CostEstimate(flops=flops, bytes_accessed=1, transcendentals=0),
    )(*mids, right)


def slot(step, source_map, lefts, psis, rights, dtype, flops, keep_mid):
    terms, _, rows, columns = rights[0].shape
    count = len(psis)
    parts = tuple((len(left), len(psi)) for left, psi in zip(lefts, psis))
    held = [part for left in lefts for part in left] + [part for psi in psis for part in psi] + list(rights)
    out = jax.ShapeDtypeStruct((count, rows, columns), dtype)
    mid = jax.ShapeDtypeStruct((count * rows, terms * columns), jnp.bfloat16)
    scratch = [pltpu.VMEM((rows, terms * columns), jnp.bfloat16)]
    if not keep_mid:
        scratch = [pltpu.VMEM(mid.shape, mid.dtype)] + scratch
    return pl.pallas_call(
        functools.partial(slot_kernel, step, parts, len(rights)),
        out_shape=(out, mid) if keep_mid else out,
        in_specs=[SMEM] + [VMEM] * len(held),
        out_specs=(VMEM, VMEM) if keep_mid else VMEM,
        scratch_shapes=scratch,
        compiler_params=pltpu.CompilerParams(vmem_limit_bytes=24 << 20),
        cost_estimate=pl.CostEstimate(flops=flops, bytes_accessed=1, transcendentals=0),
    )(source_map, *held)


def split_kernel(axis, whole, low, high):
    first = low.shape[axis]
    before = (slice(None),) * axis
    low[...] = whole[(*before, slice(0, first))]
    high[...] = whole[(*before, slice(first, None))]


def split(array, axis, first):
    def part(size):
        shape = array.shape[:axis] + (size,) + array.shape[axis + 1 :]
        return jax.ShapeDtypeStruct(shape, array.dtype)

    return pl.pallas_call(
        functools.partial(split_kernel, axis),
        out_shape=(part(first), part(array.shape[axis] - first)),
        in_specs=[VMEM],
        out_specs=(VMEM, VMEM),
        compiler_params=pltpu.CompilerParams(vmem_limit_bytes=12 << 20),
        cost_estimate=pl.CostEstimate(flops=1, bytes_accessed=1, transcendentals=0),
    )(array)


def place_kernel(starts, shared, *refs):
    *pieces, out, sem = refs
    pieces = pieces[-len(starts) :]
    me = lax.axis_index("sec")
    row = me >> 2
    outer = (row == 0) | (row == 3)

    def copies(held):
        return [
            pltpu.make_async_copy(piece.at[i], out.at[me ^ (start + i)], sem.at[start + i])
            for start, piece in held
            for i in range(piece.shape[0])
        ]

    held = list(zip(starts, pieces))
    for copy in copies(held[:shared]):
        copy.start()
    if shared < len(held):

        @pl.when(outer)
        def _():
            for copy in copies(held[shared : shared + 1]):
                copy.start()

        @pl.when(jnp.logical_not(outer))
        def _():
            for copy in copies(held[shared + 1 :]):
                copy.start()

    for copy in copies(held[: shared + 1]):
        copy.wait()


def place(sectors, held, out=None, shared=None, flops=1):
    starts, pieces = zip(*held)
    before = [] if out is None else [out]
    return pl.pallas_call(
        functools.partial(place_kernel, starts, len(held) if shared is None else shared),
        out_shape=jax.ShapeDtypeStruct((sectors,) + pieces[0].shape[1:], pieces[0].dtype),
        in_specs=[HBM] * len(before) + [VMEM] * len(pieces),
        out_specs=HBM,
        scratch_shapes=[pltpu.SemaphoreType.DMA((sectors,))],
        input_output_aliases={} if out is None else {0: 0},
        compiler_params=pltpu.CompilerParams(vmem_limit_bytes=16 << 20),
        cost_estimate=pl.CostEstimate(flops=flops, bytes_accessed=1, transcendentals=0),
    )(*before, *pieces)


def exchange(array, bits, members):
    return lax.ppermute(array, "sec", [(s, s ^ bits) for s in members])


def on_device(ops, psi, left_env, right_env, source_map):
    dtype = jnp.bfloat16 if ops == 1 else jnp.float32
    every = range(16)
    inner = range(4, 12)
    outer = [s for s in every if s not in inner]

    def products(step, lefts, psis, rights, flops=1, keep_mid=False):
        return slot(step, source_map, lefts, psis, rights, dtype, flops, keep_mid)

    near = exchange(right_env, 4, every)
    middle = exchange(right_env, 12, inner)
    x_psi = exchange(psi, 2, every)
    own = ([(left_env,), (exchange(left_env, 1, every),)], [(psi,), (exchange(psi, 1, every),)])
    own_0 = products(0, *own, (right_env,))

    near, middle, own_0 = lax.optimization_barrier((near, middle, own_0))
    far_in = exchange(near, 12, inner)
    far_out = exchange(middle, 4, inner)

    own_middle, own_mid = products(3, *own, (middle,), keep_mid=True)
    own_1 = products(1, *own, (near,))
    x_psi, left_next, own_1, own_middle = lax.optimization_barrier((x_psi, left_env, own_1, own_middle))
    x_left = exchange(left_next, 2, every)
    across_psi = [exchange(part, 1, every) for part in split(x_psi, 1, 9 * x_psi.shape[1] // 16)]
    sent_1 = exchange(own_1, 4, every)
    sent_own_middle = exchange(own_middle, 12, inner)

    far_out, far_in = lax.optimization_barrier((far_out, far_in))
    third = exchange(far_in, 4, inner)
    own_2 = products(2, *own, (far_out, far_in))
    own_2, sent_1, sent_own_middle = lax.optimization_barrier((own_2, sent_1, sent_own_middle))
    sent_2 = exchange(own_2, 8, every)

    x_left, sent_2 = lax.optimization_barrier((x_left, sent_2))
    across_left = [exchange(part, 1, every) for part in split(x_left, 0, 5 * x_left.shape[0] // 8)]
    other = ([(x_left,), across_left], [(x_psi,), across_psi])
    other_2 = products(2, *other, (far_out, far_in))
    other_sent_2 = exchange(other_2, 8, every)
    other_middle, other_mid = products(3, *other, (middle,), keep_mid=True)
    sent_other_middle = exchange(other_middle, 12, inner)
    other_1 = products(1, *other, (near,))

    third, other_1, other_2, other_middle = lax.optimization_barrier((third, other_1, other_2, other_middle))
    last_third = second((own_mid, other_mid), third, dtype, 10**10)
    last_third, other_1 = lax.optimization_barrier((last_third, other_1))
    sent_third = exchange(last_third, 12, outer)
    other_sent_1 = exchange(other_1, 4, every)
    right_last, last_third = lax.optimization_barrier((right_env, last_third))
    other_0 = products(0, *other, (right_last,))

    out = place(16, [(0, own_0), (2, other_0), (4, sent_1), (8, sent_2), (10, other_sent_2)], flops=10**10)
    last = [(12, sent_third), (12, sent_own_middle), (14, sent_other_middle)]
    out = place(16, [(6, other_sent_1)] + last, out, 1)[:, None]
    if ops > 1:
        out = lax.psum_scatter(out, "op", scatter_dimension=2, tiled=True).astype(jnp.bfloat16)
    return out


def solution(mesh):
    placed = (
        P(("group", "sec"), None, None, None),
        P(("group", "op"), "sec", None, None),
        P(("group", "op"), "sec", None, None),
        P(("group", "op"), None),
    )
    return jax.shard_map(
        functools.partial(on_device, mesh.shape["op"]),
        mesh=mesh,
        in_specs=placed,
        out_specs=P("group", "sec", "op", None),
        check_vma=False,
    )
```

```python
import functools

import jax
import jax.numpy as jnp
from jax import lax
from jax.experimental import pallas as pl
from jax.experimental.pallas import tpu as pltpu
from jax.sharding import PartitionSpec as P

HBM = pl.BlockSpec(memory_space=pltpu.HBM)
SMEM = pl.BlockSpec(memory_space=pltpu.SMEM)
VMEM = pl.BlockSpec(memory_space=pltpu.VMEM)


def slot_kernel(step, parts, choices, source, *refs):
    count = len(parts)
    lefts, psis = [], []
    for number, _ in parts:
        lefts.append(refs[:number])
        refs = refs[number:]
    for _, number in parts:
        psis.append(refs[:number])
        refs = refs[number:]
    rights = refs[:choices]
    out, mid_buf, right_buf = refs[choices:]
    terms, _, rows, columns = rights[0].shape
    me = lax.axis_index("sec")
    row = me >> 2
    q = me ^ (4 * step)
    outer = (row == 0) | (row == 3)

    def psi_block(held, sector):
        if len(held) == 1:
            return held[0][0, sector]
        low, high = held
        size = low.shape[1]
        return jnp.where(
            sector < size, low[0, jnp.minimum(sector, size - 1)], high[0, jnp.maximum(sector - size, 0)]
        )

    def left_block(held, k):
        for part in held:
            if k < part.shape[0]:
                return part[k, 0]
            k -= part.shape[0]

    for k in range(terms):
        span = pl.ds(k * columns, columns)
        right = rights[0][k, 0]
        if choices > 1:
            right = jnp.where(outer, right, rights[1][k, 0])
        right_buf[:, span] = right
        for i in range(count):
            mid = jnp.dot(
                left_block(lefts[i], k), psi_block(psis[i], source[k, q]), preferred_element_type=jnp.float32
            )
            mid_buf[pl.ds(i * rows, rows), span] = mid.astype(jnp.bfloat16)
    second_product(mid_buf, right_buf, out)


def second_product(mid, right, out):
    total = lax.dot_general(mid[...], right[...], (((1,), (1,)), ((), ())), preferred_element_type=jnp.float32)
    out[...] = total.reshape(out.shape).astype(out.dtype)


def second_kernel(*refs):
    *mids, right, out, right_buf = refs
    terms, _, _, columns = right.shape
    for k in range(terms):
        right_buf[:, pl.ds(k * columns, columns)] = right[k, 0]
    size = out.shape[0] // len(mids)
    for i, mid in enumerate(mids):
        second_product(mid, right_buf, out.at[pl.ds(i * size, size)])


def second(mids, right, dtype, flops):
    terms, _, rows, columns = right.shape
    return pl.pallas_call(
        second_kernel,
        out_shape=jax.ShapeDtypeStruct((sum(mid.shape[0] for mid in mids) // rows, rows, columns), dtype),
        in_specs=[VMEM] * (len(mids) + 1),
        out_specs=VMEM,
        scratch_shapes=[pltpu.VMEM((rows, terms * columns), jnp.bfloat16)],
        compiler_params=pltpu.CompilerParams(vmem_limit_bytes=16 << 20),
        cost_estimate=pl.CostEstimate(flops=flops, bytes_accessed=1, transcendentals=0),
    )(*mids, right)


def slot(step, source_map, lefts, psis, rights, dtype, flops, keep_mid):
    terms, _, rows, columns = rights[0].shape
    count = len(psis)
    parts = tuple((len(left), len(psi)) for left, psi in zip(lefts, psis))
    held = [part for left in lefts for part in left] + [part for psi in psis for part in psi] + list(rights)
    out = jax.ShapeDtypeStruct((count, rows, columns), dtype)
    mid = jax.ShapeDtypeStruct((count * rows, terms * columns), jnp.bfloat16)
    scratch = [pltpu.VMEM((rows, terms * columns), jnp.bfloat16)]
    if not keep_mid:
        scratch = [pltpu.VMEM(mid.shape, mid.dtype)] + scratch
    return pl.pallas_call(
        functools.partial(slot_kernel, step, parts, len(rights)),
        out_shape=(out, mid) if keep_mid else out,
        in_specs=[SMEM] + [VMEM] * len(held),
        out_specs=(VMEM, VMEM) if keep_mid else VMEM,
        scratch_shapes=scratch,
        compiler_params=pltpu.CompilerParams(vmem_limit_bytes=24 << 20),
        cost_estimate=pl.CostEstimate(flops=flops, bytes_accessed=1, transcendentals=0),
    )(source_map, *held)


def split_kernel(axis, whole, low, high):
    first = low.shape[axis]
    before = (slice(None),) * axis
    low[...] = whole[(*before, slice(0, first))]
    high[...] = whole[(*before, slice(first, None))]


def split(array, axis, first):
    def part(size):
        shape = array.shape[:axis] + (size,) + array.shape[axis + 1 :]
        return jax.ShapeDtypeStruct(shape, array.dtype)

    return pl.pallas_call(
        functools.partial(split_kernel, axis),
        out_shape=(part(first), part(array.shape[axis] - first)),
        in_specs=[VMEM],
        out_specs=(VMEM, VMEM),
        compiler_params=pltpu.CompilerParams(vmem_limit_bytes=12 << 20),
        cost_estimate=pl.CostEstimate(flops=1, bytes_accessed=1, transcendentals=0),
    )(array)


def place_kernel(starts, chosen, *refs):
    *pieces, out, sem = refs
    pieces = pieces[-len(starts) :]
    me = lax.axis_index("sec")
    row = me >> 2
    outer = (row == 0) | (row == 3)

    def copies(chosen_pieces):
        return [
            pltpu.make_async_copy(piece.at[i], out.at[me ^ (start + i)], sem.at[start + i])
            for start, piece in chosen_pieces
            for i in range(piece.shape[0])
        ]

    held = list(zip(starts, pieces))
    if chosen:

        @pl.when(outer)
        def _():
            for copy in copies(held[:1]):
                copy.start()

        @pl.when(jnp.logical_not(outer))
        def _():
            for copy in copies(held[1:]):
                copy.start()

        held = held[:1]
    else:
        for copy in copies(held):
            copy.start()
    for copy in copies(held):
        copy.wait()


def place(sectors, held, out=None, flops=1):
    starts, pieces = zip(*held)
    before = [] if out is None else [out]
    return pl.pallas_call(
        functools.partial(place_kernel, starts, out is not None),
        out_shape=jax.ShapeDtypeStruct((sectors,) + pieces[0].shape[1:], pieces[0].dtype),
        in_specs=[HBM] * len(before) + [VMEM] * len(pieces),
        out_specs=HBM,
        scratch_shapes=[pltpu.SemaphoreType.DMA((sectors,))],
        input_output_aliases={} if out is None else {0: 0},
        compiler_params=pltpu.CompilerParams(vmem_limit_bytes=16 << 20),
        cost_estimate=pl.CostEstimate(flops=flops, bytes_accessed=1, transcendentals=0),
    )(*before, *pieces)


def exchange(array, bits, members):
    return lax.ppermute(array, "sec", [(s, s ^ bits) for s in members])


def on_device(ops, psi, left_env, right_env, source_map):
    dtype = jnp.bfloat16 if ops == 1 else jnp.float32
    every = range(16)
    inner = range(4, 12)
    outer = [s for s in every if s not in inner]

    def products(step, lefts, psis, rights, flops=1, keep_mid=False):
        return slot(step, source_map, lefts, psis, rights, dtype, flops, keep_mid)

    near = exchange(right_env, 4, every)
    middle = exchange(right_env, 12, inner)
    x_psi = exchange(psi, 2, every)
    own = ([(left_env,), (exchange(left_env, 1, every),)], [(psi,), (exchange(psi, 1, every),)])
    own_0 = products(0, *own, (right_env,))

    middle, near, own_0 = lax.optimization_barrier((middle, near, own_0))
    far_in = exchange(near, 12, inner)
    far_out = exchange(middle, 4, inner)

    x_psi, left_next = lax.optimization_barrier((x_psi, left_env))
    x_left = exchange(left_next, 2, every)
    across_psi = [exchange(part, 1, every) for part in split(x_psi, 1, 6 * x_psi.shape[1] // 8)]
    own_1 = products(1, *own, (near,))
    sent_1 = exchange(own_1, 4, every)

    far_out, far_in = lax.optimization_barrier((far_out, far_in))
    third = exchange(far_in, 4, inner)
    own_2 = products(2, *own, (far_out, far_in))
    own_2, sent_1 = lax.optimization_barrier((own_2, sent_1))
    sent_2 = exchange(own_2, 8, every)

    x_left, sent_2 = lax.optimization_barrier((x_left, sent_2))
    own_middle, own_mid = products(3, *own, (middle,), keep_mid=True)
    sent_own_middle = exchange(own_middle, 12, inner)
    across_left = [exchange(part, 1, every) for part in split(x_left, 0, 5 * x_left.shape[0] // 8)]
    other = ([(x_left,), across_left], [(x_psi,), across_psi])
    other_2 = products(2, *other, (far_out, far_in))
    other_sent_2 = exchange(other_2, 8, every)
    other_middle, other_mid = products(3, *other, (middle,), keep_mid=True)
    sent_other_middle = exchange(other_middle, 12, inner)
    other_1 = products(1, *other, (near,))
    other_sent_1 = exchange(other_1, 4, every)

    third, other_2, other_middle, other_1, sent_own_middle = lax.optimization_barrier((third, other_2, other_middle, other_1, sent_own_middle))
    last_third = second((own_mid, other_mid), third, dtype, 10**10)
    sent_third = exchange(last_third, 12, outer)
    right_last, last_third = lax.optimization_barrier((right_env, last_third))
    other_0 = products(0, *other, (right_last,))

    held = [(0, own_0), (2, other_0), (8, sent_2), (10, other_sent_2), (4, sent_1), (6, other_sent_1)]
    out = place(16, held, flops=10**10)
    out = place(16, [(12, sent_third), (12, sent_own_middle), (14, sent_other_middle)], out)[:, None]
    if ops > 1:
        out = lax.psum_scatter(out, "op", scatter_dimension=2, tiled=True).astype(jnp.bfloat16)
    return out


def solution(mesh):
    placed = (
        P(("group", "sec"), None, None, None),
        P(("group", "op"), "sec", None, None),
        P(("group", "op"), "sec", None, None),
        P(("group", "op"), None),
    )
    return jax.shard_map(
        functools.partial(on_device, mesh.shape["op"]),
        mesh=mesh,
        in_specs=placed,
        out_specs=P("group", "sec", "op", None),
        check_vma=False,
    )
```

```python
import functools

import jax
import jax.numpy as jnp
from jax import lax
from jax.experimental import pallas as pl
from jax.experimental.pallas import tpu as pltpu
from jax.sharding import PartitionSpec as P

HBM = pl.BlockSpec(memory_space=pltpu.HBM)
SMEM = pl.BlockSpec(memory_space=pltpu.SMEM)
VMEM = pl.BlockSpec(memory_space=pltpu.VMEM)


def slot_kernel(step, parts, choices, source, *refs):
    count = len(parts)
    lefts, psis = [], []
    for number, _ in parts:
        lefts.append(refs[:number])
        refs = refs[number:]
    for _, number in parts:
        psis.append(refs[:number])
        refs = refs[number:]
    rights = refs[:choices]
    out, mid_buf, right_buf = refs[choices:]
    terms, _, rows, columns = rights[0].shape
    me = lax.axis_index("sec")
    row = me >> 2
    q = me ^ (4 * step)
    outer = (row == 0) | (row == 3)

    def psi_block(held, sector):
        if len(held) == 1:
            return held[0][0, sector]
        low, high = held
        size = low.shape[1]
        return jnp.where(
            sector < size, low[0, jnp.minimum(sector, size - 1)], high[0, jnp.maximum(sector - size, 0)]
        )

    def left_block(held, k):
        for part in held:
            if k < part.shape[0]:
                return part[k, 0]
            k -= part.shape[0]

    for k in range(terms):
        span = pl.ds(k * columns, columns)
        right = rights[0][k, 0]
        if choices > 1:
            right = jnp.where(outer, right, rights[1][k, 0])
        right_buf[:, span] = right
        for i in range(count):
            mid = jnp.dot(
                left_block(lefts[i], k), psi_block(psis[i], source[k, q]), preferred_element_type=jnp.float32
            )
            mid_buf[pl.ds(i * rows, rows), span] = mid.astype(jnp.bfloat16)
    second_product(mid_buf, right_buf, out)


def second_product(mid, right, out):
    total = lax.dot_general(mid[...], right[...], (((1,), (1,)), ((), ())), preferred_element_type=jnp.float32)
    out[...] = total.reshape(out.shape).astype(out.dtype)


def second_kernel(*refs):
    *mids, right, out, right_buf = refs
    terms, _, _, columns = right.shape
    for k in range(terms):
        right_buf[:, pl.ds(k * columns, columns)] = right[k, 0]
    size = out.shape[0] // len(mids)
    for i, mid in enumerate(mids):
        second_product(mid, right_buf, out.at[pl.ds(i * size, size)])


def second(mids, right, dtype, flops):
    terms, _, rows, columns = right.shape
    return pl.pallas_call(
        second_kernel,
        out_shape=jax.ShapeDtypeStruct((sum(mid.shape[0] for mid in mids) // rows, rows, columns), dtype),
        in_specs=[VMEM] * (len(mids) + 1),
        out_specs=VMEM,
        scratch_shapes=[pltpu.VMEM((rows, terms * columns), jnp.bfloat16)],
        compiler_params=pltpu.CompilerParams(vmem_limit_bytes=16 << 20),
        cost_estimate=pl.CostEstimate(flops=flops, bytes_accessed=1, transcendentals=0),
    )(*mids, right)


def slot(step, source_map, lefts, psis, rights, dtype, flops, keep_mid):
    terms, _, rows, columns = rights[0].shape
    count = len(psis)
    parts = tuple((len(left), len(psi)) for left, psi in zip(lefts, psis))
    held = [part for left in lefts for part in left] + [part for psi in psis for part in psi] + list(rights)
    out = jax.ShapeDtypeStruct((count, rows, columns), dtype)
    mid = jax.ShapeDtypeStruct((count * rows, terms * columns), jnp.bfloat16)
    scratch = [pltpu.VMEM((rows, terms * columns), jnp.bfloat16)]
    if not keep_mid:
        scratch = [pltpu.VMEM(mid.shape, mid.dtype)] + scratch
    return pl.pallas_call(
        functools.partial(slot_kernel, step, parts, len(rights)),
        out_shape=(out, mid) if keep_mid else out,
        in_specs=[SMEM] + [VMEM] * len(held),
        out_specs=(VMEM, VMEM) if keep_mid else VMEM,
        scratch_shapes=scratch,
        compiler_params=pltpu.CompilerParams(vmem_limit_bytes=24 << 20),
        cost_estimate=pl.CostEstimate(flops=flops, bytes_accessed=1, transcendentals=0),
    )(source_map, *held)


def split_kernel(axis, whole, low, high):
    first = low.shape[axis]
    before = (slice(None),) * axis
    low[...] = whole[(*before, slice(0, first))]
    high[...] = whole[(*before, slice(first, None))]


def split(array, axis, first):
    def part(size):
        shape = array.shape[:axis] + (size,) + array.shape[axis + 1 :]
        return jax.ShapeDtypeStruct(shape, array.dtype)

    return pl.pallas_call(
        functools.partial(split_kernel, axis),
        out_shape=(part(first), part(array.shape[axis] - first)),
        in_specs=[VMEM],
        out_specs=(VMEM, VMEM),
        compiler_params=pltpu.CompilerParams(vmem_limit_bytes=12 << 20),
        cost_estimate=pl.CostEstimate(flops=1, bytes_accessed=1, transcendentals=0),
    )(array)


def place_kernel(starts, chosen, *refs):
    *pieces, out, sem = refs
    pieces = pieces[-len(starts) :]
    me = lax.axis_index("sec")
    row = me >> 2
    outer = (row == 0) | (row == 3)

    def copies(chosen_pieces):
        return [
            pltpu.make_async_copy(piece.at[i], out.at[me ^ (start + i)], sem.at[start + i])
            for start, piece in chosen_pieces
            for i in range(piece.shape[0])
        ]

    held = list(zip(starts, pieces))
    if chosen:

        @pl.when(outer)
        def _():
            for copy in copies(held[:1]):
                copy.start()

        @pl.when(jnp.logical_not(outer))
        def _():
            for copy in copies(held[1:]):
                copy.start()

        held = held[:1]
    else:
        for copy in copies(held):
            copy.start()
    for copy in copies(held):
        copy.wait()


def place(sectors, held, out=None, flops=1):
    starts, pieces = zip(*held)
    before = [] if out is None else [out]
    return pl.pallas_call(
        functools.partial(place_kernel, starts, out is not None),
        out_shape=jax.ShapeDtypeStruct((sectors,) + pieces[0].shape[1:], pieces[0].dtype),
        in_specs=[HBM] * len(before) + [VMEM] * len(pieces),
        out_specs=HBM,
        scratch_shapes=[pltpu.SemaphoreType.DMA((sectors,))],
        input_output_aliases={} if out is None else {0: 0},
        compiler_params=pltpu.CompilerParams(vmem_limit_bytes=16 << 20),
        cost_estimate=pl.CostEstimate(flops=flops, bytes_accessed=1, transcendentals=0),
    )(*before, *pieces)


def exchange(array, bits, members):
    return lax.ppermute(array, "sec", [(s, s ^ bits) for s in members])


def on_device(ops, psi, left_env, right_env, source_map):
    dtype = jnp.bfloat16 if ops == 1 else jnp.float32
    every = range(16)
    inner = range(4, 12)
    outer = [s for s in every if s not in inner]

    def products(step, lefts, psis, rights, flops=1, keep_mid=False):
        return slot(step, source_map, lefts, psis, rights, dtype, flops, keep_mid)

    near = exchange(right_env, 4, every)
    middle = exchange(right_env, 12, inner)
    x_psi = exchange(psi, 2, every)
    own = ([(left_env,), (exchange(left_env, 1, every),)], [(psi,), (exchange(psi, 1, every),)])
    own_0 = products(0, *own, (right_env,))

    near, middle, own_0 = lax.optimization_barrier((near, middle, own_0))
    far_in = exchange(near, 12, inner)
    far_out = exchange(middle, 4, inner)

    own_middle, own_mid = products(3, *own, (middle,), keep_mid=True)
    own_1 = products(1, *own, (near,))
    x_psi, left_next, own_1, own_middle = lax.optimization_barrier((x_psi, left_env, own_1, own_middle))
    x_left = exchange(left_next, 2, every)
    across_psi = [exchange(part, 1, every) for part in split(x_psi, 1, 9 * x_psi.shape[1] // 16)]
    sent_1 = exchange(own_1, 4, every)
    sent_own_middle = exchange(own_middle, 12, inner)

    far_out, far_in = lax.optimization_barrier((far_out, far_in))
    third = exchange(far_in, 4, inner)
    own_2 = products(2, *own, (far_out, far_in))
    own_2, sent_1, sent_own_middle = lax.optimization_barrier((own_2, sent_1, sent_own_middle))
    sent_2 = exchange(own_2, 8, every)

    x_left, sent_2 = lax.optimization_barrier((x_left, sent_2))
    across_left = [exchange(part, 1, every) for part in split(x_left, 0, 5 * x_left.shape[0] // 8)]
    other = ([(x_left,), across_left], [(x_psi,), across_psi])
    other_2 = products(2, *other, (far_out, far_in))
    other_sent_2 = exchange(other_2, 8, every)
    other_middle, other_mid = products(3, *other, (middle,), keep_mid=True)
    sent_other_middle = exchange(other_middle, 12, inner)
    other_1 = products(1, *other, (near,))
    other_sent_1 = exchange(other_1, 4, every)

    third, other_1, other_2, sent_other_middle = lax.optimization_barrier((third, other_1, other_2, sent_other_middle))
    last_third = second((own_mid, other_mid), third, dtype, 10**10)
    sent_third = exchange(last_third, 12, outer)
    right_last, last_third = lax.optimization_barrier((right_env, last_third))
    other_0 = products(0, *other, (right_last,))

    held = [(0, own_0), (2, other_0), (8, sent_2), (10, other_sent_2), (4, sent_1), (6, other_sent_1)]
    out = place(16, held, flops=10**10)
    out = place(16, [(12, sent_third), (12, sent_own_middle), (14, sent_other_middle)], out)[:, None]
    if ops > 1:
        out = lax.psum_scatter(out, "op", scatter_dimension=2, tiled=True).astype(jnp.bfloat16)
    return out


def solution(mesh):
    placed = (
        P(("group", "sec"), None, None, None),
        P(("group", "op"), "sec", None, None),
        P(("group", "op"), "sec", None, None),
        P(("group", "op"), None),
    )
    return jax.shard_map(
        functools.partial(on_device, mesh.shape["op"]),
        mesh=mesh,
        in_specs=placed,
        out_specs=P("group", "sec", "op", None),
        check_vma=False,
    )
```

```python
import functools

import jax
import jax.numpy as jnp
from jax import lax
from jax.experimental import pallas as pl
from jax.experimental.pallas import tpu as pltpu
from jax.sharding import PartitionSpec as P

HBM = pl.BlockSpec(memory_space=pltpu.HBM)
SMEM = pl.BlockSpec(memory_space=pltpu.SMEM)
VMEM = pl.BlockSpec(memory_space=pltpu.VMEM)


def slot_kernel(step, parts, choices, source, *refs):
    count = len(parts)
    lefts, psis = [], []
    for number, _ in parts:
        lefts.append(refs[:number])
        refs = refs[number:]
    for _, number in parts:
        psis.append(refs[:number])
        refs = refs[number:]
    rights = refs[:choices]
    out, mid_buf, right_buf = refs[choices:]
    terms, _, rows, columns = rights[0].shape
    me = lax.axis_index("sec")
    row = me >> 2
    q = me ^ (4 * step)
    outer = (row == 0) | (row == 3)

    def psi_block(held, sector):
        if len(held) == 1:
            return held[0][0, sector]
        low, high = held
        size = low.shape[1]
        return jnp.where(
            sector < size, low[0, jnp.minimum(sector, size - 1)], high[0, jnp.maximum(sector - size, 0)]
        )

    def left_block(held, k):
        for part in held:
            if k < part.shape[0]:
                return part[k, 0]
            k -= part.shape[0]

    for k in range(terms):
        span = pl.ds(k * columns, columns)
        right = rights[0][k, 0]
        if choices > 1:
            right = jnp.where(outer, right, rights[1][k, 0])
        right_buf[:, span] = right
        for i in range(count):
            mid = jnp.dot(
                left_block(lefts[i], k), psi_block(psis[i], source[k, q]), preferred_element_type=jnp.float32
            )
            mid_buf[pl.ds(i * rows, rows), span] = mid.astype(jnp.bfloat16)
    second_product(mid_buf, right_buf, out)


def second_product(mid, right, out):
    total = lax.dot_general(mid[...], right[...], (((1,), (1,)), ((), ())), preferred_element_type=jnp.float32)
    out[...] = total.reshape(out.shape).astype(out.dtype)


def second_kernel(*refs):
    *mids, right, out, right_buf = refs
    terms, _, _, columns = right.shape
    for k in range(terms):
        right_buf[:, pl.ds(k * columns, columns)] = right[k, 0]
    size = out.shape[0] // len(mids)
    for i, mid in enumerate(mids):
        second_product(mid, right_buf, out.at[pl.ds(i * size, size)])


def second(mids, right, dtype, flops):
    terms, _, rows, columns = right.shape
    return pl.pallas_call(
        second_kernel,
        out_shape=jax.ShapeDtypeStruct((sum(mid.shape[0] for mid in mids) // rows, rows, columns), dtype),
        in_specs=[VMEM] * (len(mids) + 1),
        out_specs=VMEM,
        scratch_shapes=[pltpu.VMEM((rows, terms * columns), jnp.bfloat16)],
        compiler_params=pltpu.CompilerParams(vmem_limit_bytes=16 << 20),
        cost_estimate=pl.CostEstimate(flops=flops, bytes_accessed=1, transcendentals=0),
    )(*mids, right)


def slot(step, source_map, lefts, psis, rights, dtype, flops, keep_mid):
    terms, _, rows, columns = rights[0].shape
    count = len(psis)
    parts = tuple((len(left), len(psi)) for left, psi in zip(lefts, psis))
    held = [part for left in lefts for part in left] + [part for psi in psis for part in psi] + list(rights)
    out = jax.ShapeDtypeStruct((count, rows, columns), dtype)
    mid = jax.ShapeDtypeStruct((count * rows, terms * columns), jnp.bfloat16)
    scratch = [pltpu.VMEM((rows, terms * columns), jnp.bfloat16)]
    if not keep_mid:
        scratch = [pltpu.VMEM(mid.shape, mid.dtype)] + scratch
    return pl.pallas_call(
        functools.partial(slot_kernel, step, parts, len(rights)),
        out_shape=(out, mid) if keep_mid else out,
        in_specs=[SMEM] + [VMEM] * len(held),
        out_specs=(VMEM, VMEM) if keep_mid else VMEM,
        scratch_shapes=scratch,
        compiler_params=pltpu.CompilerParams(vmem_limit_bytes=24 << 20),
        cost_estimate=pl.CostEstimate(flops=flops, bytes_accessed=1, transcendentals=0),
    )(source_map, *held)


def split_kernel(axis, whole, low, high):
    first = low.shape[axis]
    before = (slice(None),) * axis
    low[...] = whole[(*before, slice(0, first))]
    high[...] = whole[(*before, slice(first, None))]


def split(array, axis, first):
    def part(size):
        shape = array.shape[:axis] + (size,) + array.shape[axis + 1 :]
        return jax.ShapeDtypeStruct(shape, array.dtype)

    return pl.pallas_call(
        functools.partial(split_kernel, axis),
        out_shape=(part(first), part(array.shape[axis] - first)),
        in_specs=[VMEM],
        out_specs=(VMEM, VMEM),
        compiler_params=pltpu.CompilerParams(vmem_limit_bytes=12 << 20),
        cost_estimate=pl.CostEstimate(flops=1, bytes_accessed=1, transcendentals=0),
    )(array)


def place_kernel(starts, chosen, *refs):
    *pieces, out, sem = refs
    pieces = pieces[-len(starts) :]
    me = lax.axis_index("sec")
    row = me >> 2
    outer = (row == 0) | (row == 3)

    def copies(chosen_pieces):
        return [
            pltpu.make_async_copy(piece.at[i], out.at[me ^ (start + i)], sem.at[start + i])
            for start, piece in chosen_pieces
            for i in range(piece.shape[0])
        ]

    held = list(zip(starts, pieces))
    if chosen:

        @pl.when(outer)
        def _():
            for copy in copies(held[:1]):
                copy.start()

        @pl.when(jnp.logical_not(outer))
        def _():
            for copy in copies(held[1:]):
                copy.start()

        held = held[:1]
    else:
        for copy in copies(held):
            copy.start()
    for copy in copies(held):
        copy.wait()


def place(sectors, held, out=None, flops=1):
    starts, pieces = zip(*held)
    before = [] if out is None else [out]
    return pl.pallas_call(
        functools.partial(place_kernel, starts, out is not None),
        out_shape=jax.ShapeDtypeStruct((sectors,) + pieces[0].shape[1:], pieces[0].dtype),
        in_specs=[HBM] * len(before) + [VMEM] * len(pieces),
        out_specs=HBM,
        scratch_shapes=[pltpu.SemaphoreType.DMA((sectors,))],
        input_output_aliases={} if out is None else {0: 0},
        compiler_params=pltpu.CompilerParams(vmem_limit_bytes=16 << 20),
        cost_estimate=pl.CostEstimate(flops=flops, bytes_accessed=1, transcendentals=0),
    )(*before, *pieces)


def exchange(array, bits, members):
    return lax.ppermute(array, "sec", [(s, s ^ bits) for s in members])


def on_device(ops, psi, left_env, right_env, source_map):
    dtype = jnp.bfloat16 if ops == 1 else jnp.float32
    every = range(16)
    inner = range(4, 12)
    outer = [s for s in every if s not in inner]

    def products(step, lefts, psis, rights, flops=1, keep_mid=False):
        return slot(step, source_map, lefts, psis, rights, dtype, flops, keep_mid)

    near = exchange(right_env, 4, every)
    middle = exchange(right_env, 12, inner)
    x_psi = exchange(psi, 2, every)
    own = ([(left_env,), (exchange(left_env, 1, every),)], [(psi,), (exchange(psi, 1, every),)])
    own_0 = products(0, *own, (right_env,))

    near, middle, own_0 = lax.optimization_barrier((near, middle, own_0))
    far_in = exchange(near, 12, inner)
    far_out = exchange(middle, 4, inner)

    own_middle, own_mid = products(3, *own, (middle,), keep_mid=True)
    own_1 = products(1, *own, (near,))
    x_psi, left_next, own_1, own_middle = lax.optimization_barrier((x_psi, left_env, own_1, own_middle))
    x_left = exchange(left_next, 2, every)
    across_psi = [exchange(part, 1, every) for part in split(x_psi, 1, 9 * x_psi.shape[1] // 16)]
    sent_1 = exchange(own_1, 4, every)
    sent_own_middle = exchange(own_middle, 12, inner)

    far_out, far_in = lax.optimization_barrier((far_out, far_in))
    third = exchange(far_in, 4, inner)
    own_2 = products(2, *own, (far_out, far_in))
    own_2, sent_1, sent_own_middle = lax.optimization_barrier((own_2, sent_1, sent_own_middle))
    sent_2 = exchange(own_2, 8, every)

    x_left, sent_2 = lax.optimization_barrier((x_left, sent_2))
    across_left = [exchange(part, 1, every) for part in split(x_left, 0, 5 * x_left.shape[0] // 8)]
    other = ([(x_left,), across_left], [(x_psi,), across_psi])
    other_middle, other_mid = products(3, *other, (middle,), keep_mid=True)
    sent_other_middle = exchange(other_middle, 12, inner)
    other_0 = products(0, *other, (right_env,))
    far_out, other_middle, other_0 = lax.optimization_barrier((far_out, other_middle, other_0))
    other_2 = products(2, *other, (far_out, far_in))
    other_sent_2 = exchange(other_2, 8, every)
    other_1 = products(1, *other, (near,))
    other_sent_1 = exchange(other_1, 4, every)

    third, other_1, other_2, other_middle = lax.optimization_barrier((third, other_1, other_2, other_middle))
    last_third = second((own_mid, other_mid), third, dtype, 10**10)
    sent_third = exchange(last_third, 12, outer)

    held = [(0, own_0), (2, other_0), (8, sent_2), (10, other_sent_2), (4, sent_1), (6, other_sent_1)]
    out = place(16, held, flops=10**10)
    out = place(16, [(12, sent_third), (12, sent_own_middle), (14, sent_other_middle)], out)[:, None]
    if ops > 1:
        out = lax.psum_scatter(out, "op", scatter_dimension=2, tiled=True).astype(jnp.bfloat16)
    return out


def solution(mesh):
    placed = (
        P(("group", "sec"), None, None, None),
        P(("group", "op"), "sec", None, None),
        P(("group", "op"), "sec", None, None),
        P(("group", "op"), None),
    )
    return jax.shard_map(
        functools.partial(on_device, mesh.shape["op"]),
        mesh=mesh,
        in_specs=placed,
        out_specs=P("group", "sec", "op", None),
        check_vma=False,
    )
```

```python
import functools

import jax
import jax.numpy as jnp
from jax import lax
from jax.experimental import pallas as pl
from jax.experimental.pallas import tpu as pltpu
from jax.sharding import PartitionSpec as P

HBM = pl.BlockSpec(memory_space=pltpu.HBM)
SMEM = pl.BlockSpec(memory_space=pltpu.SMEM)
VMEM = pl.BlockSpec(memory_space=pltpu.VMEM)


def slot_kernel(step, parts, choices, source, *refs):
    count = len(parts)
    lefts, psis = [], []
    for number, _ in parts:
        lefts.append(refs[:number])
        refs = refs[number:]
    for _, number in parts:
        psis.append(refs[:number])
        refs = refs[number:]
    rights = refs[:choices]
    out, mid_buf, right_buf = refs[choices:]
    terms, _, rows, columns = rights[0].shape
    me = lax.axis_index("sec")
    row = me >> 2
    q = me ^ (4 * step)
    outer = (row == 0) | (row == 3)

    def psi_block(held, sector):
        if len(held) == 1:
            return held[0][0, sector]
        low, high = held
        size = low.shape[1]
        return jnp.where(
            sector < size, low[0, jnp.minimum(sector, size - 1)], high[0, jnp.maximum(sector - size, 0)]
        )

    def left_block(held, k):
        for part in held:
            if k < part.shape[0]:
                return part[k, 0]
            k -= part.shape[0]

    for k in range(terms):
        span = pl.ds(k * columns, columns)
        right = rights[0][k, 0]
        if choices > 1:
            right = jnp.where(outer, right, rights[1][k, 0])
        right_buf[:, span] = right
        for i in range(count):
            mid = jnp.dot(
                left_block(lefts[i], k), psi_block(psis[i], source[k, q]), preferred_element_type=jnp.float32
            )
            mid_buf[pl.ds(i * rows, rows), span] = mid.astype(jnp.bfloat16)
    second_product(mid_buf, right_buf, out)


def second_product(mid, right, out):
    total = lax.dot_general(mid[...], right[...], (((1,), (1,)), ((), ())), preferred_element_type=jnp.float32)
    out[...] = total.reshape(out.shape).astype(out.dtype)


def second_kernel(*refs):
    *mids, right, out, right_buf = refs
    terms, _, _, columns = right.shape
    for k in range(terms):
        right_buf[:, pl.ds(k * columns, columns)] = right[k, 0]
    size = out.shape[0] // len(mids)
    for i, mid in enumerate(mids):
        second_product(mid, right_buf, out.at[pl.ds(i * size, size)])


def second(mids, right, dtype, flops):
    terms, _, rows, columns = right.shape
    return pl.pallas_call(
        second_kernel,
        out_shape=jax.ShapeDtypeStruct((sum(mid.shape[0] for mid in mids) // rows, rows, columns), dtype),
        in_specs=[VMEM] * (len(mids) + 1),
        out_specs=VMEM,
        scratch_shapes=[pltpu.VMEM((rows, terms * columns), jnp.bfloat16)],
        compiler_params=pltpu.CompilerParams(vmem_limit_bytes=16 << 20),
        cost_estimate=pl.CostEstimate(flops=flops, bytes_accessed=1, transcendentals=0),
    )(*mids, right)


def slot(step, source_map, lefts, psis, rights, dtype, flops, keep_mid):
    terms, _, rows, columns = rights[0].shape
    count = len(psis)
    parts = tuple((len(left), len(psi)) for left, psi in zip(lefts, psis))
    held = [part for left in lefts for part in left] + [part for psi in psis for part in psi] + list(rights)
    out = jax.ShapeDtypeStruct((count, rows, columns), dtype)
    mid = jax.ShapeDtypeStruct((count * rows, terms * columns), jnp.bfloat16)
    scratch = [pltpu.VMEM((rows, terms * columns), jnp.bfloat16)]
    if not keep_mid:
        scratch = [pltpu.VMEM(mid.shape, mid.dtype)] + scratch
    return pl.pallas_call(
        functools.partial(slot_kernel, step, parts, len(rights)),
        out_shape=(out, mid) if keep_mid else out,
        in_specs=[SMEM] + [VMEM] * len(held),
        out_specs=(VMEM, VMEM) if keep_mid else VMEM,
        scratch_shapes=scratch,
        compiler_params=pltpu.CompilerParams(vmem_limit_bytes=24 << 20),
        cost_estimate=pl.CostEstimate(flops=flops, bytes_accessed=1, transcendentals=0),
    )(source_map, *held)


def split_kernel(axis, whole, low, high):
    first = low.shape[axis]
    before = (slice(None),) * axis
    low[...] = whole[(*before, slice(0, first))]
    high[...] = whole[(*before, slice(first, None))]


def split(array, axis, first):
    def part(size):
        shape = array.shape[:axis] + (size,) + array.shape[axis + 1 :]
        return jax.ShapeDtypeStruct(shape, array.dtype)

    return pl.pallas_call(
        functools.partial(split_kernel, axis),
        out_shape=(part(first), part(array.shape[axis] - first)),
        in_specs=[VMEM],
        out_specs=(VMEM, VMEM),
        compiler_params=pltpu.CompilerParams(vmem_limit_bytes=12 << 20),
        cost_estimate=pl.CostEstimate(flops=1, bytes_accessed=1, transcendentals=0),
    )(array)


def place_kernel(starts, shared, *refs):
    *pieces, out, sem = refs
    pieces = pieces[-len(starts) :]
    me = lax.axis_index("sec")
    row = me >> 2
    outer = (row == 0) | (row == 3)

    def copies(held):
        return [
            pltpu.make_async_copy(piece.at[i], out.at[me ^ (start + i)], sem.at[start + i])
            for start, piece in held
            for i in range(piece.shape[0])
        ]

    held = list(zip(starts, pieces))
    for copy in copies(held[:shared]):
        copy.start()
    if shared < len(held):

        @pl.when(outer)
        def _():
            for copy in copies(held[shared : shared + 1]):
                copy.start()

        @pl.when(jnp.logical_not(outer))
        def _():
            for copy in copies(held[shared + 1 :]):
                copy.start()

    for copy in copies(held[: shared + 1]):
        copy.wait()


def place(sectors, held, out=None, shared=None, flops=1):
    starts, pieces = zip(*held)
    before = [] if out is None else [out]
    return pl.pallas_call(
        functools.partial(place_kernel, starts, len(held) if shared is None else shared),
        out_shape=jax.ShapeDtypeStruct((sectors,) + pieces[0].shape[1:], pieces[0].dtype),
        in_specs=[HBM] * len(before) + [VMEM] * len(pieces),
        out_specs=HBM,
        scratch_shapes=[pltpu.SemaphoreType.DMA((sectors,))],
        input_output_aliases={} if out is None else {0: 0},
        compiler_params=pltpu.CompilerParams(vmem_limit_bytes=16 << 20),
        cost_estimate=pl.CostEstimate(flops=flops, bytes_accessed=1, transcendentals=0),
    )(*before, *pieces)


def exchange(array, bits, members):
    return lax.ppermute(array, "sec", [(s, s ^ bits) for s in members])


def on_device(ops, psi, left_env, right_env, source_map):
    dtype = jnp.bfloat16 if ops == 1 else jnp.float32
    every = range(16)
    inner = range(4, 12)
    outer = [s for s in every if s not in inner]

    def products(step, lefts, psis, rights, flops=1, keep_mid=False):
        return slot(step, source_map, lefts, psis, rights, dtype, flops, keep_mid)

    near = exchange(right_env, 4, every)
    middle = exchange(right_env, 12, inner)
    x_psi = exchange(psi, 2, every)
    own = ([(left_env,), (exchange(left_env, 1, every),)], [(psi,), (exchange(psi, 1, every),)])
    own_0 = products(0, *own, (right_env,))

    near, middle, own_0 = lax.optimization_barrier((near, middle, own_0))
    far_in = exchange(near, 12, inner)
    far_out = exchange(middle, 4, inner)

    own_middle, own_mid = products(3, *own, (middle,), keep_mid=True)
    own_1 = products(1, *own, (near,))
    x_psi, left_next, own_1, own_middle = lax.optimization_barrier((x_psi, left_env, own_1, own_middle))
    x_left = exchange(left_next, 2, every)
    across_psi = [exchange(part, 1, every) for part in split(x_psi, 1, 9 * x_psi.shape[1] // 16)]
    sent_1 = exchange(own_1, 4, every)
    sent_own_middle = exchange(own_middle, 12, inner)

    far_out, far_in = lax.optimization_barrier((far_out, far_in))
    third = exchange(far_in, 4, inner)
    own_2 = products(2, *own, (far_out, far_in))
    own_2, sent_1, sent_own_middle = lax.optimization_barrier((own_2, sent_1, sent_own_middle))
    sent_2 = exchange(own_2, 8, every)

    x_left, sent_2 = lax.optimization_barrier((x_left, sent_2))
    across_left = [exchange(part, 1, every) for part in split(x_left, 0, 5 * x_left.shape[0] // 8)]
    other = ([(x_left,), across_left], [(x_psi,), across_psi])
    other_middle, other_mid = products(3, *other, (middle,), keep_mid=True)
    sent_other_middle = exchange(other_middle, 12, inner)
    far_out, other_middle = lax.optimization_barrier((far_out, other_middle))
    other_2 = products(2, *other, (far_out, far_in))
    other_sent_2 = exchange(other_2, 8, every)
    other_1 = products(1, *other, (near,))
    other_sent_1 = exchange(other_1, 4, every)

    third, other_1, other_2, other_middle = lax.optimization_barrier((third, other_1, other_2, other_middle))
    last_third = second((own_mid, other_mid), third, dtype, 10**10)
    sent_third = exchange(last_third, 12, outer)
    right_last, last_third = lax.optimization_barrier((right_env, last_third))
    other_0 = products(0, *other, (right_last,))

    out = place(16, [(0, own_0), (2, other_0), (4, sent_1), (8, sent_2)], flops=10**10)
    last = [(12, sent_third), (12, sent_own_middle), (14, sent_other_middle)]
    out = place(16, [(10, other_sent_2), (6, other_sent_1)] + last, out, 2)[:, None]
    if ops > 1:
        out = lax.psum_scatter(out, "op", scatter_dimension=2, tiled=True).astype(jnp.bfloat16)
    return out


def solution(mesh):
    placed = (
        P(("group", "sec"), None, None, None),
        P(("group", "op"), "sec", None, None),
        P(("group", "op"), "sec", None, None),
        P(("group", "op"), None),
    )
    return jax.shard_map(
        functools.partial(on_device, mesh.shape["op"]),
        mesh=mesh,
        in_specs=placed,
        out_specs=P("group", "sec", "op", None),
        check_vma=False,
    )
```

```python
import functools

import jax
import jax.numpy as jnp
from jax import lax
from jax.experimental import pallas as pl
from jax.experimental.pallas import tpu as pltpu
from jax.sharding import PartitionSpec as P

HBM = pl.BlockSpec(memory_space=pltpu.HBM)
SMEM = pl.BlockSpec(memory_space=pltpu.SMEM)
VMEM = pl.BlockSpec(memory_space=pltpu.VMEM)


def slot_kernel(step, parts, choices, source, *refs):
    count = len(parts)
    lefts, psis = [], []
    for number, _ in parts:
        lefts.append(refs[:number])
        refs = refs[number:]
    for _, number in parts:
        psis.append(refs[:number])
        refs = refs[number:]
    rights = refs[:choices]
    out, mid_buf, right_buf = refs[choices:]
    terms, _, rows, columns = rights[0].shape
    me = lax.axis_index("sec")
    row = me >> 2
    q = me ^ (4 * step)
    outer = (row == 0) | (row == 3)

    def psi_block(held, sector):
        if len(held) == 1:
            return held[0][0, sector]
        low, high = held
        size = low.shape[1]
        return jnp.where(
            sector < size, low[0, jnp.minimum(sector, size - 1)], high[0, jnp.maximum(sector - size, 0)]
        )

    def left_block(held, k):
        for part in held:
            if k < part.shape[0]:
                return part[k, 0]
            k -= part.shape[0]

    for k in range(terms):
        span = pl.ds(k * columns, columns)
        right = rights[0][k, 0]
        if choices > 1:
            right = jnp.where(outer, right, rights[1][k, 0])
        right_buf[:, span] = right
        for i in range(count):
            mid = jnp.dot(
                left_block(lefts[i], k), psi_block(psis[i], source[k, q]), preferred_element_type=jnp.float32
            )
            mid_buf[pl.ds(i * rows, rows), span] = mid.astype(jnp.bfloat16)
    second_product(mid_buf, right_buf, out)


def second_product(mid, right, out):
    total = lax.dot_general(mid[...], right[...], (((1,), (1,)), ((), ())), preferred_element_type=jnp.float32)
    out[...] = total.reshape(out.shape).astype(out.dtype)


def second_kernel(*refs):
    *mids, right, out, right_buf = refs
    terms, _, _, columns = right.shape
    for k in range(terms):
        right_buf[:, pl.ds(k * columns, columns)] = right[k, 0]
    size = out.shape[0] // len(mids)
    for i, mid in enumerate(mids):
        second_product(mid, right_buf, out.at[pl.ds(i * size, size)])


def second(mids, right, dtype, flops):
    terms, _, rows, columns = right.shape
    return pl.pallas_call(
        second_kernel,
        out_shape=jax.ShapeDtypeStruct((sum(mid.shape[0] for mid in mids) // rows, rows, columns), dtype),
        in_specs=[VMEM] * (len(mids) + 1),
        out_specs=VMEM,
        scratch_shapes=[pltpu.VMEM((rows, terms * columns), jnp.bfloat16)],
        compiler_params=pltpu.CompilerParams(vmem_limit_bytes=16 << 20),
        cost_estimate=pl.CostEstimate(flops=flops, bytes_accessed=1, transcendentals=0),
    )(*mids, right)


def slot(step, source_map, lefts, psis, rights, dtype, flops, keep_mid):
    terms, _, rows, columns = rights[0].shape
    count = len(psis)
    parts = tuple((len(left), len(psi)) for left, psi in zip(lefts, psis))
    held = [part for left in lefts for part in left] + [part for psi in psis for part in psi] + list(rights)
    out = jax.ShapeDtypeStruct((count, rows, columns), dtype)
    mid = jax.ShapeDtypeStruct((count * rows, terms * columns), jnp.bfloat16)
    scratch = [pltpu.VMEM((rows, terms * columns), jnp.bfloat16)]
    if not keep_mid:
        scratch = [pltpu.VMEM(mid.shape, mid.dtype)] + scratch
    return pl.pallas_call(
        functools.partial(slot_kernel, step, parts, len(rights)),
        out_shape=(out, mid) if keep_mid else out,
        in_specs=[SMEM] + [VMEM] * len(held),
        out_specs=(VMEM, VMEM) if keep_mid else VMEM,
        scratch_shapes=scratch,
        compiler_params=pltpu.CompilerParams(vmem_limit_bytes=24 << 20),
        cost_estimate=pl.CostEstimate(flops=flops, bytes_accessed=1, transcendentals=0),
    )(source_map, *held)


def split_kernel(axis, whole, low, high):
    first = low.shape[axis]
    before = (slice(None),) * axis
    low[...] = whole[(*before, slice(0, first))]
    high[...] = whole[(*before, slice(first, None))]


def split(array, axis, first):
    def part(size):
        shape = array.shape[:axis] + (size,) + array.shape[axis + 1 :]
        return jax.ShapeDtypeStruct(shape, array.dtype)

    return pl.pallas_call(
        functools.partial(split_kernel, axis),
        out_shape=(part(first), part(array.shape[axis] - first)),
        in_specs=[VMEM],
        out_specs=(VMEM, VMEM),
        compiler_params=pltpu.CompilerParams(vmem_limit_bytes=12 << 20),
        cost_estimate=pl.CostEstimate(flops=1, bytes_accessed=1, transcendentals=0),
    )(array)


def place_kernel(starts, shared, *refs):
    *pieces, out, sem = refs
    pieces = pieces[-len(starts) :]
    me = lax.axis_index("sec")
    row = me >> 2
    outer = (row == 0) | (row == 3)

    def copies(held):
        return [
            pltpu.make_async_copy(piece.at[i], out.at[me ^ (start + i)], sem.at[start + i])
            for start, piece in held
            for i in range(piece.shape[0])
        ]

    held = list(zip(starts, pieces))
    for copy in copies(held[:shared]):
        copy.start()
    if shared < len(held):

        @pl.when(outer)
        def _():
            for copy in copies(held[shared : shared + 1]):
                copy.start()

        @pl.when(jnp.logical_not(outer))
        def _():
            for copy in copies(held[shared + 1 :]):
                copy.start()

    for copy in copies(held[: shared + 1]):
        copy.wait()


def place(sectors, held, out=None, shared=None, flops=1):
    starts, pieces = zip(*held)
    before = [] if out is None else [out]
    return pl.pallas_call(
        functools.partial(place_kernel, starts, len(held) if shared is None else shared),
        out_shape=jax.ShapeDtypeStruct((sectors,) + pieces[0].shape[1:], pieces[0].dtype),
        in_specs=[HBM] * len(before) + [VMEM] * len(pieces),
        out_specs=HBM,
        scratch_shapes=[pltpu.SemaphoreType.DMA((sectors,))],
        input_output_aliases={} if out is None else {0: 0},
        compiler_params=pltpu.CompilerParams(vmem_limit_bytes=16 << 20),
        cost_estimate=pl.CostEstimate(flops=flops, bytes_accessed=1, transcendentals=0),
    )(*before, *pieces)


def exchange(array, bits, members):
    return lax.ppermute(array, "sec", [(s, s ^ bits) for s in members])


def on_device(ops, psi, left_env, right_env, source_map):
    dtype = jnp.bfloat16 if ops == 1 else jnp.float32
    every = range(16)
    inner = range(4, 12)
    outer = [s for s in every if s not in inner]

    def products(step, lefts, psis, rights, flops=1, keep_mid=False):
        return slot(step, source_map, lefts, psis, rights, dtype, flops, keep_mid)

    near = exchange(right_env, 4, every)
    middle = exchange(right_env, 12, inner)
    x_psi = exchange(psi, 2, every)
    own = ([(left_env,), (exchange(left_env, 1, every),)], [(psi,), (exchange(psi, 1, every),)])
    own_0 = products(0, *own, (right_env,), flops=2 * 10**10)

    near, middle, own_0 = lax.optimization_barrier((near, middle, own_0))
    far_in = exchange(near, 12, inner)
    far_out = exchange(middle, 4, inner)

    own_middle, own_mid = products(3, *own, (middle,), keep_mid=True)
    own_1 = products(1, *own, (near,))
    x_psi, left_next, own_1, own_middle = lax.optimization_barrier((x_psi, left_env, own_1, own_middle))
    x_left = exchange(left_next, 2, every)
    across_psi = [exchange(part, 1, every) for part in split(x_psi, 1, 9 * x_psi.shape[1] // 16)]
    sent_1 = exchange(own_1, 4, every)
    sent_own_middle = exchange(own_middle, 12, inner)

    far_out, far_in = lax.optimization_barrier((far_out, far_in))
    third = exchange(far_in, 4, inner)
    own_2 = products(2, *own, (far_out, far_in))
    own_2, sent_1, sent_own_middle = lax.optimization_barrier((own_2, sent_1, sent_own_middle))
    sent_2 = exchange(own_2, 8, every)

    x_left, sent_2 = lax.optimization_barrier((x_left, sent_2))
    across_left = [exchange(part, 1, every) for part in split(x_left, 0, 5 * x_left.shape[0] // 8)]
    other = ([(x_left,), across_left], [(x_psi,), across_psi])
    other_middle, other_mid = products(3, *other, (middle,), keep_mid=True)
    sent_other_middle = exchange(other_middle, 12, inner)
    far_out, other_middle = lax.optimization_barrier((far_out, other_middle))
    other_2 = products(2, *other, (far_out, far_in))
    other_sent_2 = exchange(other_2, 8, every)
    other_1 = products(1, *other, (near,))
    other_sent_1 = exchange(other_1, 4, every)

    third, other_1, other_2, other_middle = lax.optimization_barrier((third, other_1, other_2, other_middle))
    last_third = second((own_mid, other_mid), third, dtype, 10**10)
    sent_third = exchange(last_third, 12, outer)
    right_last, last_third = lax.optimization_barrier((right_env, last_third))
    other_0 = products(0, *other, (right_last,))

    out = place(16, [(0, own_0), (2, other_0), (4, sent_1), (8, sent_2)], flops=10**10)
    last = [(12, sent_third), (12, sent_own_middle), (14, sent_other_middle)]
    out = place(16, [(10, other_sent_2), (6, other_sent_1)] + last, out, 2)[:, None]
    if ops > 1:
        out = lax.psum_scatter(out, "op", scatter_dimension=2, tiled=True).astype(jnp.bfloat16)
    return out


def solution(mesh):
    placed = (
        P(("group", "sec"), None, None, None),
        P(("group", "op"), "sec", None, None),
        P(("group", "op"), "sec", None, None),
        P(("group", "op"), None),
    )
    return jax.shard_map(
        functools.partial(on_device, mesh.shape["op"]),
        mesh=mesh,
        in_specs=placed,
        out_specs=P("group", "sec", "op", None),
        check_vma=False,
    )
```

```python
import functools

import jax
import jax.numpy as jnp
from jax import lax
from jax.experimental import pallas as pl
from jax.experimental.pallas import tpu as pltpu
from jax.sharding import PartitionSpec as P

HBM = pl.BlockSpec(memory_space=pltpu.HBM)
SMEM = pl.BlockSpec(memory_space=pltpu.SMEM)
VMEM = pl.BlockSpec(memory_space=pltpu.VMEM)


def slot_kernel(step, parts, choices, source, *refs):
    count = len(parts)
    lefts, psis = [], []
    for number, _ in parts:
        lefts.append(refs[:number])
        refs = refs[number:]
    for _, number in parts:
        psis.append(refs[:number])
        refs = refs[number:]
    rights = refs[:choices]
    out, mid_buf, right_buf = refs[choices:]
    terms, _, rows, columns = rights[0].shape
    me = lax.axis_index("sec")
    row = me >> 2
    q = me ^ (4 * step)
    outer = (row == 0) | (row == 3)

    def psi_block(held, sector):
        if len(held) == 1:
            return held[0][0, sector]
        low, high = held
        size = low.shape[1]
        return jnp.where(
            sector < size, low[0, jnp.minimum(sector, size - 1)], high[0, jnp.maximum(sector - size, 0)]
        )

    def left_block(held, k):
        for part in held:
            if k < part.shape[0]:
                return part[k, 0]
            k -= part.shape[0]

    for k in range(terms):
        span = pl.ds(k * columns, columns)
        right = rights[0][k, 0]
        if choices > 1:
            right = jnp.where(outer, right, rights[1][k, 0])
        right_buf[:, span] = right
        for i in range(count):
            mid = jnp.dot(
                left_block(lefts[i], k), psi_block(psis[i], source[k, q]), preferred_element_type=jnp.float32
            )
            mid_buf[pl.ds(i * rows, rows), span] = mid.astype(jnp.bfloat16)
    second_product(mid_buf, right_buf, out)


def second_product(mid, right, out):
    total = lax.dot_general(mid[...], right[...], (((1,), (1,)), ((), ())), preferred_element_type=jnp.float32)
    out[...] = total.reshape(out.shape).astype(out.dtype)


def second_kernel(*refs):
    *mids, right, out, right_buf = refs
    terms, _, _, columns = right.shape
    for k in range(terms):
        right_buf[:, pl.ds(k * columns, columns)] = right[k, 0]
    size = out.shape[0] // len(mids)
    for i, mid in enumerate(mids):
        second_product(mid, right_buf, out.at[pl.ds(i * size, size)])


def second(mids, right, dtype, flops):
    terms, _, rows, columns = right.shape
    return pl.pallas_call(
        second_kernel,
        out_shape=jax.ShapeDtypeStruct((sum(mid.shape[0] for mid in mids) // rows, rows, columns), dtype),
        in_specs=[VMEM] * (len(mids) + 1),
        out_specs=VMEM,
        scratch_shapes=[pltpu.VMEM((rows, terms * columns), jnp.bfloat16)],
        compiler_params=pltpu.CompilerParams(vmem_limit_bytes=16 << 20),
        cost_estimate=pl.CostEstimate(flops=flops, bytes_accessed=1, transcendentals=0),
    )(*mids, right)


def slot(step, source_map, lefts, psis, rights, dtype, flops, keep_mid):
    terms, _, rows, columns = rights[0].shape
    count = len(psis)
    parts = tuple((len(left), len(psi)) for left, psi in zip(lefts, psis))
    held = [part for left in lefts for part in left] + [part for psi in psis for part in psi] + list(rights)
    out = jax.ShapeDtypeStruct((count, rows, columns), dtype)
    mid = jax.ShapeDtypeStruct((count * rows, terms * columns), jnp.bfloat16)
    scratch = [pltpu.VMEM((rows, terms * columns), jnp.bfloat16)]
    if not keep_mid:
        scratch = [pltpu.VMEM(mid.shape, mid.dtype)] + scratch
    return pl.pallas_call(
        functools.partial(slot_kernel, step, parts, len(rights)),
        out_shape=(out, mid) if keep_mid else out,
        in_specs=[SMEM] + [VMEM] * len(held),
        out_specs=(VMEM, VMEM) if keep_mid else VMEM,
        scratch_shapes=scratch,
        compiler_params=pltpu.CompilerParams(vmem_limit_bytes=24 << 20),
        cost_estimate=pl.CostEstimate(flops=flops, bytes_accessed=1, transcendentals=0),
    )(source_map, *held)


def split_kernel(axis, whole, low, high):
    first = low.shape[axis]
    before = (slice(None),) * axis
    low[...] = whole[(*before, slice(0, first))]
    high[...] = whole[(*before, slice(first, None))]


def split(array, axis, first):
    def part(size):
        shape = array.shape[:axis] + (size,) + array.shape[axis + 1 :]
        return jax.ShapeDtypeStruct(shape, array.dtype)

    return pl.pallas_call(
        functools.partial(split_kernel, axis),
        out_shape=(part(first), part(array.shape[axis] - first)),
        in_specs=[VMEM],
        out_specs=(VMEM, VMEM),
        compiler_params=pltpu.CompilerParams(vmem_limit_bytes=12 << 20),
        cost_estimate=pl.CostEstimate(flops=1, bytes_accessed=1, transcendentals=0),
    )(array)


def place_kernel(starts, shared, *refs):
    *pieces, out, sem = refs
    pieces = pieces[-len(starts) :]
    me = lax.axis_index("sec")
    row = me >> 2
    outer = (row == 0) | (row == 3)

    def copies(held):
        return [
            pltpu.make_async_copy(piece.at[i], out.at[me ^ (start + i)], sem.at[start + i])
            for start, piece in held
            for i in range(piece.shape[0])
        ]

    held = list(zip(starts, pieces))
    for copy in copies(held[:shared]):
        copy.start()
    if shared < len(held):

        @pl.when(outer)
        def _():
            for copy in copies(held[shared : shared + 1]):
                copy.start()

        @pl.when(jnp.logical_not(outer))
        def _():
            for copy in copies(held[shared + 1 :]):
                copy.start()

    for copy in copies(held[: shared + 1]):
        copy.wait()


def place(sectors, held, out=None, shared=None, flops=1):
    starts, pieces = zip(*held)
    before = [] if out is None else [out]
    return pl.pallas_call(
        functools.partial(place_kernel, starts, len(held) if shared is None else shared),
        out_shape=jax.ShapeDtypeStruct((sectors,) + pieces[0].shape[1:], pieces[0].dtype),
        in_specs=[HBM] * len(before) + [VMEM] * len(pieces),
        out_specs=HBM,
        scratch_shapes=[pltpu.SemaphoreType.DMA((sectors,))],
        input_output_aliases={} if out is None else {0: 0},
        compiler_params=pltpu.CompilerParams(vmem_limit_bytes=16 << 20),
        cost_estimate=pl.CostEstimate(flops=flops, bytes_accessed=1, transcendentals=0),
    )(*before, *pieces)


def exchange(array, bits, members):
    return lax.ppermute(array, "sec", [(s, s ^ bits) for s in members])


def on_device(ops, psi, left_env, right_env, source_map):
    dtype = jnp.bfloat16 if ops == 1 else jnp.float32
    every = range(16)
    inner = range(4, 12)
    outer = [s for s in every if s not in inner]

    def products(step, lefts, psis, rights, flops=1, keep_mid=False):
        return slot(step, source_map, lefts, psis, rights, dtype, flops, keep_mid)

    near = exchange(right_env, 4, every)
    middle = exchange(right_env, 12, inner)
    x_psi = exchange(psi, 2, every)
    own = ([(left_env,), (exchange(left_env, 1, every),)], [(psi,), (exchange(psi, 1, every),)])
    own_0 = products(0, *own, (right_env,), flops=2 * 10**10)

    near, middle, own_0 = lax.optimization_barrier((near, middle, own_0))
    far_in = exchange(near, 12, inner)
    far_out = exchange(middle, 4, inner)

    own_middle, own_mid = products(3, *own, (middle,), keep_mid=True)
    own_1 = products(1, *own, (near,))
    x_psi, left_next, own_1, own_middle = lax.optimization_barrier((x_psi, left_env, own_1, own_middle))
    x_left = exchange(left_next, 2, every)
    across_psi = [exchange(part, 1, every) for part in split(x_psi, 1, 9 * x_psi.shape[1] // 16)]
    sent_1 = exchange(own_1, 4, every)
    sent_own_middle = exchange(own_middle, 12, inner)

    far_out, far_in = lax.optimization_barrier((far_out, far_in))
    third = exchange(far_in, 4, inner)
    own_2 = products(2, *own, (far_out, far_in))
    own_2, sent_1, sent_own_middle = lax.optimization_barrier((own_2, sent_1, sent_own_middle))
    sent_2 = exchange(own_2, 8, every)

    x_left, sent_2 = lax.optimization_barrier((x_left, sent_2))
    across_left = [exchange(part, 1, every) for part in split(x_left, 0, 5 * x_left.shape[0] // 8)]
    other = ([(x_left,), across_left], [(x_psi,), across_psi])
    other_2 = products(2, *other, (far_out, far_in))
    other_sent_2 = exchange(other_2, 8, every)
    other_middle, other_mid = products(3, *other, (middle,), keep_mid=True)
    sent_other_middle = exchange(other_middle, 12, inner)
    other_1 = products(1, *other, (near,))
    other_sent_1 = exchange(other_1, 4, every)

    third, other_1, other_middle, other_2 = lax.optimization_barrier((third, other_1, other_middle, other_2))
    last_third = second((own_mid, other_mid), third, dtype, 10**10)
    sent_third = exchange(last_third, 12, outer)
    right_last, last_third = lax.optimization_barrier((right_env, last_third))
    other_0 = products(0, *other, (right_last,))

    out = place(16, [(0, own_0), (2, other_0), (4, sent_1), (8, sent_2)], flops=10**10)
    last = [(12, sent_third), (12, sent_own_middle), (14, sent_other_middle)]
    out = place(16, [(10, other_sent_2), (6, other_sent_1)] + last, out, 2)[:, None]
    if ops > 1:
        out = lax.psum_scatter(out, "op", scatter_dimension=2, tiled=True).astype(jnp.bfloat16)
    return out


def solution(mesh):
    placed = (
        P(("group", "sec"), None, None, None),
        P(("group", "op"), "sec", None, None),
        P(("group", "op"), "sec", None, None),
        P(("group", "op"), None),
    )
    return jax.shard_map(
        functools.partial(on_device, mesh.shape["op"]),
        mesh=mesh,
        in_specs=placed,
        out_specs=P("group", "sec", "op", None),
        check_vma=False,
    )
```

```python
import functools

import jax
import jax.numpy as jnp
from jax import lax
from jax.experimental import pallas as pl
from jax.experimental.pallas import tpu as pltpu
from jax.sharding import PartitionSpec as P

HBM = pl.BlockSpec(memory_space=pltpu.HBM)
SMEM = pl.BlockSpec(memory_space=pltpu.SMEM)
VMEM = pl.BlockSpec(memory_space=pltpu.VMEM)


def slot_kernel(step, parts, choices, source, *refs):
    count = len(parts)
    lefts, psis = [], []
    for number, _ in parts:
        lefts.append(refs[:number])
        refs = refs[number:]
    for _, number in parts:
        psis.append(refs[:number])
        refs = refs[number:]
    rights = refs[:choices]
    out, mid_buf, right_buf = refs[choices:]
    terms, _, rows, columns = rights[0].shape
    me = lax.axis_index("sec")
    row = me >> 2
    q = me ^ (4 * step)
    outer = (row == 0) | (row == 3)

    def psi_block(held, sector):
        if len(held) == 1:
            return held[0][0, sector]
        low, high = held
        size = low.shape[1]
        return jnp.where(
            sector < size, low[0, jnp.minimum(sector, size - 1)], high[0, jnp.maximum(sector - size, 0)]
        )

    def left_block(held, k):
        for part in held:
            if k < part.shape[0]:
                return part[k, 0]
            k -= part.shape[0]

    for k in range(terms):
        span = pl.ds(k * columns, columns)
        right = rights[0][k, 0]
        if choices > 1:
            right = jnp.where(outer, right, rights[1][k, 0])
        right_buf[:, span] = right
        for i in range(count):
            mid = jnp.dot(
                left_block(lefts[i], k), psi_block(psis[i], source[k, q]), preferred_element_type=jnp.float32
            )
            mid_buf[pl.ds(i * rows, rows), span] = mid.astype(jnp.bfloat16)
    second_product(mid_buf, right_buf, out)


def second_product(mid, right, out):
    total = lax.dot_general(mid[...], right[...], (((1,), (1,)), ((), ())), preferred_element_type=jnp.float32)
    out[...] = total.reshape(out.shape).astype(out.dtype)


def second_kernel(*refs):
    *mids, right, out, right_buf = refs
    terms, _, _, columns = right.shape
    for k in range(terms):
        right_buf[:, pl.ds(k * columns, columns)] = right[k, 0]
    size = out.shape[0] // len(mids)
    for i, mid in enumerate(mids):
        second_product(mid, right_buf, out.at[pl.ds(i * size, size)])


def second(mids, right, dtype, flops):
    terms, _, rows, columns = right.shape
    return pl.pallas_call(
        second_kernel,
        out_shape=jax.ShapeDtypeStruct((sum(mid.shape[0] for mid in mids) // rows, rows, columns), dtype),
        in_specs=[VMEM] * (len(mids) + 1),
        out_specs=VMEM,
        scratch_shapes=[pltpu.VMEM((rows, terms * columns), jnp.bfloat16)],
        compiler_params=pltpu.CompilerParams(vmem_limit_bytes=16 << 20),
        cost_estimate=pl.CostEstimate(flops=flops, bytes_accessed=1, transcendentals=0),
    )(*mids, right)


def slot(step, source_map, lefts, psis, rights, dtype, flops, keep_mid):
    terms, _, rows, columns = rights[0].shape
    count = len(psis)
    parts = tuple((len(left), len(psi)) for left, psi in zip(lefts, psis))
    held = [part for left in lefts for part in left] + [part for psi in psis for part in psi] + list(rights)
    out = jax.ShapeDtypeStruct((count, rows, columns), dtype)
    mid = jax.ShapeDtypeStruct((count * rows, terms * columns), jnp.bfloat16)
    scratch = [pltpu.VMEM((rows, terms * columns), jnp.bfloat16)]
    if not keep_mid:
        scratch = [pltpu.VMEM(mid.shape, mid.dtype)] + scratch
    return pl.pallas_call(
        functools.partial(slot_kernel, step, parts, len(rights)),
        out_shape=(out, mid) if keep_mid else out,
        in_specs=[SMEM] + [VMEM] * len(held),
        out_specs=(VMEM, VMEM) if keep_mid else VMEM,
        scratch_shapes=scratch,
        compiler_params=pltpu.CompilerParams(vmem_limit_bytes=24 << 20),
        cost_estimate=pl.CostEstimate(flops=flops, bytes_accessed=1, transcendentals=0),
    )(source_map, *held)


def split_kernel(axis, whole, low, high):
    first = low.shape[axis]
    before = (slice(None),) * axis
    low[...] = whole[(*before, slice(0, first))]
    high[...] = whole[(*before, slice(first, None))]


def split(array, axis, first):
    def part(size):
        shape = array.shape[:axis] + (size,) + array.shape[axis + 1 :]
        return jax.ShapeDtypeStruct(shape, array.dtype)

    return pl.pallas_call(
        functools.partial(split_kernel, axis),
        out_shape=(part(first), part(array.shape[axis] - first)),
        in_specs=[VMEM],
        out_specs=(VMEM, VMEM),
        compiler_params=pltpu.CompilerParams(vmem_limit_bytes=12 << 20),
        cost_estimate=pl.CostEstimate(flops=1, bytes_accessed=1, transcendentals=0),
    )(array)


def place_kernel(starts, shared, *refs):
    *pieces, out, sem = refs
    pieces = pieces[-len(starts) :]
    me = lax.axis_index("sec")
    row = me >> 2
    outer = (row == 0) | (row == 3)

    def copies(held):
        return [
            pltpu.make_async_copy(piece.at[i], out.at[me ^ (start + i)], sem.at[start + i])
            for start, piece in held
            for i in range(piece.shape[0])
        ]

    held = list(zip(starts, pieces))
    for copy in copies(held[:shared]):
        copy.start()
    if shared < len(held):

        @pl.when(outer)
        def _():
            for copy in copies(held[shared : shared + 1]):
                copy.start()

        @pl.when(jnp.logical_not(outer))
        def _():
            for copy in copies(held[shared + 1 :]):
                copy.start()

    for copy in copies(held[: shared + 1]):
        copy.wait()


def place(sectors, held, out=None, shared=None, flops=1):
    starts, pieces = zip(*held)
    before = [] if out is None else [out]
    return pl.pallas_call(
        functools.partial(place_kernel, starts, len(held) if shared is None else shared),
        out_shape=jax.ShapeDtypeStruct((sectors,) + pieces[0].shape[1:], pieces[0].dtype),
        in_specs=[HBM] * len(before) + [VMEM] * len(pieces),
        out_specs=HBM,
        scratch_shapes=[pltpu.SemaphoreType.DMA((sectors,))],
        input_output_aliases={} if out is None else {0: 0},
        compiler_params=pltpu.CompilerParams(vmem_limit_bytes=16 << 20),
        cost_estimate=pl.CostEstimate(flops=flops, bytes_accessed=1, transcendentals=0),
    )(*before, *pieces)


def exchange(array, bits, members):
    return lax.ppermute(array, "sec", [(s, s ^ bits) for s in members])


def on_device(ops, psi, left_env, right_env, source_map):
    dtype = jnp.bfloat16 if ops == 1 else jnp.float32
    every = range(16)
    inner = range(4, 12)
    outer = [s for s in every if s not in inner]

    def products(step, lefts, psis, rights, flops=1, keep_mid=False):
        return slot(step, source_map, lefts, psis, rights, dtype, flops, keep_mid)

    near = exchange(right_env, 4, every)
    middle = exchange(right_env, 12, inner)
    x_psi = exchange(psi, 2, every)
    own = ([(left_env,), (exchange(left_env, 1, every),)], [(psi,), (exchange(psi, 1, every),)])
    own_0 = products(0, *own, (right_env,), flops=2 * 10**10)

    near, middle, own_0 = lax.optimization_barrier((near, middle, own_0))
    far_in = exchange(near, 12, inner)
    far_out = exchange(middle, 4, inner)

    own_middle, own_mid = products(3, *own, (middle,), keep_mid=True)
    own_1 = products(1, *own, (near,))
    x_psi, left_next, own_1, own_middle = lax.optimization_barrier((x_psi, left_env, own_1, own_middle))
    x_left = exchange(left_next, 2, every)
    across_psi = [exchange(part, 1, every) for part in split(x_psi, 1, 9 * x_psi.shape[1] // 16)]
    sent_1 = exchange(own_1, 4, every)
    sent_own_middle = exchange(own_middle, 12, inner)

    far_out, far_in = lax.optimization_barrier((far_out, far_in))
    third = exchange(far_in, 4, inner)
    own_2 = products(2, *own, (far_out, far_in))
    own_2, sent_1, sent_own_middle = lax.optimization_barrier((own_2, sent_1, sent_own_middle))
    sent_2 = exchange(own_2, 8, every)

    x_left, sent_2 = lax.optimization_barrier((x_left, sent_2))
    across_left = [exchange(part, 1, every) for part in split(x_left, 0, 5 * x_left.shape[0] // 8)]
    other = ([(x_left,), across_left], [(x_psi,), across_psi])
    other_2 = products(2, *other, (far_out, far_in))
    other_sent_2 = exchange(other_2, 8, every)
    other_middle, other_mid = products(3, *other, (middle,), keep_mid=True)
    sent_other_middle = exchange(other_middle, 12, inner)
    other_1 = products(1, *other, (near,))
    other_sent_1 = exchange(other_1, 4, every)

    third, other_2, other_middle, other_1 = lax.optimization_barrier((third, other_2, other_middle, other_1))
    last_third = second((own_mid, other_mid), third, dtype, 10**10)
    sent_third = exchange(last_third, 12, outer)
    right_last, last_third = lax.optimization_barrier((right_env, last_third))
    other_0 = products(0, *other, (right_last,))

    out = place(16, [(0, own_0), (2, other_0), (4, sent_1), (8, sent_2)], flops=10**10)
    last = [(12, sent_third), (12, sent_own_middle), (14, sent_other_middle)]
    out = place(16, [(10, other_sent_2), (6, other_sent_1)] + last, out, 2)[:, None]
    if ops > 1:
        out = lax.psum_scatter(out, "op", scatter_dimension=2, tiled=True).astype(jnp.bfloat16)
    return out


def solution(mesh):
    placed = (
        P(("group", "sec"), None, None, None),
        P(("group", "op"), "sec", None, None),
        P(("group", "op"), "sec", None, None),
        P(("group", "op"), None),
    )
    return jax.shard_map(
        functools.partial(on_device, mesh.shape["op"]),
        mesh=mesh,
        in_specs=placed,
        out_specs=P("group", "sec", "op", None),
        check_vma=False,
    )
```

```python
import functools

import jax
import jax.numpy as jnp
from jax import lax
from jax.experimental import pallas as pl
from jax.experimental.pallas import tpu as pltpu
from jax.sharding import PartitionSpec as P

HBM = pl.BlockSpec(memory_space=pltpu.HBM)
SMEM = pl.BlockSpec(memory_space=pltpu.SMEM)
VMEM = pl.BlockSpec(memory_space=pltpu.VMEM)


def slot_kernel(step, parts, choices, source, *refs):
    count = len(parts)
    lefts, psis = [], []
    for number, _ in parts:
        lefts.append(refs[:number])
        refs = refs[number:]
    for _, number in parts:
        psis.append(refs[:number])
        refs = refs[number:]
    rights = refs[:choices]
    out, mid_buf, right_buf = refs[choices:]
    terms, _, rows, columns = rights[0].shape
    me = lax.axis_index("sec")
    row = me >> 2
    q = me ^ (4 * step)
    outer = (row == 0) | (row == 3)

    def psi_block(held, sector):
        if len(held) == 1:
            return held[0][0, sector]
        low, high = held
        size = low.shape[1]
        return jnp.where(
            sector < size, low[0, jnp.minimum(sector, size - 1)], high[0, jnp.maximum(sector - size, 0)]
        )

    def left_block(held, k):
        for part in held:
            if k < part.shape[0]:
                return part[k, 0]
            k -= part.shape[0]

    for k in range(terms):
        span = pl.ds(k * columns, columns)
        right = rights[0][k, 0]
        if choices > 1:
            right = jnp.where(outer, right, rights[1][k, 0])
        right_buf[:, span] = right
        for i in range(count):
            mid = jnp.dot(
                left_block(lefts[i], k), psi_block(psis[i], source[k, q]), preferred_element_type=jnp.float32
            )
            mid_buf[pl.ds(i * rows, rows), span] = mid.astype(jnp.bfloat16)
    second_product(mid_buf, right_buf, out)


def second_product(mid, right, out):
    total = lax.dot_general(mid[...], right[...], (((1,), (1,)), ((), ())), preferred_element_type=jnp.float32)
    out[...] = total.reshape(out.shape).astype(out.dtype)


def second_kernel(*refs):
    *mids, right, out, right_buf = refs
    terms, _, _, columns = right.shape
    for k in range(terms):
        right_buf[:, pl.ds(k * columns, columns)] = right[k, 0]
    size = out.shape[0] // len(mids)
    for i, mid in enumerate(mids):
        second_product(mid, right_buf, out.at[pl.ds(i * size, size)])


def second(mids, right, dtype, flops):
    terms, _, rows, columns = right.shape
    return pl.pallas_call(
        second_kernel,
        out_shape=jax.ShapeDtypeStruct((sum(mid.shape[0] for mid in mids) // rows, rows, columns), dtype),
        in_specs=[VMEM] * (len(mids) + 1),
        out_specs=VMEM,
        scratch_shapes=[pltpu.VMEM((rows, terms * columns), jnp.bfloat16)],
        compiler_params=pltpu.CompilerParams(vmem_limit_bytes=16 << 20),
        cost_estimate=pl.CostEstimate(flops=flops, bytes_accessed=1, transcendentals=0),
    )(*mids, right)


def slot(step, source_map, lefts, psis, rights, dtype, flops, keep_mid):
    terms, _, rows, columns = rights[0].shape
    count = len(psis)
    parts = tuple((len(left), len(psi)) for left, psi in zip(lefts, psis))
    held = [part for left in lefts for part in left] + [part for psi in psis for part in psi] + list(rights)
    out = jax.ShapeDtypeStruct((count, rows, columns), dtype)
    mid = jax.ShapeDtypeStruct((count * rows, terms * columns), jnp.bfloat16)
    scratch = [pltpu.VMEM((rows, terms * columns), jnp.bfloat16)]
    if not keep_mid:
        scratch = [pltpu.VMEM(mid.shape, mid.dtype)] + scratch
    return pl.pallas_call(
        functools.partial(slot_kernel, step, parts, len(rights)),
        out_shape=(out, mid) if keep_mid else out,
        in_specs=[SMEM] + [VMEM] * len(held),
        out_specs=(VMEM, VMEM) if keep_mid else VMEM,
        scratch_shapes=scratch,
        compiler_params=pltpu.CompilerParams(vmem_limit_bytes=24 << 20),
        cost_estimate=pl.CostEstimate(flops=flops, bytes_accessed=1, transcendentals=0),
    )(source_map, *held)


def split_kernel(axis, whole, low, high):
    first = low.shape[axis]
    before = (slice(None),) * axis
    low[...] = whole[(*before, slice(0, first))]
    high[...] = whole[(*before, slice(first, None))]


def split(array, axis, first):
    def part(size):
        shape = array.shape[:axis] + (size,) + array.shape[axis + 1 :]
        return jax.ShapeDtypeStruct(shape, array.dtype)

    return pl.pallas_call(
        functools.partial(split_kernel, axis),
        out_shape=(part(first), part(array.shape[axis] - first)),
        in_specs=[VMEM],
        out_specs=(VMEM, VMEM),
        compiler_params=pltpu.CompilerParams(vmem_limit_bytes=12 << 20),
        cost_estimate=pl.CostEstimate(flops=1, bytes_accessed=1, transcendentals=0),
    )(array)


def place_kernel(starts, shared, *refs):
    *pieces, out, sem = refs
    pieces = pieces[-len(starts) :]
    me = lax.axis_index("sec")
    row = me >> 2
    outer = (row == 0) | (row == 3)

    def copies(held):
        return [
            pltpu.make_async_copy(piece.at[i], out.at[me ^ (start + i)], sem.at[start + i])
            for start, piece in held
            for i in range(piece.shape[0])
        ]

    held = list(zip(starts, pieces))
    for copy in copies(held[:shared]):
        copy.start()
    if shared < len(held):

        @pl.when(outer)
        def _():
            for copy in copies(held[shared : shared + 1]):
                copy.start()

        @pl.when(jnp.logical_not(outer))
        def _():
            for copy in copies(held[shared + 1 :]):
                copy.start()

    for copy in copies(held[: shared + 1]):
        copy.wait()


def place(sectors, held, out=None, shared=None, flops=1):
    starts, pieces = zip(*held)
    before = [] if out is None else [out]
    return pl.pallas_call(
        functools.partial(place_kernel, starts, len(held) if shared is None else shared),
        out_shape=jax.ShapeDtypeStruct((sectors,) + pieces[0].shape[1:], pieces[0].dtype),
        in_specs=[HBM] * len(before) + [VMEM] * len(pieces),
        out_specs=HBM,
        scratch_shapes=[pltpu.SemaphoreType.DMA((sectors,))],
        input_output_aliases={} if out is None else {0: 0},
        compiler_params=pltpu.CompilerParams(vmem_limit_bytes=16 << 20),
        cost_estimate=pl.CostEstimate(flops=flops, bytes_accessed=1, transcendentals=0),
    )(*before, *pieces)


def exchange(array, bits, members):
    return lax.ppermute(array, "sec", [(s, s ^ bits) for s in members])


def on_device(ops, psi, left_env, right_env, source_map):
    dtype = jnp.bfloat16 if ops == 1 else jnp.float32
    every = range(16)
    inner = range(4, 12)
    outer = [s for s in every if s not in inner]

    def products(step, lefts, psis, rights, flops=1, keep_mid=False):
        return slot(step, source_map, lefts, psis, rights, dtype, flops, keep_mid)

    near = exchange(right_env, 4, every)
    middle = exchange(right_env, 12, inner)
    x_psi = exchange(psi, 2, every)
    own = ([(left_env,), (exchange(left_env, 1, every),)], [(psi,), (exchange(psi, 1, every),)])
    own_0 = products(0, *own, (right_env,), flops=2 * 10**10)

    near, middle, own_0 = lax.optimization_barrier((near, middle, own_0))
    far_in = exchange(near, 12, inner)
    far_out = exchange(middle, 4, inner)

    own_middle, own_mid = products(3, *own, (middle,), keep_mid=True)
    own_1 = products(1, *own, (near,))
    x_psi, left_next, own_1, own_middle = lax.optimization_barrier((x_psi, left_env, own_1, own_middle))
    x_left = exchange(left_next, 2, every)
    across_psi = [exchange(part, 1, every) for part in split(x_psi, 1, 9 * x_psi.shape[1] // 16)]
    sent_1 = exchange(own_1, 4, every)
    sent_own_middle = exchange(own_middle, 12, inner)

    far_out, far_in = lax.optimization_barrier((far_out, far_in))
    third = exchange(far_in, 4, inner)
    own_2 = products(2, *own, (far_out, far_in))
    own_2, sent_1, sent_own_middle = lax.optimization_barrier((own_2, sent_1, sent_own_middle))
    sent_2 = exchange(own_2, 8, every)

    x_left, sent_2 = lax.optimization_barrier((x_left, sent_2))
    across_left = [exchange(part, 1, every) for part in split(x_left, 0, 5 * x_left.shape[0] // 8)]
    other = ([(x_left,), across_left], [(x_psi,), across_psi])
    other_2 = products(2, *other, (far_out, far_in))
    other_sent_2 = exchange(other_2, 8, every)
    other_middle, other_mid = products(3, *other, (middle,), keep_mid=True)
    sent_other_middle = exchange(other_middle, 12, inner)
    other_1 = products(1, *other, (near,))
    other_sent_1 = exchange(other_1, 4, every)

    third, other_1, other_middle, other_2 = lax.optimization_barrier((third, other_1, other_middle, other_2))
    last_third = second((own_mid, other_mid), third, dtype, 10**10)
    sent_third = exchange(last_third, 12, outer)
    right_last, last_third = lax.optimization_barrier((right_env, last_third))
    other_0 = products(0, *other, (right_last,))

    out = place(16, [(0, own_0), (2, other_0), (4, sent_1), (8, sent_2)], flops=10**10)
    last = [(12, sent_third), (12, sent_own_middle), (14, sent_other_middle)]
    out = place(16, [(10, other_sent_2)] + last, out, 1)
    out = place(16, [(6, other_sent_1)], out)[:, None]
    if ops > 1:
        out = lax.psum_scatter(out, "op", scatter_dimension=2, tiled=True).astype(jnp.bfloat16)
    return out


def solution(mesh):
    placed = (
        P(("group", "sec"), None, None, None),
        P(("group", "op"), "sec", None, None),
        P(("group", "op"), "sec", None, None),
        P(("group", "op"), None),
    )
    return jax.shard_map(
        functools.partial(on_device, mesh.shape["op"]),
        mesh=mesh,
        in_specs=placed,
        out_specs=P("group", "sec", "op", None),
        check_vma=False,
    )
```

```python
import functools

import jax
import jax.numpy as jnp
from jax import lax
from jax.experimental import pallas as pl
from jax.experimental.pallas import tpu as pltpu
from jax.sharding import PartitionSpec as P

HBM = pl.BlockSpec(memory_space=pltpu.HBM)
SMEM = pl.BlockSpec(memory_space=pltpu.SMEM)
VMEM = pl.BlockSpec(memory_space=pltpu.VMEM)


def slot_kernel(step, parts, choices, source, *refs):
    count = len(parts)
    lefts, psis = [], []
    for number, _ in parts:
        lefts.append(refs[:number])
        refs = refs[number:]
    for _, number in parts:
        psis.append(refs[:number])
        refs = refs[number:]
    rights = refs[:choices]
    out, mid_buf, right_buf = refs[choices:]
    terms, _, rows, columns = rights[0].shape
    me = lax.axis_index("sec")
    row = me >> 2
    q = me ^ (4 * step)
    outer = (row == 0) | (row == 3)

    def psi_block(held, sector):
        if len(held) == 1:
            return held[0][0, sector]
        low, high = held
        size = low.shape[1]
        return jnp.where(
            sector < size, low[0, jnp.minimum(sector, size - 1)], high[0, jnp.maximum(sector - size, 0)]
        )

    def left_block(held, k):
        for part in held:
            if k < part.shape[0]:
                return part[k, 0]
            k -= part.shape[0]

    for k in range(terms):
        span = pl.ds(k * columns, columns)
        right = rights[0][k, 0]
        if choices > 1:
            right = jnp.where(outer, right, rights[1][k, 0])
        right_buf[:, span] = right
        for i in range(count):
            mid = jnp.dot(
                left_block(lefts[i], k), psi_block(psis[i], source[k, q]), preferred_element_type=jnp.float32
            )
            mid_buf[pl.ds(i * rows, rows), span] = mid.astype(jnp.bfloat16)
    second_product(mid_buf, right_buf, out)


def second_product(mid, right, out):
    total = lax.dot_general(mid[...], right[...], (((1,), (1,)), ((), ())), preferred_element_type=jnp.float32)
    out[...] = total.reshape(out.shape).astype(out.dtype)


def second_kernel(*refs):
    *mids, right, out, right_buf = refs
    terms, _, _, columns = right.shape
    for k in range(terms):
        right_buf[:, pl.ds(k * columns, columns)] = right[k, 0]
    size = out.shape[0] // len(mids)
    for i, mid in enumerate(mids):
        second_product(mid, right_buf, out.at[pl.ds(i * size, size)])


def second(mids, right, dtype, flops):
    terms, _, rows, columns = right.shape
    return pl.pallas_call(
        second_kernel,
        out_shape=jax.ShapeDtypeStruct((sum(mid.shape[0] for mid in mids) // rows, rows, columns), dtype),
        in_specs=[VMEM] * (len(mids) + 1),
        out_specs=VMEM,
        scratch_shapes=[pltpu.VMEM((rows, terms * columns), jnp.bfloat16)],
        compiler_params=pltpu.CompilerParams(vmem_limit_bytes=16 << 20),
        cost_estimate=pl.CostEstimate(flops=flops, bytes_accessed=1, transcendentals=0),
    )(*mids, right)


def slot(step, source_map, lefts, psis, rights, dtype, flops, keep_mid):
    terms, _, rows, columns = rights[0].shape
    count = len(psis)
    parts = tuple((len(left), len(psi)) for left, psi in zip(lefts, psis))
    held = [part for left in lefts for part in left] + [part for psi in psis for part in psi] + list(rights)
    out = jax.ShapeDtypeStruct((count, rows, columns), dtype)
    mid = jax.ShapeDtypeStruct((count * rows, terms * columns), jnp.bfloat16)
    scratch = [pltpu.VMEM((rows, terms * columns), jnp.bfloat16)]
    if not keep_mid:
        scratch = [pltpu.VMEM(mid.shape, mid.dtype)] + scratch
    return pl.pallas_call(
        functools.partial(slot_kernel, step, parts, len(rights)),
        out_shape=(out, mid) if keep_mid else out,
        in_specs=[SMEM] + [VMEM] * len(held),
        out_specs=(VMEM, VMEM) if keep_mid else VMEM,
        scratch_shapes=scratch,
        compiler_params=pltpu.CompilerParams(vmem_limit_bytes=24 << 20),
        cost_estimate=pl.CostEstimate(flops=flops, bytes_accessed=1, transcendentals=0),
    )(source_map, *held)


def split_kernel(axis, whole, low, high):
    first = low.shape[axis]
    before = (slice(None),) * axis
    low[...] = whole[(*before, slice(0, first))]
    high[...] = whole[(*before, slice(first, None))]


def split(array, axis, first):
    def part(size):
        shape = array.shape[:axis] + (size,) + array.shape[axis + 1 :]
        return jax.ShapeDtypeStruct(shape, array.dtype)

    return pl.pallas_call(
        functools.partial(split_kernel, axis),
        out_shape=(part(first), part(array.shape[axis] - first)),
        in_specs=[VMEM],
        out_specs=(VMEM, VMEM),
        compiler_params=pltpu.CompilerParams(vmem_limit_bytes=12 << 20),
        cost_estimate=pl.CostEstimate(flops=1, bytes_accessed=1, transcendentals=0),
    )(array)


def place_kernel(starts, shared, *refs):
    *pieces, out, sem = refs
    pieces = pieces[-len(starts) :]
    me = lax.axis_index("sec")
    row = me >> 2
    outer = (row == 0) | (row == 3)

    def copies(held):
        return [
            pltpu.make_async_copy(piece.at[i], out.at[me ^ (start + i)], sem.at[start + i])
            for start, piece in held
            for i in range(piece.shape[0])
        ]

    held = list(zip(starts, pieces))
    for copy in copies(held[:shared]):
        copy.start()
    if shared < len(held):

        @pl.when(outer)
        def _():
            for copy in copies(held[shared : shared + 1]):
                copy.start()

        @pl.when(jnp.logical_not(outer))
        def _():
            for copy in copies(held[shared + 1 :]):
                copy.start()

    for copy in copies(held[: shared + 1]):
        copy.wait()


def place(sectors, held, out=None, shared=None, flops=1):
    starts, pieces = zip(*held)
    before = [] if out is None else [out]
    return pl.pallas_call(
        functools.partial(place_kernel, starts, len(held) if shared is None else shared),
        out_shape=jax.ShapeDtypeStruct((sectors,) + pieces[0].shape[1:], pieces[0].dtype),
        in_specs=[HBM] * len(before) + [VMEM] * len(pieces),
        out_specs=HBM,
        scratch_shapes=[pltpu.SemaphoreType.DMA((sectors,))],
        input_output_aliases={} if out is None else {0: 0},
        compiler_params=pltpu.CompilerParams(vmem_limit_bytes=16 << 20),
        cost_estimate=pl.CostEstimate(flops=flops, bytes_accessed=1, transcendentals=0),
    )(*before, *pieces)


def exchange(array, bits, members):
    return lax.ppermute(array, "sec", [(s, s ^ bits) for s in members])


def on_device(ops, psi, left_env, right_env, source_map):
    dtype = jnp.bfloat16 if ops == 1 else jnp.float32
    every = range(16)
    inner = range(4, 12)
    outer = [s for s in every if s not in inner]

    def products(step, lefts, psis, rights, flops=1, keep_mid=False):
        return slot(step, source_map, lefts, psis, rights, dtype, flops, keep_mid)

    near = exchange(right_env, 4, every)
    middle = exchange(right_env, 12, inner)
    x_psi = exchange(psi, 2, every)
    own = ([(left_env,), (exchange(left_env, 1, every),)], [(psi,), (exchange(psi, 1, every),)])
    own_0 = products(0, *own, (right_env,), flops=2 * 10**10)

    near, middle, own_0 = lax.optimization_barrier((near, middle, own_0))
    far_in = exchange(near, 12, inner)
    far_out = exchange(middle, 4, inner)

    own_middle, own_mid = products(3, *own, (middle,), keep_mid=True)
    own_1 = products(1, *own, (near,))
    x_psi, left_next, own_1, own_middle = lax.optimization_barrier((x_psi, left_env, own_1, own_middle))
    x_left = exchange(left_next, 2, every)
    across_psi = [exchange(part, 1, every) for part in split(x_psi, 1, 9 * x_psi.shape[1] // 16)]
    sent_1 = exchange(own_1, 4, every)
    sent_own_middle = exchange(own_middle, 12, inner)

    far_out, far_in = lax.optimization_barrier((far_out, far_in))
    third = exchange(far_in, 4, inner)
    own_2 = products(2, *own, (far_out, far_in))
    own_2, sent_1, sent_own_middle = lax.optimization_barrier((own_2, sent_1, sent_own_middle))
    sent_2 = exchange(own_2, 8, every)

    x_left, sent_2 = lax.optimization_barrier((x_left, sent_2))
    across_left = [exchange(part, 1, every) for part in split(x_left, 0, 5 * x_left.shape[0] // 8)]
    other = ([(x_left,), across_left], [(x_psi,), across_psi])
    other_2 = products(2, *other, (far_out, far_in))
    other_sent_2 = exchange(other_2, 8, every)
    other_middle, other_mid = products(3, *other, (middle,), keep_mid=True)
    sent_other_middle = exchange(other_middle, 12, inner)
    other_1 = products(1, *other, (near,))
    other_sent_1 = exchange(other_1, 4, every)

    third, other_1, other_middle, other_2 = lax.optimization_barrier((third, other_1, other_middle, other_2))
    last_third = second((own_mid, other_mid), third, dtype, 10**10)
    sent_third = exchange(last_third, 12, outer)
    right_last, last_third = lax.optimization_barrier((right_env, last_third))
    other_0 = products(0, *other, (right_last,))

    out = place(16, [(0, own_0), (2, other_0), (4, sent_1), (8, sent_2), (10, other_sent_2)], flops=10**10)
    last = [(12, sent_third), (12, sent_own_middle), (14, sent_other_middle)]
    out = place(16, [(6, other_sent_1)] + last, out, 1)[:, None]
    if ops > 1:
        out = lax.psum_scatter(out, "op", scatter_dimension=2, tiled=True).astype(jnp.bfloat16)
    return out


def solution(mesh):
    placed = (
        P(("group", "sec"), None, None, None),
        P(("group", "op"), "sec", None, None),
        P(("group", "op"), "sec", None, None),
        P(("group", "op"), None),
    )
    return jax.shard_map(
        functools.partial(on_device, mesh.shape["op"]),
        mesh=mesh,
        in_specs=placed,
        out_specs=P("group", "sec", "op", None),
        check_vma=False,
    )
```
